128 devices in a mesh: expert: 32 (over z, y, core), shard: 4 (over x).
Axes of the slice: x: 4, y: 4, z: 4, core: 2. Of those that a mesh axis runs over, the one named last changes fastest.
Arguments:
- tokens: bfloat16 [32768, 1024], P(('expert', 'shard')), may hold values from -6 to 6
- lengths: int32 [32, 4], P('expert'), may hold values from 1 to 1020, as said below
- routes: int32 [32768, 8], P(('expert', 'shard')), may hold values from 0 to 31, all different within a row; in each aligned block of 256 rows (0 to 255, 256 to 511, ...) at most 96 rows name the same one
- norm1_gain: bfloat16 [1024], P('shard'), may hold values from 0.5 to 1.5
- w_query: bfloat16 [1024, 1024], P('shard'), may hold values from -0.1875 to 0.1875
- w_key: bfloat16 [1024, 512], P('shard'), may hold values from -0.1875 to 0.1875
- w_value: bfloat16 [1024, 512], P('shard'), may hold values from -0.1875 to 0.1875
- query_gain: bfloat16 [64], P('shard'), may hold values from 0.5 to 1.5
- key_gain: bfloat16 [64], P('shard'), may hold values from 0.5 to 1.5
- w_out: bfloat16 [1024, 1024], P('shard'), may hold values from -3 to 3
- norm2_gain: bfloat16 [1024], P('shard'), may hold values from 0.5 to 1.5
- w_router: bfloat16 [1024, 32], P('shard'), may hold values from -0.09375 to 0.09375
- w_gate: bfloat16 [32, 1024, 512], P('expert', None, 'shard'), may hold values from -0.1875 to 0.1875
- w_up: bfloat16 [32, 1024, 512], P('expert', None, 'shard'), may hold values from -0.1875 to 0.1875
- w_down: bfloat16 [32, 512, 1024], P('expert', 'shard'), may hold values from -0.75 to 0.75
- cotangent: bfloat16 [32768, 1024], P(('expert', 'shard')), may hold values from -6 to 6
Outputs:
- layer_out: bfloat16 [32768, 1024], P(('expert', 'shard'))
- tokens_grad: float32 [32768, 1024], P(('expert', 'shard'))
- norm1_gain_grad: float32 [1024], P('shard')
- w_query_grad: float32 [1024, 1024], P('shard')
- w_key_grad: float32 [1024, 512], P('shard')
- w_value_grad: float32 [1024, 512], P('shard')
- query_gain_grad: float32 [64], P('shard')
- key_gain_grad: float32 [64], P('shard')
- w_out_grad: float32 [1024, 1024], P('shard')
- norm2_gain_grad: float32 [1024], P('shard')
- w_router_grad: float32 [1024, 32], P('shard')
- w_gate_grad: float32 [32, 1024, 512], P('expert', None, 'shard')
- w_up_grad: float32 [32, 1024, 512], P('expert', None, 'shard')
- w_down_grad: float32 [32, 512, 1024], P('expert', 'shard')
The draws below stay inside these ranges and needn't reach their ends.
Inputs may be any that keep to these rules, and one draw needn't show every extreme that they name: `lengths`: lengths of a sequence sum to less than 1024, so each ends in padding; one document of each sequence is longer than 768. `routes`: each row names 8 different experts; the rows of one device name no expert more than 96 times.
All inputs are finite; a program needn't handle non-finite values.
Results may differ from the reference program's by a relative error of at most 0.025.
Values may be sent and summed in bfloat16 or wider, within the bound.
A program may use at most 256 MiB of HBM per device.

```python
import math
import jax
import jax.numpy as jnp
import numpy as np
from jax import lax

D = 1024
HEADS = 16
KV_HEADS = 8
HD = 64
FF = 512
EXPERTS = 32
TOPK = 8
TOK_DEV = 256
DOCS = 4
QDIM = 1024
KVDIM = 512
LENGTH = 1024
SEQS = 32
TOKENS = 32768
CAP = 96
N_EXPERT = 32
N_SHARD = 4


def draw_lengths(key, part):
    key = jax.random.fold_in(key, 7)
    key_other, key_padding, key_longest, key_tight = jax.random.split(key, 4)
    others = jax.random.randint(key_other, (SEQS, DOCS), 1, TOK_DEV // 4)
    padding = jax.random.randint(key_padding, (SEQS, 1), 1, TOK_DEV // 4)
    longest = jax.random.randint(key_longest, (SEQS, 1), 0, DOCS)
    squeezed_seq = jax.random.randint(key_tight, (), 0, SEQS)
    squeezed = (jnp.arange(SEQS) == squeezed_seq)[:, None]
    others = jnp.where(squeezed, 1, others)
    padding = jnp.where(squeezed, 1, padding)
    chosen = jnp.arange(DOCS)[None, :] == longest
    remainder = jnp.sum(jnp.where(chosen, 0, others), axis=1, keepdims=True)
    return jnp.where(chosen, LENGTH - padding - remainder, others).astype(jnp.int32)


def shard_levels(rng, extent, cuts, least, top_value):
    level, own = 1.0, jax.random.fold_in(rng, 6)
    for position, parts in cuts:
        steps = jnp.exp(jax.random.uniform(jax.random.fold_in(own, position), (parts,), jnp.float32, least / len(cuts), top_value / len(cuts)))
        level = level * jnp.repeat(steps, extent[position] // parts).reshape([-1 if axis == position else 1 for axis in range(len(extent))])
    return level


def routed_block(stream_key, own, number, rows, number_of, top, reach, skew):
    order = jax.random.permutation(stream_key, number_of)
    crowded, common = portions_of(number_of, rows * top, reach, skew, True), portions_of(number_of, rows * top, reach, skew, False)
    places = jnp.arange(number_of)

    def named(tallies, turn):
        used = int((tallies > 0).sum())
        fixed = max(1, used // 4)
        moved = fixed + (places - fixed + turn * (used - fixed)) % max(1, number_of - fixed)
        return jnp.zeros((number_of,), jnp.int32).at[order[jnp.where(places < fixed, places, moved)]].set(jnp.asarray(tallies, jnp.int32))

    tallies = jnp.where(number % 4 == 0, named(crowded, number // 4), named(common, number - number // 4 - 1))
    mixed = jax.random.permutation(jax.random.fold_in(own, 3), number_of)
    giver, sink = mixed[0:number_of // 2 * 2:2], mixed[1:number_of // 2 * 2:2]
    room = jnp.minimum(tallies[giver] - 1, reach - tallies[sink]) // 2
    room = jnp.where((giver == order[0]) | (sink == order[0]) | (tallies[sink] == 0), 0, jnp.maximum(room, 0))
    moved = jax.random.randint(jax.random.fold_in(own, 4), (number_of // 2,), 0, 1 << 20) % (room + 1)
    tallies = tallies.at[giver].add(-moved).at[sink].add(moved)
    labels = jnp.searchsorted(jnp.cumsum(tallies), jnp.arange(rows * top), side="right").astype(jnp.int32)
    table = labels.reshape(top, rows).T
    table = table[jax.random.permutation(jax.random.fold_in(own, 1), rows)]
    turn = jax.random.randint(jax.random.fold_in(own, 2), (rows, 1), 0, top)
    return jnp.take_along_axis(table, (jnp.arange(top)[None, :] + turn) % top, axis=1)


def portions_of(count, total, reach, lean, full):
    loads = [(1 << 20) // math.isqrt(grade ** lean) + 1 for grade in range(1, count + 1)]
    largest = reach if full else min(reach, max(-(-total // count), total * loads[0] // sum(loads)))
    least = 1 if total - largest >= count - 1 else 0
    counts, surplus = [largest] + [least] * (count - 1), total - largest - least * (count - 1)
    while surplus > 0:
        movable = [i for i in range(1, count) if counts[i] < largest] or [i for i in range(1, count) if counts[i] < reach]
        mass, left = sum([loads[i] for i in movable]), surplus
        for i in movable:
            addition = min(reach - counts[i], max(1, left * loads[i] // mass), surplus)
            counts[i] = counts[i] + addition
            surplus = surplus - addition
    return np.array(counts)


def centred(rng, extent, deviation, bound, cuts=(), held_as=jnp.bfloat16):
    drawn = deviation * jax.random.normal(rng, extent, jnp.float32)
    if cuts:
        drawn = drawn * shard_levels(rng, extent, cuts, -0.22, 0.18)
    return jnp.clip(drawn, -bound, bound).astype(held_as)


def setup_inputs(seed: int = 0) -> dict:
    seeds = jax.random.split(jax.random.key(seed), 17)
    tokens = centred(seeds[0], (TOKENS, D), 1.0, 6.0, ((0, 128),))
    lengths = draw_lengths(jax.random.fold_in(seeds[16], 71), 0)
    routes_keys = jax.random.split(jax.random.fold_in(seeds[2], 1), TOKENS // TOK_DEV)
    routes_turns = jax.random.permutation(jax.random.fold_in(seeds[2], 3), TOKENS // TOK_DEV)
    routes = jax.vmap(lambda own, number: routed_block(jax.random.fold_in(seeds[2], 2), own, number, TOK_DEV, EXPERTS, TOPK, CAP, 1))(routes_keys, routes_turns).reshape((TOKENS, TOPK))
    norm1_gain = jnp.clip(1.0 + 0.1 * jax.random.normal(seeds[3], (D,), jnp.float32), 0.5, 1.5).astype(jnp.bfloat16)
    w_query = centred(seeds[4], (D, QDIM), D ** -0.5, 0.1875, ((0, 4),))
    w_key = centred(seeds[5], (D, KVDIM), D ** -0.5, 0.1875, ((0, 4),))
    w_value = centred(seeds[6], (D, KVDIM), D ** -0.5, 0.1875, ((0, 4),))
    query_gain = jnp.clip(1.0 + 0.1 * jax.random.normal(seeds[7], (HD,), jnp.float32), 0.5, 1.5).astype(jnp.bfloat16)
    key_gain = jnp.clip(1.0 + 0.1 * jax.random.normal(seeds[8], (HD,), jnp.float32), 0.5, 1.5).astype(jnp.bfloat16)
    w_out = centred(seeds[9], (QDIM, D), (max(QDIM // 256, 1)) ** -0.5, 3.0, ((0, 4),))
    norm2_gain = jnp.clip(1.0 + 0.1 * jax.random.normal(seeds[10], (D,), jnp.float32), 0.5, 1.5).astype(jnp.bfloat16)
    w_router = centred(seeds[11], (D, EXPERTS), (4 * D) ** -0.5, 0.09375, ((0, 4),))
    w_gate = centred(seeds[12], (EXPERTS, D, FF), D ** -0.5, 0.1875, ((0, 32), (2, 4)))
    w_up = centred(seeds[13], (EXPERTS, D, FF), D ** -0.5, 0.1875, ((0, 32), (2, 4)))
    w_down = centred(seeds[14], (EXPERTS, FF, D), (max(FF // 8, 1)) ** -0.5, 0.75, ((0, 32), (1, 4)))
    cotangent = centred(seeds[15], (TOKENS, D), 1.0, 6.0, ((0, 128),))
    return {"tokens": tokens, "lengths": lengths, "routes": routes, "norm1_gain": norm1_gain, "w_query": w_query, "w_key": w_key, "w_value": w_value, "query_gain": query_gain, "key_gain": key_gain, "w_out": w_out, "norm2_gain": norm2_gain, "w_router": w_router, "w_gate": w_gate, "w_up": w_up, "w_down": w_down, "cotangent": cotangent}


EPS = 1e-06
ROPE_BASE = 10000.0

@jax.custom_vjp
def low(v):
    return lax.optimization_barrier(v.astype(jnp.bfloat16)).astype(jnp.float32)

@jax.custom_vjp
def low_back(v):
    return v

def low_keep(v):
    return (low(v), None)

def low_pass(kept, grad):
    return (grad,)

def back_keep(v):
    return (v, None)

def back_low(kept, grad):
    return (low(grad),)
low.defvjp(low_keep, low_pass)
low_back.defvjp(back_keep, back_low)

def matmul_high(left, right):
    return jnp.dot(left, right, precision=lax.Precision.HIGHEST, preferred_element_type=jnp.float32)

def rms_norm(values, gain):
    inv_rms = lax.rsqrt(lax.optimization_barrier(jnp.mean(values * values, axis=-1, keepdims=True)) + EPS)
    return values * inv_rms * gain

def rope_tables(positions, head_dim):
    half_dim = head_dim // 2
    frequency = ROPE_BASE ** (-(jnp.arange(half_dim, dtype=jnp.float32) * (2.0 / head_dim)))
    angles = positions.astype(jnp.float32)[:, None] * frequency[None, :]
    return (jnp.cos(angles), jnp.sin(angles))

def rotate(values, cosine, sine_table):
    half_dim = values.shape[-1] // 2
    lower_half = values[..., :half_dim]
    upper_half = values[..., half_dim:]
    cosine = cosine[:, None, :]
    sine_table = sine_table[:, None, :]
    return jnp.concatenate([lower_half * cosine - upper_half * sine_table, upper_half * cosine + lower_half * sine_table], axis=-1)

def layout(lengths_row, positions):
    doc_ends = jnp.cumsum(lengths_row)
    passed = positions[:, None] >= doc_ends[None, :]
    doc_ids = lax.optimization_barrier(jnp.sum(passed.astype(jnp.int32), axis=1))
    doc_start = lax.optimization_barrier(jnp.sum(jnp.where(passed, lengths_row[None, :], 0), axis=1))
    return (doc_ids, positions - doc_start)

def attend(packed):
    query, keys, values, lengths_row = packed
    doc_ids = layout(lengths_row, jnp.arange(LENGTH, dtype=jnp.int32))[0]
    grouped = query.reshape(LENGTH, KV_HEADS, HEADS // KV_HEADS, HD)
    scores = jnp.einsum('tkgd,skd->kgts', grouped, keys, precision=lax.Precision.HIGHEST) / math.sqrt(HD)
    scores = low_back(scores)
    same_doc = doc_ids[:, None] == doc_ids[None, :]
    scores = jnp.where(same_doc[None, None], scores, -1e+30)
    attn_probs = jax.nn.softmax(scores, axis=-1)
    attn_mixed = jnp.einsum('kgts,skd->tkgd', low(attn_probs), values, precision=lax.Precision.HIGHEST)
    live_rows = (doc_ids < DOCS).astype(jnp.float32)
    return attn_mixed.reshape(LENGTH, QDIM) * live_rows[:, None]

def block_forward(tokens, norm1_gain, w_query, w_key, w_value, query_gain, key_gain, w_out, norm2_gain, w_router, w_gate, w_up, w_down, lengths, routes):
    normed_one = low(rms_norm(tokens, norm1_gain))
    query_pre = low_back(matmul_high(normed_one, w_query))
    key_pre = low_back(matmul_high(normed_one, w_key))
    value_pre = low_back(matmul_high(normed_one, w_value))
    positions = jnp.arange(LENGTH, dtype=jnp.int32)
    rope_pos = jax.vmap(lambda lengths_row: layout(lengths_row, positions)[1])(lengths).reshape(TOKENS)
    cosine, sine_table = rope_tables(rope_pos, HD)
    query = low(rotate(rms_norm(query_pre.reshape(TOKENS, HEADS, HD), query_gain), cosine, sine_table))
    keys = low(rotate(rms_norm(key_pre.reshape(TOKENS, KV_HEADS, HD), key_gain), cosine, sine_table))
    values = low(value_pre)
    attn_mixed = lax.map(jax.checkpoint(attend), (query.reshape(SEQS, LENGTH, HEADS, HD), keys.reshape(SEQS, LENGTH, KV_HEADS, HD), values.reshape(SEQS, LENGTH, KV_HEADS, HD), lengths))
    attn_low = low(low_back(attn_mixed.reshape(TOKENS, QDIM)))
    middle = tokens + low_back(matmul_high(attn_low, w_out))
    routed_low = low(rms_norm(middle, norm2_gain))
    logits = matmul_high(routed_low, w_router)
    chosen = jnp.take_along_axis(logits, routes, axis=1)
    gate_weights = jax.nn.softmax(chosen, axis=-1)
    flat_experts = routes.reshape(-1)
    flat_gates = gate_weights.reshape(-1)
    rows_most = CAP * N_EXPERT * N_SHARD

    def expert_term(token_ids, weight, expert_id):
        rows_in = low_back(routed_low[token_ids])
        gate_pre = low_back(matmul_high(rows_in, w_gate[expert_id]))
        up_pre = low_back(matmul_high(rows_in, w_up[expert_id]))
        activated = low(jax.nn.silu(gate_pre) * up_pre)
        expert_rows = low(low_back(matmul_high(activated, w_down[expert_id])))
        return expert_rows * weight[:, None]
    checked_term = jax.checkpoint(expert_term)

    def accumulate(running, expert_id):
        member = flat_experts == expert_id
        picked = jnp.nonzero(member, size=rows_most, fill_value=0)[0].astype(jnp.int32)
        live = (jnp.arange(rows_most, dtype=jnp.int32) < jnp.sum(member.astype(jnp.int32))).astype(jnp.float32)
        token_ids = picked // TOPK
        weight = flat_gates[picked] * live
        return (running.at[token_ids].add(checked_term(token_ids, weight, expert_id)), None)
    expert_mix = lax.scan(accumulate, jnp.zeros((TOKENS, D), jnp.float32), jnp.arange(EXPERTS, dtype=jnp.int32))[0]
    return middle + expert_mix

def reference(tokens, lengths, routes, norm1_gain, w_query, w_key, w_value, query_gain, key_gain, w_out, norm2_gain, w_router, w_gate, w_up, w_down, cotangent):
    floats = tuple((member_array.astype(jnp.float32) for member_array in (tokens, norm1_gain, w_query, w_key, w_value, query_gain, key_gain, w_out, norm2_gain, w_router, w_gate, w_up, w_down)))

    def forward(*params):
        return block_forward(*params, lengths, routes)
    result, pullback = jax.vjp(forward, *floats)
    gradients = pullback(cotangent.astype(jnp.float32))
    return (result.astype(jnp.bfloat16), gradients[0], gradients[1], gradients[2], gradients[3], gradients[4], gradients[5], gradients[6], gradients[7], gradients[8], gradients[9], gradients[10], gradients[11], gradients[12])
```

```python
import math

import jax
import jax.numpy as jnp
from jax import lax
from jax.experimental import pallas as pl
from jax.experimental.pallas import tpu as pltpu
from jax.sharding import PartitionSpec as P

CAP = 96
EPS = 1e-06
ROPE_BASE = 10000.0
BF = jnp.bfloat16
F32 = jnp.float32
MESH = pl.DeviceIdType.MESH
ANY = pl.BlockSpec(memory_space=pl.ANY)
VMEM = pl.BlockSpec(memory_space=pltpu.VMEM)
MIB = 1 << 20
W_COLS = 3328
W_HALF = W_COLS // 2
ROWS = 256
BLOCK = 272
HALF = 128


class Place:
    def __init__(self):
        self.expert = lax.axis_index("expert")
        self.x = lax.axis_index("shard")
        self.core = self.expert % 2
        self.chip = self.expert // 2
        y, z = self.chip % 4, self.chip // 4
        self.first = z + self.core * (y - z)
        self.second = y + self.core * (z - y)
        self.first_stride = 8 - 6 * self.core
        self.second_stride = 2 + 6 * self.core

    def block(self, first, second):
        return ((self.first + first + 4) % 4) * 4 + (self.second + second + 4) % 4

    def at(self, first, second):
        near = ((self.first + first + 4) % 4) * self.first_stride
        return {"expert": near + ((self.second + second + 4) % 4) * self.second_stride + self.core}

    def along_x(self, step):
        return {"shard": (self.x + step + 4) % 4}

    def sibling(self):
        return {"expert": self.expert + 1 - 2 * self.core}


def greet(devices):
    barrier = pltpu.get_barrier_semaphore()
    for device in devices:
        pl.semaphore_signal(barrier, inc=1, device_id=device, device_id_type=MESH)
    pl.semaphore_wait(barrier, len(devices))


class Copy:
    def __init__(self, *parts):
        self.parts = parts

    def made(self):
        return pltpu.make_async_remote_copy(*self.parts, device_id_type=MESH)

    def start(self):
        self.made().start()

    def wait_send(self):
        self.made().wait_send()

    def wait_recv(self):
        self.made().wait_recv()


class Wires:
    def __init__(self, send, recv):
        self.send, self.recv = send, recv

    def copy(self, source, target, number, device):
        return Copy(source, target, self.send.at[number], self.recv.at[number], device)


class GatherRing:
    def __init__(self, wires, base, at, own, right, left, half, rows):
        low, high, full = pl.ds(0, half), pl.ds(half, rows - half), pl.ds(0, rows)
        copy = wires.copy
        self.go = [copy(own, at(0, full), base, right), copy(own, at(0, full), base + 1, left)]
        self.came = [copy(at(-1, full), at(-1, full), base, right), copy(at(1, full), at(1, full), base + 1, left)]
        self.on = [copy(at(-1, low), at(-1, low), base + 2, right), copy(at(1, high), at(1, high), base + 3, left)]
        self.far = [copy(at(2, low), at(2, low), base + 2, right), copy(at(2, high), at(2, high), base + 3, left)]

    def start(self):
        for step in self.go:
            step.start()

    def forward(self, way):
        self.came[way].wait_recv()
        self.on[way].start()

    def wait_far(self):
        for step in self.far:
            step.wait_recv()

    def wait_sent(self):
        for step in self.go + self.on:
            step.wait_send()


class ReduceRing:
    def __init__(self, wires, base, at, near, landing, right, left, half, rows):
        low, high, full = pl.ds(0, half), pl.ds(half, rows - half), pl.ds(0, rows)
        copy = wires.copy
        self.at, self.near, self.landing = at, near, landing
        self.parts = [low, high, full]
        self.far = [copy(at(2, low), near(low), base, right), copy(at(2, high), near(high), base + 1, left)]
        self.mid = [copy(at(1, full), landing(0), base + 2, right), copy(at(-1, full), landing(1), base + 3, left)]

    def start(self):
        for step in self.far:
            step.start()

    def middle(self, way):
        self.far[way].wait_recv()
        side = 1 - 2 * way
        add_into(self.at(side, self.parts[way]), self.near(self.parts[way]))
        self.mid[way].start()

    def finish(self):
        for step in self.mid:
            step.wait_recv()
        add_into(self.at(0, self.parts[2]), self.landing(0), self.landing(1))

    def wait_sent(self):
        for step in self.far + self.mid:
            step.wait_send()


def add_into(target, *terms):
    rows = target.shape[0]

    @pl.loop(0, rows // 16)
    def _(i):
        here = pl.ds(pl.multiple_of(i * 16, 16), 16)
        total = target[here, :].astype(F32)
        for term in terms:
            total = total + term[here, :].astype(F32)
        target[here, :] = total.astype(target.dtype)


def dot(a, b, contract=((1,), (0,))):
    return lax.dot_general(a, b, (contract, ((), ())), preferred_element_type=F32)


NT = ((1,), (1,))
TN = ((0,), (0,))


def call(kernel, out_shape, in_specs, out_specs, scratch, ident, vmem=56):
    return pl.pallas_call(
        kernel,
        out_shape=out_shape,
        in_specs=in_specs,
        out_specs=out_specs,
        scratch_shapes=scratch,
        compiler_params=pltpu.CompilerParams(
            collective_id=ident, has_side_effects=True, vmem_limit_bytes=vmem * MIB
        ),
    )


def gather_kernel(
    wall, wg, wu, wd, g, wall_full, wg_full, wu_full, wd_full, g_all, local, w_send, w_recv, e_send, e_recv, g_send, g_recv
):
    me = Place()
    x, core = me.x, me.core
    right, left, sibling = me.along_x(1), me.along_x(-1), me.sibling()
    greet([right, left, sibling, me.at(1, 0), me.at(-1, 0), me.at(0, 1), me.at(0, -1)])
    w_wires, e_wires, g_wires = Wires(w_send, w_recv), Wires(e_send, e_recv), Wires(g_send, g_recv)
    cols = pl.ds(pl.multiple_of(core * W_HALF, 128), W_HALF)

    def shard(step):
        return (x + step + 4) % 4

    def w_at(k, rows):
        return wall_full.at[shard(k), rows, cols]

    def slice_of(k):
        return pl.ds(pl.multiple_of(shard(k) * 128, 128), 128)

    w_ring = GatherRing(w_wires, 0, w_at, wall.at[:, cols], right, left, HALF, ROWS)
    w_ring.start()
    first = GatherRing(
        g_wires, 0, lambda k, rows: g_all.at[me.block(k, 0), rows], g, me.at(1, 0), me.at(-1, 0), HALF, BLOCK
    )
    first.start()

    def second(fo, base, own=None):
        own = g_all.at[me.block(fo, 0)] if own is None else own
        return GatherRing(
            g_wires, base, lambda k, rows: g_all.at[me.block(fo, k), rows], own, me.at(0, 1), me.at(0, -1), HALF, BLOCK
        )

    seconds = [second(0, 4, g), second(-1, 8), second(1, 12), second(2, 16)]
    seconds[0].start()
    own_copies = [
        pltpu.make_async_copy(wall, wall_full.at[x], local.at[0]),
        pltpu.make_async_copy(wg, wg_full.at[core, :, slice_of(0)], local.at[1]),
        pltpu.make_async_copy(wu, wu_full.at[core, :, slice_of(0)], local.at[2]),
        pltpu.make_async_copy(wd, wd_full.at[core, slice_of(0), :], local.at[3]),
        pltpu.make_async_copy(g, g_all.at[me.block(0, 0)], local.at[4]),
    ]
    for step in own_copies:
        step.start()

    def g_at(k):
        return wg_full.at[core, :, slice_of(k)]

    def u_at(k):
        return wu_full.at[core, :, slice_of(k)]

    def d_at(k, start=0, size=128):
        return wd_full.at[core, pl.ds(pl.multiple_of(shard(k) * 128 + start, 64), size), :]

    def e_copy(ref, number, device, own=None):
        return e_wires.copy(ref if own is None else own, ref, number, device)

    e_go = [
        e_copy(at(0), way * 3 + i, device, own)
        for way, device in enumerate((right, left))
        for i, (at, own) in enumerate(((g_at, wg), (u_at, wu), (d_at, wd)))
    ]
    e_came = [e_copy(at(side), way * 3 + i, right) for way, side in enumerate((-1, 1)) for i, at in enumerate((g_at, u_at, d_at))]
    e_on = [
        e_copy(g_at(-1), 6, right),
        e_copy(d_at(-1, 0, 64), 7, right),
        e_copy(u_at(1), 8, left),
        e_copy(d_at(1, 64, 64), 9, left),
    ]
    e_far = [e_copy(g_at(2), 6, right), e_copy(d_at(2, 0, 64), 7, right), e_copy(u_at(2), 8, left), e_copy(d_at(2, 64, 64), 9, left)]
    e_pair = [e_copy(ref.at[core], 10 + i, sibling) for i, ref in enumerate((wg_full, wu_full, wd_full))]
    e_pair_came = [e_copy(ref.at[1 - core], 10 + i, sibling) for i, ref in enumerate((wg_full, wu_full, wd_full))]

    other = pl.ds(pl.multiple_of((1 - core) * W_HALF, 128), W_HALF)

    def w_pair(k, number):
        return w_wires.copy(w_at(k, pl.ds(0, ROWS)), w_at(k, pl.ds(0, ROWS)), number, sibling)

    def w_pair_came(k, number):
        ref = wall_full.at[shard(k), :, other]
        return w_wires.copy(ref, ref, number, sibling)

    pairs = [w_pair(-1, 4), w_pair(1, 5), w_pair(2, 6)]
    w_ring.forward(0)
    pairs[0].start()
    w_ring.forward(1)
    pairs[1].start()
    for step in e_go:
        step.start()
    first.forward(0)
    seconds[1].start()
    first.forward(1)
    seconds[2].start()
    seconds[0].forward(0)
    seconds[0].forward(1)
    w_ring.wait_far()
    pairs[2].start()
    first.wait_far()
    seconds[3].start()
    for i in range(3):
        e_came[i].wait_recv()
    e_on[0].start()
    e_on[1].start()
    for i in range(3, 6):
        e_came[i].wait_recv()
    e_on[2].start()
    e_on[3].start()
    for step in seconds[1:3]:
        step.forward(0)
        step.forward(1)
    for step in e_far:
        step.wait_recv()
    for step in own_copies:
        step.wait()
    for step in e_pair:
        step.start()
    seconds[3].forward(0)
    seconds[3].forward(1)
    for i, k in enumerate((-1, 1, 2)):
        w_pair_came(k, 4 + i).wait_recv()
    for step in e_pair_came:
        step.wait_recv()
    for ring in seconds:
        ring.wait_far()
    for ring in [w_ring, first] + seconds:
        ring.wait_sent()
    for step in pairs + e_go + e_on + e_pair:
        step.wait_send()


def gather_all(wall, wg, wu, wd, g):
    dma = pltpu.SemaphoreType.DMA
    return call(
        gather_kernel,
        (
            jax.ShapeDtypeStruct((4, ROWS, W_COLS), BF),
            jax.ShapeDtypeStruct((2, 1024, 512), BF),
            jax.ShapeDtypeStruct((2, 1024, 512), BF),
            jax.ShapeDtypeStruct((2, 512, 1024), BF),
            jax.ShapeDtypeStruct((16, BLOCK, 1024), BF),
        ),
        [ANY] * 5,
        (ANY,) * 5,
        [dma((5,)), dma((7,)), dma((7,)), dma((13,)), dma((13,)), dma((20,)), dma((20,))],
        0,
        vmem=16,
    )(wall, wg, wu, wd, g)


def expert_kernel(
    h_ref,
    g_ref,
    wg,
    wu,
    wd,
    wr,
    dx_out,
    y_out,
    gw_out,
    uw_out,
    dw_out,
    buf,
    gbuf,
    acc_g,
    acc_u,
    acc_d,
    near,
    landing,
    near_f,
    landing_f,
    xb,
    gxb,
    yb,
    act,
    dgb,
    dub,
    hot,
    weight,
    dgate,
    ystage,
    a_send,
    a_recv,
    r_send,
    r_recv,
    local,
    g_local,
    y_local,
):
    me = Place()
    f_right, f_left, s_right, s_left = me.at(1, 0), me.at(-1, 0), me.at(0, 1), me.at(0, -1)
    greet([f_right, f_left, s_right, s_left])
    a_wires, r_wires = Wires(a_send, a_recv), Wires(r_send, r_recv)
    own = buf.at[me.block(0, 0), pl.ds(0, ROWS)]
    fetch = pltpu.make_async_copy(h_ref, own, local.at[0])
    fetch.start()

    def order(i):
        return (3 * i + (i // 2) * (3 + 2 * (i % 2))) % 4

    first = GatherRing(
        a_wires, 0, lambda k, rows: buf.at[me.block(k, 0), rows], own, f_right, f_left, HALF, ROWS
    )

    def second(i):
        fo = order(i)

        def at(k, rows):
            return buf.at[me.block(fo, k), rows]

        return GatherRing(a_wires, 4 + 4 * i, at, at(0, pl.ds(0, ROWS)), s_right, s_left, HALF, ROWS)

    def reduce_second(i):
        fo = order(i)
        return ReduceRing(
            r_wires,
            4 + 4 * i,
            lambda k, rows: buf.at[me.block(fo, k), rows],
            lambda rows: near.at[i, rows],
            lambda way: landing.at[i, way],
            s_right,
            s_left,
            HALF,
            BLOCK,
        )

    reduce_first = ReduceRing(
        r_wires,
        0,
        lambda k, rows: buf.at[me.block(k, 0), rows],
        lambda rows: near_f.at[rows],
        lambda way: landing_f.at[way],
        f_right,
        f_left,
        HALF,
        BLOCK,
    )

    def load_g(i):
        start = ((me.first + order(i)) % 4) * 4
        return pltpu.make_async_copy(g_ref.at[pl.ds(start, 4)], gbuf.at[i % 2], g_local.at[i % 2])

    def store_y(i, j):
        return pltpu.make_async_copy(ystage.at[j], y_out.at[((me.first + order(i)) % 4) * 4 + j], y_local.at[j])

    fetch.wait()
    first.start()
    second(0).start()
    load_g(0).start()
    for acc in (acc_g, acc_u, acc_d):

        @pl.loop(0, acc.shape[1] // 32)
        def _(r):
            acc[:, pl.ds(pl.multiple_of(r * 32, 32), 32), :] = jnp.zeros((2, 32, acc.shape[2]), F32)

    first.forward(0)
    second(1).start()
    first.forward(1)
    second(2).start()
    second(0).forward(0)
    second(0).forward(1)
    first.wait_far()
    second(3).start()

    expert_row = lax.broadcasted_iota(jnp.int32, (32, 256), 0)
    slot_row = lax.broadcasted_iota(jnp.int32, (CAP, 256), 0).astype(F32)
    low_row = lax.broadcasted_iota(jnp.int32, (8, 1024), 0)
    quarter = lax.broadcasted_iota(jnp.int32, (8, 1024), 1) // 256
    my_quarter = quarter == me.chip // 4
    my_low = 2 * (me.chip % 4)

    def pick(table, e):
        return jnp.sum(jnp.where(expert_row == 2 * me.chip + e, table, 0.0), axis=0, keepdims=True)

    @pl.loop(0, 4)
    def _(i):
        base = ((me.first + order(i)) % 4) * 4
        slot = i % 2
        second(i).wait_far()

        @pl.when(i < 3)
        def _():
            load_g(i + 1).start()

        load_g(i).wait()

        @pl.loop(0, 4)
        def _(j):
            h = buf[base + j, pl.ds(0, ROWS), :]
            g = gbuf[slot, j, pl.ds(0, ROWS), :]
            packed = gbuf[slot, j, pl.ds(ROWS, 16), :].astype(F32)[0:8]
            places = jnp.concatenate([packed[:, q * 256 : (q + 1) * 256] for q in range(4)], axis=0)
            logits = dot(wr[...], h, NT)
            routed = places >= 0.0
            top = jnp.max(jnp.where(routed, logits, -1e30), axis=0, keepdims=True)
            terms = jnp.where(routed, jnp.exp(jnp.where(routed, logits - top, 0.0)), 0.0)
            gates = terms / jnp.sum(terms, axis=0, keepdims=True)
            for e in range(2):
                hit = pick(places, e) == slot_row
                rows = pl.ds(e * CAP, CAP)
                weight[j, rows, :] = jnp.sum(jnp.where(hit, pick(gates, e), 0.0), axis=1, keepdims=True)
                hot[j, rows, :] = hit.astype(F32).astype(BF)
            xb[j] = dot(hot[j], h).astype(BF)
            gx = dot(hot[j], g)
            gxb[j] = gx.astype(BF)

        @pl.when(i < 3)
        def _():
            second(i + 1).forward(0)
            second(i + 1).forward(1)

        @pl.loop(0, 2)
        def _(e):
            rows = pl.ds(pl.multiple_of(e * CAP, 32), CAP)
            x = xb[:, rows, :].reshape(4 * CAP, 1024)
            gx = gxb[:, rows, :].reshape(4 * CAP, 1024)
            gate = weight[:, rows, :].reshape(4 * CAP, 1)
            dy = (gate * gx.astype(F32)).astype(BF)
            gate_pre = dot(x, wg[e])
            up_pre = dot(x, wu[e])
            grad_act = dot(dy, wd[e], NT)
            sig = 1.0 / (1.0 + jnp.exp(-gate_pre))
            silu = gate_pre * sig
            active = (silu * up_pre).astype(BF)
            grad_gate = (grad_act * up_pre * (sig * (1.0 + gate_pre * (1.0 - sig)))).astype(BF)
            grad_up = (grad_act * silu).astype(BF)
            act[:, rows, :] = active.reshape(4, CAP, 512)
            dgb[:, rows, :] = grad_gate.reshape(4, CAP, 512)
            dub[:, rows, :] = grad_up.reshape(4, CAP, 512)
            out = dot(active, wd[e]).astype(BF).astype(F32)
            dgate[:, rows, :] = jnp.sum(gx.astype(F32) * out, axis=1, keepdims=True).reshape(4, CAP, 1)
            yb[:, rows, :] = (gate * out).astype(BF).reshape(4, CAP, 1024)

        second(i).wait_sent()

        @pl.when(i == 0)
        def _():
            for step in first.go:
                step.wait_send()

        @pl.when(i == 1)
        def _():
            first.on[0].wait_send()

        @pl.when(i == 2)
        def _():
            first.on[1].wait_send()

        @pl.loop(0, 4)
        def _(j):
            @pl.when(i > 0)
            def _():
                store_y(i - 1, j).wait()

            ystage[j] = dot(hot[j], yb[j], TN).astype(BF)
            store_y(i, j).start()
            spots = hot[j].astype(F32) * dgate[j]
            grad_rows = [jnp.sum(spots[e * CAP : (e + 1) * CAP], axis=0, keepdims=True) for e in range(2)]
            wide = [jnp.concatenate([row] * 4, axis=1) for row in grad_rows]
            mine = jnp.where(low_row == my_low, wide[0], jnp.where(low_row == my_low + 1, wide[1], 0.0))
            mine = jnp.where(my_quarter, mine, 0.0)
            high = mine.astype(BF).astype(F32)
            buf[base + j, pl.ds(ROWS, 16), :] = jnp.concatenate([high, mine - high], axis=0).astype(BF)

        @pl.loop(0, 2)
        def _(e):
            rows = pl.ds(pl.multiple_of(e * CAP, 32), CAP)
            grad_in = dot(dgb[:, rows, :].reshape(4 * CAP, 512), wg[e], NT)
            grad_in = grad_in + dot(dub[:, rows, :].reshape(4 * CAP, 512), wu[e], NT)
            yb[:, rows, :] = grad_in.astype(BF).reshape(4, CAP, 1024)

        @pl.loop(0, 4)
        def _(j):
            buf[base + j, pl.ds(0, ROWS), :] = dot(hot[j], yb[j], TN).astype(BF)

        reduce_second(i).start()

        @pl.when(i > 0)
        def _():
            reduce_second(i - 1).middle(0)
            reduce_second(i - 1).middle(1)

        @pl.loop(0, 2)
        def _(e):
            rows = pl.ds(pl.multiple_of(e * CAP, 32), CAP)
            x = xb[:, rows, :].reshape(4 * CAP, 1024)
            gate = weight[:, rows, :].reshape(4 * CAP, 1)
            dy = (gate * gxb[:, rows, :].reshape(4 * CAP, 1024).astype(F32)).astype(BF)
            grad_gate = dgb[:, rows, :].reshape(4 * CAP, 512)
            grad_up = dub[:, rows, :].reshape(4 * CAP, 512)
            active = act[:, rows, :].reshape(4 * CAP, 512)
            acc_g[e] += dot(x, grad_gate, TN)
            acc_u[e] += dot(x, grad_up, TN)
            acc_d[e] += dot(active, dy, TN)

        @pl.when(i > 1)
        def _():
            reduce_second(i - 2).finish()

    reduce_second(3).middle(0)
    reduce_second(3).middle(1)
    reduce_second(2).finish()
    reduce_second(3).finish()
    reduce_first.start()
    for j in range(4):
        store_y(3, j).wait()

    def stage(slot, width):
        return ystage.at[slot] if width == 1024 else ystage.at[slot, :, pl.ds(0, width)]

    def drain(acc, out):
        width = acc.shape[2]
        blocks = acc.shape[1] // 256

        def leave(n, slot):
            rows = pl.ds(pl.multiple_of((n % blocks) * 256, 256), 256)
            return pltpu.make_async_copy(stage(slot, width), out.at[n // blocks, rows, :], y_local.at[slot])

        @pl.loop(0, 2 * blocks // 4)
        def _(n):
            for slot in range(4):
                number = n * 4 + slot

                @pl.when(n > 0)
                def _():
                    leave(number - 4, slot).wait()

                rows = pl.ds(pl.multiple_of((number % blocks) * 256, 256), 256)
                ystage[slot, :, pl.ds(0, width)] = acc[number // blocks, rows, :].astype(BF)
                leave(number, slot).start()

        for slot in range(4):
            leave(2 * blocks - 4 + slot, slot).wait()

    reduce_first.middle(0)
    reduce_first.middle(1)
    drain(acc_g, gw_out)
    drain(acc_u, uw_out)
    drain(acc_d, dw_out)
    reduce_first.finish()
    dx_out[...] = buf[me.block(0, 0)]
    for step in range(4):
        reduce_second(step).wait_sent()
    reduce_first.wait_sent()


def expert_stage(h, g_all, wg, wu, wd, router):
    dma = pltpu.SemaphoreType.DMA
    return call(
        expert_kernel,
        (
            jax.ShapeDtypeStruct((BLOCK, 1024), BF),
            jax.ShapeDtypeStruct((16, ROWS, 1024), BF),
            jax.ShapeDtypeStruct((2, 1024, 512), BF),
            jax.ShapeDtypeStruct((2, 1024, 512), BF),
            jax.ShapeDtypeStruct((2, 512, 1024), BF),
        ),
        [ANY, ANY, VMEM, VMEM, VMEM, VMEM],
        (VMEM, ANY, ANY, ANY, ANY),
        [
            pltpu.VMEM((16, BLOCK, 1024), BF),
            pltpu.VMEM((2, 4, BLOCK, 1024), BF),
            pltpu.VMEM((2, 1024, 512), F32),
            pltpu.VMEM((2, 1024, 512), F32),
            pltpu.VMEM((2, 512, 1024), F32),
            pltpu.VMEM((4, BLOCK, 1024), BF),
            pltpu.VMEM((4, 2, BLOCK, 1024), BF),
            pltpu.VMEM((BLOCK, 1024), BF),
            pltpu.VMEM((2, BLOCK, 1024), BF),
            pltpu.VMEM((4, 2 * CAP, 1024), BF),
            pltpu.VMEM((4, 2 * CAP, 1024), BF),
            pltpu.VMEM((4, 2 * CAP, 1024), BF),
            pltpu.VMEM((4, 2 * CAP, 512), BF),
            pltpu.VMEM((4, 2 * CAP, 512), BF),
            pltpu.VMEM((4, 2 * CAP, 512), BF),
            pltpu.VMEM((4, 2 * CAP, 256), BF),
            pltpu.VMEM((4, 2 * CAP, 1), F32),
            pltpu.VMEM((4, 2 * CAP, 1), F32),
            pltpu.VMEM((4, ROWS, 1024), BF),
            dma((20,)),
            dma((20,)),
            dma((20,)),
            dma((20,)),
            dma((1,)),
            dma((2,)),
            dma((4,)),
        ],
        1,
        vmem=62,
    )(h, g_all, wg, wu, wd, router)


def reduce_kernel(
    gw,
    uw,
    dw,
    wall,
    y,
    g_out,
    u_out,
    d_out,
    w_out,
    y_out,
    own_g,
    own_u,
    own_d,
    pair_g,
    pair_u,
    pair_d,
    near_g,
    near_u,
    near_d,
    land_g,
    land_u,
    land_d,
    own_w,
    pair_w,
    near_w,
    land_w,
    part_f,
    part_s,
    total_w,
    buf,
    near_s,
    land_s,
    near_f,
    land_f,
    e_send,
    e_recv,
    w_send,
    w_recv,
    p_send,
    p_recv,
    y_send,
    y_recv,
    local,
):
    me = Place()
    x, core = me.x, me.core
    right, left, sibling = me.along_x(1), me.along_x(-1), me.sibling()
    planes = [me.at(1, 0), me.at(-1, 0), me.at(2, 0), me.at(0, 1), me.at(0, -1), me.at(0, 2)]
    greet([right, left, sibling] + planes)
    e_wires, w_wires = Wires(e_send, e_recv), Wires(w_send, w_recv)
    p_wires, y_wires = Wires(p_send, p_recv), Wires(y_send, y_recv)
    cols = pl.ds(pl.multiple_of(core * W_HALF, 128), W_HALF)
    other = pl.ds(pl.multiple_of((1 - core) * W_HALF, 128), W_HALF)

    def shard(step):
        return (x + step + 4) % 4

    pulls = [
        pltpu.make_async_copy(wall.at[:, :, cols], own_w, local.at[0]),
        pltpu.make_async_copy(gw.at[core], own_g, local.at[1]),
        pltpu.make_async_copy(uw.at[core], own_u, local.at[2]),
        pltpu.make_async_copy(dw.at[core], own_d, local.at[3]),
        pltpu.make_async_copy(y, buf, local.at[4]),
    ]
    for step in pulls:
        step.start()
    w_pair = w_wires.copy(wall.at[:, :, other], pair_w, 0, sibling)
    w_pair.start()
    e_pair = [
        e_wires.copy(ref.at[1 - core], land, i, sibling)
        for i, (ref, land) in enumerate(((gw, pair_g), (uw, pair_u), (dw, pair_d)))
    ]
    for step in e_pair:
        step.start()

    def order(i):
        return (3 * i + (i // 2) * (3 + 2 * (i % 2))) % 4

    def y_second(i):
        fo = order(i)
        return ReduceRing(
            y_wires,
            4 + 4 * i,
            lambda k, rows: buf.at[me.block(fo, k), rows],
            lambda rows: near_s.at[i, rows],
            lambda way: land_s.at[i, way],
            me.at(0, 1),
            me.at(0, -1),
            HALF,
            ROWS,
        )

    y_first = ReduceRing(
        y_wires,
        0,
        lambda k, rows: buf.at[me.block(k, 0), rows],
        lambda rows: near_f.at[rows],
        lambda way: land_f.at[way],
        me.at(1, 0),
        me.at(-1, 0),
        HALF,
        ROWS,
    )
    pulls[4].wait()
    y_rings = [y_second(i) for i in range(4)]
    for ring in y_rings:
        ring.start()

    w_ring = ReduceRing(
        w_wires,
        1,
        lambda k, rows: own_w.at[shard(k), rows],
        lambda rows: near_w.at[rows],
        lambda way: land_w.at[way],
        right,
        left,
        HALF,
        ROWS,
    )
    pulls[0].wait()
    w_pair.wait_recv()
    for k in (2, 1, -1, 0):
        add_into(own_w.at[shard(k)], pair_w.at[shard(k)])
        if k == 2:
            w_ring.start()
    for i, (own, land) in enumerate(((own_g, pair_g), (own_u, pair_u), (own_d, pair_d))):
        pulls[1 + i].wait()
        e_pair[i].wait_recv()
        add_into(own, land)

    def slice_of(k):
        return pl.ds(pl.multiple_of(shard(k) * 128, 128), 128)

    def g_at(k):
        return own_g.at[:, slice_of(k)]

    def u_at(k):
        return own_u.at[:, slice_of(k)]

    def d_at(k, start=0, size=128):
        return own_d.at[pl.ds(pl.multiple_of(shard(k) * 128 + start, 64), size), :]

    e_far = [
        e_wires.copy(g_at(2), near_g, 3, right),
        e_wires.copy(d_at(2, 0, 64), near_d.at[0], 4, right),
        e_wires.copy(u_at(2), near_u, 5, left),
        e_wires.copy(d_at(2, 64, 64), near_d.at[1], 6, left),
    ]
    w_ring.middle(0)
    w_ring.middle(1)
    for step in e_far:
        step.start()
    w_ring.finish()

    def piece(base, size, k, at):
        return pl.ds(pl.multiple_of(base + ((at + k + 4) % 4) * size, 16), size)

    mine = own_w.at[x]

    def spread(source, device, land, number):
        return p_wires.copy(source, land, number, device)

    far_f = [
        spread(mine.at[piece(0, 64, k, me.first), :], me.at(k, 0), part_f.at[n], n) for n, k in enumerate((1, 2, 3))
    ]
    for step in far_f:
        step.start()

    e_far[0].wait_recv()
    add_into(g_at(1), near_g)
    e_far[1].wait_recv()
    add_into(d_at(1, 0, 64), near_d.at[0])
    e_mid = [
        e_wires.copy(ref, land.at[way], 7 + way * 3 + i, device)
        for way, (k, device) in enumerate(((1, right), (-1, left)))
        for i, (ref, land) in enumerate(((g_at(k), land_g), (u_at(k), land_u), (d_at(k), land_d)))
    ]
    for step in e_mid[:3]:
        step.start()
    e_far[2].wait_recv()
    add_into(u_at(-1), near_u)
    e_far[3].wait_recv()
    add_into(d_at(-1, 64, 64), near_d.at[1])
    for step in e_mid[3:]:
        step.start()

    for ring in y_rings:
        ring.middle(0)
        ring.middle(1)

    base_f = me.first * 64
    for step in far_f:
        step.wait_recv()
    add_into(mine.at[piece(0, 64, 0, me.first), :], *[part_f.at[n] for n in range(3)])
    far_s = [
        spread(mine.at[piece(base_f, 16, k, me.second), :], me.at(0, k), part_s.at[n], 3 + n)
        for n, k in enumerate((1, 2, 3))
    ]
    for step in far_s:
        step.start()
    for ring in y_rings:
        ring.finish()
    y_first.start()
    for step in far_s:
        step.wait_recv()
    final = piece(base_f, 16, 0, me.second)
    add_into(mine.at[final, :], *[part_s.at[n] for n in range(3)])
    total_w[core, final, :] = mine[final, :]

    def gather(k, number, rows, device):
        here = total_w.at[core, rows]
        return p_wires.copy(here, here, number, device)

    out_s = [gather(k, 6 + n, final, me.at(0, k)) for n, k in enumerate((1, 2, 3))]
    in_s = [gather(k, 6 + n, piece(base_f, 16, -k, me.second), me.at(0, k)) for n, k in enumerate((1, 2, 3))]
    for step in out_s:
        step.start()
    for step in e_mid:
        step.wait_recv()
    for out, at, land in ((g_out, g_at, land_g), (u_out, u_at, land_u), (d_out, d_at, land_d)):

        @pl.loop(0, out.shape[0] // 16)
        def _(i):
            here = pl.ds(pl.multiple_of(i * 16, 16), 16)
            out[here, :] = at(0)[here, :].astype(F32) + land[0, here, :].astype(F32) + land[1, here, :].astype(F32)

    for step in in_s:
        step.wait_recv()
    own_rows = piece(0, 64, 0, me.first)
    out_f = [gather(k, 9 + n, own_rows, me.at(k, 0)) for n, k in enumerate((1, 2, 3))]
    in_f = [gather(k, 9 + n, piece(0, 64, -k, me.first), me.at(k, 0)) for n, k in enumerate((1, 2, 3))]
    for step in out_f:
        step.start()
    y_first.middle(0)
    y_first.middle(1)
    for step in in_f:
        step.wait_recv()
    w_last = w_wires.copy(total_w.at[core], total_w.at[core], 5, sibling)
    w_last.start()
    y_first.finish()
    y_out[...] = buf[me.block(0, 0)]
    w_wires.copy(total_w.at[1 - core], total_w.at[1 - core], 5, sibling).wait_recv()

    @pl.loop(0, ROWS // 16)
    def _(i):
        here = pl.ds(pl.multiple_of(i * 16, 16), 16)
        for half in range(2):
            w_out[here, pl.ds(half * W_HALF, W_HALF)] = total_w[half, here, :].astype(F32)

    for step in [w_pair, w_last] + e_pair + e_far + e_mid + far_f + far_s + out_s + out_f:
        step.wait_send()
    for ring in y_rings + [y_first, w_ring]:
        ring.wait_sent()


def reduce_all(gw, uw, dw, wall, y):
    dma = pltpu.SemaphoreType.DMA
    v = pltpu.VMEM
    return call(
        reduce_kernel,
        (
            jax.ShapeDtypeStruct((1024, 128), F32),
            jax.ShapeDtypeStruct((1024, 128), F32),
            jax.ShapeDtypeStruct((128, 1024), F32),
            jax.ShapeDtypeStruct((ROWS, W_COLS), F32),
            jax.ShapeDtypeStruct((ROWS, 1024), BF),
        ),
        [ANY] * 5,
        (VMEM,) * 5,
        [
            v((1024, 512), BF),
            v((1024, 512), BF),
            v((512, 1024), BF),
            v((1024, 512), BF),
            v((1024, 512), BF),
            v((512, 1024), BF),
            v((1024, 128), BF),
            v((1024, 128), BF),
            v((2, 64, 1024), BF),
            v((2, 1024, 128), BF),
            v((2, 1024, 128), BF),
            v((2, 128, 1024), BF),
            v((4, ROWS, W_HALF), BF),
            v((4, ROWS, W_HALF), BF),
            v((ROWS, W_HALF), BF),
            v((2, ROWS, W_HALF), BF),
            v((3, 64, W_HALF), BF),
            v((3, 16, W_HALF), BF),
            v((2, ROWS, W_HALF), BF),
            v((16, ROWS, 1024), BF),
            v((4, ROWS, 1024), BF),
            v((4, 2, ROWS, 1024), BF),
            v((ROWS, 1024), BF),
            v((2, ROWS, 1024), BF),
            dma((13,)),
            dma((13,)),
            dma((6,)),
            dma((6,)),
            dma((12,)),
            dma((12,)),
            dma((20,)),
            dma((20,)),
            dma((5,)),
        ],
        2,
        vmem=56,
    )(gw, uw, dw, wall, y)


def rms_norm(values, gain):
    inv_rms = lax.rsqrt(jnp.mean(values * values, axis=-1, keepdims=True) + EPS)
    return values * inv_rms * gain


def rope_tables(positions, head_dim):
    half_dim = head_dim // 2
    frequency = ROPE_BASE ** (-(jnp.arange(half_dim, dtype=F32) * (2.0 / head_dim)))
    angles = positions.astype(F32)[:, None] * frequency[None, :]
    return (jnp.cos(angles), jnp.sin(angles))


def rotate(values, cosine, sine_table):
    half_dim = values.shape[-1] // 2
    lower_half = values[..., :half_dim]
    upper_half = values[..., half_dim:]
    cosine = cosine[:, None, :]
    sine_table = sine_table[:, None, :]
    return jnp.concatenate(
        [
            lower_half * cosine - upper_half * sine_table,
            upper_half * cosine + lower_half * sine_table,
        ],
        axis=-1,
    )


def layout(lengths_row, positions):
    doc_ends = jnp.cumsum(lengths_row)
    passed = positions[:, None] >= doc_ends[None, :]
    doc_ids = jnp.sum(passed.astype(jnp.int32), axis=1)
    doc_start = jnp.sum(jnp.where(passed, lengths_row[None, :], 0), axis=1)
    return (doc_ids, positions - doc_start)


def masked_scores(query_low, keys_low, same_doc, kv_heads, head_dim):
    grouped = query_low.reshape(query_low.shape[0], kv_heads, -1, head_dim)
    keyed = keys_low.reshape(keys_low.shape[0], kv_heads, head_dim)
    scores = jnp.einsum("tkgd,skd->kgts", grouped, keyed, preferred_element_type=F32) / math.sqrt(head_dim)
    return jnp.where(same_doc[None, None], scores, -1e30)


def body(
    tokens,
    lengths,
    routes,
    norm1_gain,
    w_query,
    w_key,
    w_value,
    query_gain,
    key_gain,
    w_out,
    norm2_gain,
    w_router,
    w_gate,
    w_up,
    w_down,
    cotangent,
):
    highest = lax.Precision.HIGHEST
    row_count = tokens.shape[0]
    length = row_count * 4
    heads, kv_heads, head_dim, experts, docs = 16, 8, 64, 32, 4
    group = heads // kv_heads
    inv_root = 1.0 / math.sqrt(head_dim)

    hits = jnp.sum((routes[:, :, None] == jnp.arange(experts, dtype=jnp.int32)).astype(F32), axis=1)
    before = (jnp.arange(row_count)[:, None] > jnp.arange(row_count)[None, :]).astype(BF)
    ranks = jnp.dot(before, hits.astype(BF), preferred_element_type=F32)
    hits_t = hits.T
    places = jnp.where(hits_t > 0, ranks.T, -1.0)
    packed = places.reshape(4, 8, row_count).transpose(1, 0, 2).reshape(8, 1024)
    g_block = jnp.concatenate([cotangent, packed.astype(BF), jnp.zeros((8, 1024), BF)], axis=0)

    def column(v):
        return jnp.pad(v.reshape(-1, 1), ((0, row_count - v.shape[0]), (0, 0)))

    extras = jnp.concatenate(
        [w_router, column(norm1_gain), column(norm2_gain), column(query_gain), column(key_gain), jnp.zeros((row_count, 220), BF)],
        axis=1,
    )
    wall = jnp.concatenate([w_query, w_key, w_value, w_out, extras], axis=1)
    wall_full, gate_full, up_full, down_full, g_all = gather_all(wall, w_gate[0], w_up[0], w_down[0], g_block)
    query_full = wall_full[:, :, 0:1024].reshape(1024, 1024)
    key_full = wall_full[:, :, 1024:1536].reshape(1024, 512)
    value_full = wall_full[:, :, 1536:2048].reshape(1024, 512)
    out_full = wall_full[:, :, 2048:3072].reshape(1024, 1024)
    small = wall_full[:, :, 3072:].reshape(1024, 256)
    router_full = small[:, :32]
    gain_first = small[:, 32].astype(F32)
    gain_second = small[:, 33].astype(F32)
    gain_query = small[:, 34].reshape(4, 256)[:, :16].reshape(64).astype(F32)
    gain_key = small[:, 35].reshape(4, 256)[:, :16].reshape(64).astype(F32)

    tokens_float = tokens.astype(F32)
    normed_one, norm_one_back = jax.vjp(rms_norm, tokens_float, gain_first)
    normed_low = normed_one.astype(BF)
    query_pre = jnp.dot(normed_low, query_full, preferred_element_type=F32)
    key_pre = jnp.dot(normed_low, key_full, preferred_element_type=F32)
    value_pre = jnp.dot(normed_low, value_full, preferred_element_type=F32)
    positions = lax.axis_index("shard") * row_count + jnp.arange(row_count, dtype=jnp.int32)
    doc_query, rope_pos = layout(lengths[0], positions)
    doc_key = layout(lengths[0], jnp.arange(length, dtype=jnp.int32))[0]
    cosine, sine_table = rope_tables(rope_pos, head_dim)

    def shape_heads(query_in, key_in, gain_q, gain_k):
        query_rot = rotate(rms_norm(query_in.reshape(row_count, heads, head_dim), gain_q), cosine, sine_table)
        key_rot = rotate(rms_norm(key_in.reshape(row_count, kv_heads, head_dim), gain_k), cosine, sine_table)
        return (query_rot.reshape(row_count, heads * head_dim), key_rot.reshape(row_count, kv_heads * head_dim))

    (query_rot, key_rot), heads_back = jax.vjp(shape_heads, query_pre, key_pre, gain_query, gain_key)
    query_low = query_rot.astype(BF)
    key_low = key_rot.astype(BF)
    value_low = value_pre.astype(BF)
    keys_all, values_all = (
        lax.all_gather(key_low, "shard", axis=0, tiled=True),
        lax.all_gather(value_low, "shard", axis=0, tiled=True),
    )
    same_doc = doc_query[:, None] == doc_key[None, :]
    live_rows = (doc_query < docs)[:, None]
    scores = masked_scores(query_low, keys_all, same_doc, kv_heads, head_dim)
    top_score = jnp.max(scores, axis=-1, keepdims=True)
    exponent_terms = jnp.exp(scores - top_score)
    denominator = jnp.sum(exponent_terms, axis=-1, keepdims=True)
    probs_low = (exponent_terms / denominator).astype(BF)
    log_total = top_score + jnp.log(denominator)
    attn_mixed = jnp.einsum(
        "kgts,skd->tkgd",
        probs_low,
        values_all.reshape(length, kv_heads, head_dim),
        preferred_element_type=F32,
    ).reshape(row_count, heads * head_dim)
    mixed_low = jnp.where(live_rows, attn_mixed, 0.0).astype(BF)
    middle = tokens_float + jnp.dot(mixed_low, out_full, preferred_element_type=F32)
    normed_two, norm_two_back = jax.vjp(rms_norm, middle, gain_second)
    routed_low = normed_two.astype(BF)

    logits = lax.dot_general(router_full, routed_low, (((0,), (1,)), ((), ())), preferred_element_type=F32)
    used = hits_t > 0
    top = jnp.max(jnp.where(used, logits, -1e30), axis=0, keepdims=True)
    terms = jnp.where(used, jnp.exp(jnp.where(used, logits - top, 0.0)), 0.0)
    gates = terms / jnp.sum(terms, axis=0, keepdims=True)

    summed, y_part, gw, uw, dw = expert_stage(routed_low, g_all, gate_full, up_full, down_full, router_full.T)

    grad_result = cotangent.astype(F32)
    grad_routed = summed[:row_count].astype(F32)
    grad_gates = summed[row_count:].astype(F32)
    grad_gates = (grad_gates[:8] + grad_gates[8:]).reshape(8, 4, row_count).transpose(1, 0, 2).reshape(experts, row_count)
    grad_logits = gates * (grad_gates - jnp.sum(gates * grad_gates, axis=0, keepdims=True))
    grad_router = lax.dot_general(
        routed_low.astype(F32), grad_logits, (((0,), (1,)), ((), ())), precision=highest, preferred_element_type=F32
    )
    grad_routed = grad_routed + lax.dot_general(
        grad_logits, router_full.astype(F32), (((0,), (1,)), ((), ())), precision=highest, preferred_element_type=F32
    )
    grad_middle_norm, grad_gain_second = norm_two_back(grad_routed)
    grad_middle = grad_result + grad_middle_norm
    grad_attn_low = grad_middle.astype(BF)
    grad_out_w = jnp.dot(mixed_low.T, grad_attn_low, preferred_element_type=F32)
    grad_mixed = jnp.dot(grad_attn_low, out_full.T, preferred_element_type=F32)
    grad_mixed_low = jnp.where(live_rows, grad_mixed.astype(BF), jnp.zeros((), BF))
    scores_again = masked_scores(query_low, keys_all, same_doc, kv_heads, head_dim)
    attn_probs = jnp.exp(scores_again - log_total)
    grad_heads = grad_mixed_low.reshape(row_count, kv_heads, group, head_dim)
    keys_grouped = keys_all.reshape(length, kv_heads, head_dim)
    values_grouped = values_all.reshape(length, kv_heads, head_dim)
    query_grouped = query_low.reshape(row_count, kv_heads, group, head_dim)
    grad_probs = jnp.einsum("tkgd,skd->kgts", grad_heads, values_grouped, preferred_element_type=F32)
    row_dot = jnp.sum(attn_probs * grad_probs, axis=-1, keepdims=True)
    grad_scores = jnp.where(same_doc[None, None], attn_probs * (grad_probs - row_dot), 0.0).astype(BF)
    grad_values = jnp.einsum("kgts,tkgd->skd", attn_probs.astype(BF), grad_heads, preferred_element_type=F32)
    grad_keys = jnp.einsum("kgts,tkgd->skd", grad_scores, query_grouped, preferred_element_type=F32) * inv_root
    grad_query = jnp.einsum("kgts,skd->tkgd", grad_scores, keys_grouped, preferred_element_type=F32) * inv_root
    own_keys, own_values = (
        lax.psum_scatter(
            grad_keys.reshape(length, kv_heads * head_dim).astype(BF), "shard", scatter_dimension=0, tiled=True
        ).astype(F32),
        lax.psum_scatter(
            grad_values.reshape(length, kv_heads * head_dim).astype(BF), "shard", scatter_dimension=0, tiled=True
        ).astype(F32),
    )
    grad_query_pre, grad_key_pre, grad_gain_query, grad_gain_key = heads_back(
        (grad_query.reshape(row_count, heads * head_dim), own_keys)
    )
    query_grad_low = grad_query_pre.astype(BF)
    key_grad_low = grad_key_pre.astype(BF)
    value_grad_low = own_values.astype(BF)
    grad_query_w = jnp.dot(normed_low.T, query_grad_low, preferred_element_type=F32)
    grad_key_w = jnp.dot(normed_low.T, key_grad_low, preferred_element_type=F32)
    grad_value_w = jnp.dot(normed_low.T, value_grad_low, preferred_element_type=F32)
    grad_normed = (
        jnp.dot(query_grad_low, query_full.T, preferred_element_type=F32)
        + jnp.dot(key_grad_low, key_full.T, preferred_element_type=F32)
        + jnp.dot(value_grad_low, value_full.T, preferred_element_type=F32)
    )
    grad_tokens_norm, grad_gain_first = norm_one_back(grad_normed)
    grad_tokens = grad_middle + grad_tokens_norm

    def spread(v):
        return jnp.pad(v.reshape(4, 16), ((0, 0), (0, row_count - 16))).reshape(1024, 1).astype(BF)

    wall_grad = jnp.concatenate(
        [
            grad_query_w.astype(BF),
            grad_key_w.astype(BF),
            grad_value_w.astype(BF),
            grad_out_w.astype(BF),
            grad_router.astype(BF),
            grad_gain_first.reshape(1024, 1).astype(BF),
            grad_gain_second.reshape(1024, 1).astype(BF),
            spread(grad_gain_query),
            spread(grad_gain_key),
            jnp.zeros((1024, 220), BF),
        ],
        axis=1,
    ).reshape(4, row_count, W_COLS)
    gate_grad, up_grad, down_grad, w_grad, y_sum = reduce_all(gw, uw, dw, wall_grad, y_part)
    result = (middle + y_sum.astype(F32)).astype(BF)
    return (
        result,
        grad_tokens,
        w_grad[:, 3104],
        w_grad[:, 0:1024],
        w_grad[:, 1024:1536],
        w_grad[:, 1536:2048],
        w_grad[:16, 3106],
        w_grad[:16, 3107],
        w_grad[:, 2048:3072],
        w_grad[:, 3105],
        w_grad[:, 3072:3104],
        gate_grad[None],
        up_grad[None],
        down_grad[None],
    )


def solution(mesh):
    rows = P(("expert", "shard"), None)
    by_shard = P("shard", None)
    columns = P("expert", None, "shard")
    placed = (
        rows,
        P("expert", None),
        rows,
        P("shard"),
        by_shard,
        by_shard,
        by_shard,
        P("shard"),
        P("shard"),
        by_shard,
        P("shard"),
        by_shard,
        columns,
        columns,
        P("expert", "shard", None),
        rows,
    )
    return jax.shard_map(
        body,
        mesh=mesh,
        in_specs=placed,
        out_specs=(
            rows,
            rows,
            P("shard"),
            by_shard,
            by_shard,
            by_shard,
            P("shard"),
            P("shard"),
            by_shard,
            P("shard"),
            by_shard,
            columns,
            columns,
            P("expert", "shard", None),
        ),
        check_vma=False,
    )
```

```python
import math

import jax
import jax.numpy as jnp
import numpy as np
from jax import lax
from jax.experimental import pallas as pl
from jax.experimental.pallas import tpu as pltpu
from jax.sharding import PartitionSpec as P

CAP = 96
EPS = 1e-06
ROPE_BASE = 10000.0
BF = jnp.bfloat16
F32 = jnp.float32
MESH = pl.DeviceIdType.MESH
ANY = pl.BlockSpec(memory_space=pl.ANY)
VMEM = pl.BlockSpec(memory_space=pltpu.VMEM)
MIB = 1 << 20
W_COLS = 3328
W_HALF = W_COLS // 2
ROWS = 256
BLOCK = 272
HALF = 128


class Place:
    def __init__(self):
        self.expert = lax.axis_index("expert")
        self.x = lax.axis_index("shard")
        self.core = self.expert % 2
        self.chip = self.expert // 2
        y, z = self.chip % 4, self.chip // 4
        self.first = z + self.core * (y - z)
        self.second = y + self.core * (z - y)
        self.first_stride = 8 - 6 * self.core
        self.second_stride = 2 + 6 * self.core

    def block(self, first, second):
        return ((self.first + first + 4) % 4) * 4 + (self.second + second + 4) % 4

    def at(self, first, second):
        near = ((self.first + first + 4) % 4) * self.first_stride
        return {"expert": near + ((self.second + second + 4) % 4) * self.second_stride + self.core}

    def along_x(self, step):
        return {"shard": (self.x + step + 4) % 4}

    def sibling(self):
        return {"expert": self.expert + 1 - 2 * self.core}


def greet(devices):
    barrier = pltpu.get_barrier_semaphore()
    for device in devices:
        pl.semaphore_signal(barrier, inc=1, device_id=device, device_id_type=MESH)
    pl.semaphore_wait(barrier, len(devices))


class Copy:
    def __init__(self, *parts):
        self.parts = parts

    def made(self):
        return pltpu.make_async_remote_copy(*self.parts, device_id_type=MESH)

    def start(self):
        self.made().start()

    def wait_send(self):
        self.made().wait_send()

    def wait_recv(self):
        self.made().wait_recv()


class Wires:
    def __init__(self, send, recv):
        self.send, self.recv = send, recv

    def copy(self, source, target, number, device):
        return Copy(source, target, self.send.at[number], self.recv.at[number], device)


class GatherRing:
    def __init__(self, wires, base, at, own, right, left, half, rows):
        low, high, full = pl.ds(0, half), pl.ds(half, rows - half), pl.ds(0, rows)
        copy = wires.copy
        self.go = [copy(own, at(0, full), base, right), copy(own, at(0, full), base + 1, left)]
        self.came = [copy(at(-1, full), at(-1, full), base, right), copy(at(1, full), at(1, full), base + 1, left)]
        self.on = [copy(at(-1, low), at(-1, low), base + 2, right), copy(at(1, high), at(1, high), base + 3, left)]
        self.far = [copy(at(2, low), at(2, low), base + 2, right), copy(at(2, high), at(2, high), base + 3, left)]

    def start(self):
        for step in self.go:
            step.start()

    def forward(self, way):
        self.came[way].wait_recv()
        self.on[way].start()

    def wait_far(self):
        for step in self.far:
            step.wait_recv()

    def wait_sent(self):
        for step in self.go + self.on:
            step.wait_send()


class ReduceRing:
    def __init__(self, wires, base, at, near, landing, right, left, half, rows):
        low, high, full = pl.ds(0, half), pl.ds(half, rows - half), pl.ds(0, rows)
        copy = wires.copy
        self.at, self.near, self.landing = at, near, landing
        self.parts = [low, high, full]
        self.far = [copy(at(2, low), near(low), base, right), copy(at(2, high), near(high), base + 1, left)]
        self.mid = [copy(at(1, full), landing(0), base + 2, right), copy(at(-1, full), landing(1), base + 3, left)]

    def start(self):
        for step in self.far:
            step.start()

    def middle(self, way):
        self.far[way].wait_recv()
        side = 1 - 2 * way
        add_into(self.at(side, self.parts[way]), self.near(self.parts[way]))
        self.mid[way].start()

    def middle_both(self):
        for way in range(2):
            self.far[way].wait_recv()
        for way in range(2):
            add_into(self.at(1 - 2 * way, self.parts[way]), self.near(self.parts[way]))
        for way in range(2):
            self.mid[way].start()

    def finish(self, target=None):
        for step in self.mid:
            step.wait_recv()
        own = self.at(0, self.parts[2])
        if target is None:
            add_into(own, self.landing(0), self.landing(1))
        else:
            add_up(target, own, self.landing(0), self.landing(1))

    def wait_sent(self):
        for step in self.far + self.mid:
            step.wait_send()


def add_up(target, *terms):
    rows, columns = target.shape
    size = min(rows, 16 * max(1, 1024 // columns))

    @pl.loop(0, rows // size)
    def _(i):
        here = pl.ds(pl.multiple_of(i * size, 16), size)
        total = terms[0][here, :].astype(F32)
        for term in terms[1:]:
            total = total + term[here, :].astype(F32)
        target[here, :] = total.astype(target.dtype)


def add_into(target, *terms):
    add_up(target, target, *terms)


def dot(a, b, contract=((1,), (0,))):
    return lax.dot_general(a, b, (contract, ((), ())), preferred_element_type=F32)


NT = ((1,), (1,))
TN = ((0,), (0,))


def call(kernel, out_shape, in_specs, out_specs, scratch, ident, vmem=56):
    return pl.pallas_call(
        kernel,
        out_shape=out_shape,
        in_specs=in_specs,
        out_specs=out_specs,
        scratch_shapes=scratch,
        compiler_params=pltpu.CompilerParams(
            collective_id=ident, has_side_effects=True, vmem_limit_bytes=vmem * MIB
        ),
    )


HEAD_PAIRS = 4
NORM_ROW, QUERY_ROW = 0, 2
ROUTER_ROW = 16
SMALL = 48


def lanes(rows=ROWS, columns=128):
    return lax.broadcasted_iota(jnp.int32, (rows, columns), 1)


def head_map(columns):
    column = lax.broadcasted_iota(jnp.int32, (columns, 128), 0) // 64
    return (column == lax.broadcasted_iota(jnp.int32, (columns, 128), 1)).astype(F32).astype(BF)


def split_dot(a, exact, contract=((1,), (0,))):
    high = a.astype(BF)
    low = (a - high.astype(F32)).astype(BF)
    return dot(high, exact, contract) + dot(low, exact, contract)


def head_scale(v, heads):
    mean = split_dot(v * v, heads) * (1.0 / 64)
    return split_dot(lax.rsqrt(mean + EPS), heads, NT)


def turn(v, cosine, sine):
    lower = lanes() % 64 < 32
    swapped = jnp.where(lower, pltpu.roll(v, 96, 1), pltpu.roll(v, 32, 1))
    return v * cosine + swapped * sine


def split_heads(block, odd):
    keep = lanes() >= 64 if odd else lanes() < 64
    rolled = pltpu.roll(block, 64, 1)
    first, second = (rolled, block) if odd else (block, rolled)
    return jnp.where(keep, first, 0.0), jnp.where(keep, second, 0.0)


def join_heads(first, second, odd):
    low = pltpu.roll(first, 64, 1) if odd else first
    high = second if odd else pltpu.roll(second, 64, 1)
    return jnp.where(lanes() < 64, low, high)


def three_parts(v):
    high = v.astype(BF).astype(F32)
    middle = (v - high).astype(BF).astype(F32)
    return high, middle, v - high - middle


def passed_documents(lengths, rows, first):
    position = (lax.broadcasted_iota(jnp.int32, (rows, 128), 0) + first).astype(F32)
    end = jnp.zeros((1, 1), F32)
    number, start = jnp.zeros((rows, 128), F32), jnp.zeros((rows, 128), F32)
    for d in range(4):
        length = lengths[:, d : d + 1]
        end = end + length
        number = number + jnp.where(position >= end, 1.0, 0.0)
        start = start + jnp.where(position >= end, length, 0.0)
    return number, position - start


def attention_kernel(
    tok,
    routes,
    lengths,
    gains,
    router,
    frequency,
    wk_in,
    wv_in,
    wq_in,
    wo_in,
    g,
    h2_out,
    middle_out,
    mixed_out,
    h1_out,
    qpre_out,
    kpre_out,
    qa_out,
    kv_out,
    wq_out,
    wk_out,
    wv_out,
    wo_out,
    small_out,
    rope_out,
    aug_out,
    places_out,
    g_all,
    small,
    small_all,
    g_own,
    total,
    h2,
    middle,
    mixed,
    h1,
    qpre,
    kpre,
    qa,
    kv,
    wq,
    wk,
    wv,
    wo,
    params_low,
    rope,
    aug,
    places,
    local,
    leave,
    w_send,
    w_recv,
    k_send,
    k_recv,
    g_send,
    g_recv,
):
    me = Place()
    x, core = me.x, me.core
    right, left, sibling = me.along_x(1), me.along_x(-1), me.sibling()
    w_wires, k_wires, g_wires = Wires(w_send, w_recv), Wires(k_send, k_recv), Wires(g_send, g_recv)

    def shard(step):
        return (x + step + 4) % 4

    leaving = []

    def store(source, target):
        step = pltpu.make_async_copy(source, target, leave.at[len(leaving)])
        leaving.append(step)
        step.start()

    load_g = pltpu.make_async_copy(g, g_own.at[pl.ds(0, ROWS)], local.at[4])
    load_g.start()
    wide = lanes(1, 1024)
    row = lax.broadcasted_iota(jnp.int32, (16, 1024), 0)
    source = lax.broadcasted_iota(jnp.int32, (128, 1024), 0)
    here = wide // ROWS == x
    column = lanes(128, 1024)
    spread = ((column % 16 == source) & ((column % 64) // 16 == x)).astype(F32).astype(BF)

    def whole(gain):
        return jnp.where(here, jnp.concatenate([gain.astype(F32)] * 4, axis=1), 0.0)

    def tiled(gain):
        return dot(jnp.broadcast_to(gain, (16, 128)), spread)[0:1]

    block = jnp.zeros((16, 1024), F32)
    parts = (whole(gains[0:1, :]), whole(gains[1:2, :]), tiled(gains[2:3, 0:128]), tiled(gains[3:4, 0:128]))
    for n, part in enumerate(parts):
        block = jnp.where(row == n, part, block)
    small[pl.ds(0, 16), :] = block.astype(BF)
    small[pl.ds(16, 32), :] = whole(router[...]).astype(BF)

    expert = lax.broadcasted_iota(jnp.int32, (32, ROWS), 0)
    hits = sum(jnp.where(routes[k : k + 1, :] == expert, 1.0, 0.0) for k in range(8))
    before = (lax.broadcasted_iota(jnp.int32, (ROWS, ROWS), 0) < lanes(ROWS, ROWS)).astype(F32).astype(BF)
    places[...] = jnp.where(hits > 0.0, dot(hits.astype(BF), before), -1.0)
    packed = jnp.concatenate([places[q * 8 : (q + 1) * 8] for q in range(4)], axis=1)
    g_own[pl.ds(ROWS, 16), :] = jnp.concatenate([packed, jnp.zeros((8, 1024), F32)], axis=0).astype(BF)
    load_g.wait()
    greet([right, left, sibling, me.at(1, 0), me.at(-1, 0), me.at(0, 1), me.at(0, -1)])
    small_ring = GatherRing(w_wires, 0, lambda k, rows: small_all.at[shard(k), rows], small, right, left, 32, SMALL)
    small_ring.start()

    class Weight:
        def __init__(self, source, target, base):
            def at(k, rows, half):
                start = pl.multiple_of(shard(k) * ROWS + half * HALF + rows.start, 64)
                return target.at[pl.ds(start, rows.size), :]

            own = source.at[pl.ds(pl.multiple_of(core * HALF, HALF), HALF), :]
            full = pl.ds(0, HALF)
            self.ring = GatherRing(w_wires, base, lambda k, rows: at(k, rows, core), own, right, left, 64, HALF)
            self.pass_on = [
                w_wires.copy(at(k, full, core), at(k, full, core), base + 4 + n, sibling) for n, k in enumerate((-1, 1, 2))
            ]
            self.passed = [
                w_wires.copy(at(k, full, 1 - core), at(k, full, 1 - core), base + 4 + n, sibling)
                for n, k in enumerate((-1, 1, 2))
            ]
            self.keep = pltpu.make_async_copy(
                source, target.at[pl.ds(pl.multiple_of(x * ROWS, ROWS), ROWS), :], local.at[base // 7]
            )

        def start(self):
            self.ring.start()

        def forward(self):
            for way in range(2):
                self.ring.forward(way)
                self.pass_on[way].start()

        def finish(self):
            self.ring.wait_far()
            self.pass_on[2].start()

        def ready(self):
            for step in self.passed:
                step.wait_recv()

        def wait_sent(self):
            self.ring.wait_sent()
            for step in self.pass_on:
                step.wait_send()

    key_weight, value_weight = Weight(wk_in, wk, 4), Weight(wv_in, wv, 11)
    query_weight, out_weight = Weight(wq_in, wq, 18), Weight(wo_in, wo, 25)
    weights = [key_weight, value_weight, query_weight, out_weight]
    key_weight.start()
    value_weight.start()
    query_weight.keep.start()
    out_weight.keep.start()

    def g_at(fo):
        return lambda k, rows: g_all.at[me.block(fo, k), rows]

    first = GatherRing(
        g_wires, 0, lambda k, rows: g_all.at[me.block(k, 0), rows], g_own, me.at(1, 0), me.at(-1, 0), HALF, BLOCK
    )
    seconds = [
        GatherRing(
            g_wires,
            4 + 4 * i,
            g_at(fo),
            g_own if fo == 0 else g_all.at[me.block(fo, 0)],
            me.at(0, 1),
            me.at(0, -1),
            HALF,
            BLOCK,
        )
        for i, fo in enumerate((-1, 1, 2, 0))
    ]
    first.start()
    seconds[3].start()
    own_copies = [
        pltpu.make_async_copy(g_own, g_all.at[me.block(0, 0)], local.at[4]),
        pltpu.make_async_copy(small, small_all.at[x], local.at[5]),
        key_weight.keep,
        value_weight.keep,
    ]
    for step in own_copies:
        step.start()

    ends = lengths[...].astype(F32)
    doc, since = passed_documents(ends, ROWS, x * ROWS)
    lane = lanes()
    aug[pl.ds(0, ROWS), :] = jnp.where(
        lane.astype(F32) == doc, 16.0, jnp.where(lane == 8, -128.0, 0.0)
    ).astype(BF)
    angles = since * frequency[...]
    rope[0] = jnp.cos(angles)
    sine_table = jnp.sin(angles)
    rope[1] = jnp.where(lane % 64 < 32, -sine_table, sine_table)
    doc = passed_documents(ends, 1024, 0)[0]
    lane = lanes(1024)
    aug[pl.ds(ROWS, 1024), :] = jnp.where(
        lane.astype(F32) == doc, 8.0, jnp.where((lane >= 5) & (lane < 9), 1.0, 0.0)
    ).astype(BF)
    store(rope, rope_out)
    store(aug, aug_out)
    store(places, places_out)
    tokens = tok[...].astype(F32)
    tokens = tokens * lax.rsqrt(jnp.mean(tokens * tokens, axis=1, keepdims=True) + EPS)

    for way in range(2):
        small_ring.forward(way)
    key_weight.forward()
    value_weight.forward()
    query_weight.start()
    first.forward(0)
    seconds[0].start()
    first.forward(1)
    seconds[1].start()
    small_ring.wait_far()
    own_copies[1].wait()
    params = sum((small_all[k].astype(F32) for k in range(1, 4)), small_all[0].astype(F32))
    params_low[...] = params.astype(BF)
    store(params_low, small_out)
    h1[...] = (tokens * params[0:1]).astype(BF)
    store(h1, h1_out)
    key_weight.finish()
    value_weight.finish()
    key_weight.ready()
    key_weight.keep.wait()
    kpre[...] = dot(h1[...], wk[...])
    value_weight.ready()
    value_weight.keep.wait()
    kv[x, :, pl.ds(512, 512)] = dot(h1[...], wv[...]).astype(BF)
    keys = kpre[...]
    keys = keys * head_scale(keys, head_map(512)) * params[3:4, 0:512]
    for j in range(4):
        block = keys[:, j * 128 : (j + 1) * 128]
        kv[x, :, pl.ds(j * 128, 128)] = turn(block, rope[0], rope[1]).astype(BF)
    kv_ring = GatherRing(k_wires, 0, lambda k, rows: kv.at[shard(k), rows], kv.at[x], right, left, HALF, ROWS)
    query_weight.forward()
    kv_ring.start()
    store(kpre, kpre_out)
    store(wk, wk_out)
    store(wv, wv_out)
    first.wait_far()
    seconds[2].start()
    query_weight.finish()
    query_weight.ready()
    query_weight.keep.wait()
    qpre[...] = dot(h1[...], wq[...])
    store(qpre, qpre_out)
    store(wq, wq_out)
    queries = qpre[...]
    queries = queries * head_scale(queries, head_map(1024)) * params[2:3]
    for j in range(8):
        block = turn(queries[:, j * 128 : (j + 1) * 128], rope[0], rope[1]) * 0.125
        for n, head in enumerate(split_heads(block, j % 2 == 1)):
            start = ((j % 2) * 2 + n) * ROWS
            qa[j // 2, pl.ds(start, ROWS), pl.ds(0, 128)] = head.astype(BF)
            qa[j // 2, pl.ds(start, ROWS), pl.ds(128, 128)] = aug[pl.ds(0, ROWS), :]

    def attend(k):
        there = shard(k)
        marks = aug[pl.ds(pl.multiple_of(there * ROWS + ROWS, ROWS), ROWS), :]

        @pl.loop(0, HEAD_PAIRS)
        def _(pair):
            start = pl.multiple_of(pair * 128, 128)
            keyed = jnp.concatenate([kv[there, :, pl.ds(start, 128)], marks], axis=1)
            valued = jnp.concatenate([kv[there, :, pl.ds(start + 512, 128)], marks], axis=1)
            p = jnp.exp(dot(qa[pair], keyed, NT)).astype(BF)
            weighted = dot(p, valued)
            if k == 0:
                total[pair] = weighted
            else:
                total[pair] += weighted

    attend(0)
    kv_ring.forward(0)
    kv_ring.forward(1)
    out_weight.start()
    seconds[3].forward(0)
    seconds[3].forward(1)
    attend(-1)
    attend(1)
    for ring in seconds[0:2]:
        ring.forward(0)
        ring.forward(1)
    kv_ring.wait_far()
    attend(2)
    store(kv, kv_out)
    out_weight.forward()
    seconds[2].forward(0)
    seconds[2].forward(1)

    live = aug[pl.ds(0, ROWS), 4:5].astype(F32) == 0.0
    lane = lanes(1024)

    @pl.loop(0, HEAD_PAIRS)
    def _(pair):
        weighted = total[pair]
        mass = weighted[:, 133:134]
        heads = weighted[:, 0:128] / mass
        parts = three_parts(-jnp.log(mass))
        marks = qa[pair, :, pl.ds(128, 128)].astype(F32)
        for n, part in enumerate(parts):
            marks = jnp.where(lane == 5 + n, part, marks)
        qa[pair, :, pl.ds(128, 128)] = marks.astype(BF)
        heads = [heads[n * ROWS : (n + 1) * ROWS] for n in range(4)]
        for odd in range(2):
            joined = join_heads(heads[2 * odd], heads[2 * odd + 1], odd == 1)
            start = pl.multiple_of(pair * 256 + odd * 128, 128)
            mixed[:, pl.ds(start, 128)] = jnp.where(live, joined, 0.0).astype(BF)

    store(qa, qa_out)
    store(mixed, mixed_out)
    out_weight.finish()
    out_weight.ready()
    out_weight.keep.wait()
    store(wo, wo_out)
    middle[...] = tok[...].astype(F32) + dot(mixed[...], wo[...])
    store(middle, middle_out)
    scale = lax.rsqrt(jnp.mean(middle[...] * middle[...], axis=1, keepdims=True) + EPS)
    h2[...] = (middle[...] * scale * params_low[1:2, :].astype(F32)).astype(BF)
    store(h2, h2_out)
    for ring in [small_ring, kv_ring, first] + weights:
        ring.wait_sent()
    own_copies[0].wait()
    for ring in seconds:
        ring.wait_far()
    for ring in seconds:
        ring.wait_sent()
    for step in leaving:
        step.wait()


def attention_forward(*arrays):
    dma = pltpu.SemaphoreType.DMA
    s, v = jax.ShapeDtypeStruct, pltpu.VMEM
    stored = (
        ((ROWS, 1024), BF),
        ((ROWS, 1024), F32),
        ((ROWS, 1024), BF),
        ((ROWS, 1024), BF),
        ((ROWS, 1024), F32),
        ((ROWS, 512), F32),
        ((HEAD_PAIRS, 1024, 256), BF),
        ((4, ROWS, 1024), BF),
        ((1024, 1024), BF),
        ((1024, 512), BF),
        ((1024, 512), BF),
        ((1024, 1024), BF),
        ((SMALL, 1024), BF),
        ((2, ROWS, 128), F32),
        ((ROWS + 1024, 128), BF),
        ((32, ROWS), F32),
    )
    return call(
        attention_kernel,
        tuple(s(*one) for one in stored) + (s((16, BLOCK, 1024), BF),),
        [VMEM] * 6 + [ANY] * 5,
        (ANY,) * 17,
        [v((SMALL, 1024), BF), v((4, SMALL, 1024), BF), v((BLOCK, 1024), BF), v((HEAD_PAIRS, 1024, 256), F32)]
        + [v(*one) for one in stored]
        + [
            dma((6,)),
            dma((16,)),
            dma((32,)),
            dma((32,)),
            dma((4,)),
            dma((4,)),
            dma((20,)),
            dma((20,)),
        ],
        0,
        vmem=56,
    )(*arrays)


ORDER = (-1, 1, 2, 0)


def nth_place(i):
    return (3 + 2 * i + (i // 2) * 3) % 4


class ColumnWeight:
    def __init__(self, me, wires, base, source, target, by_rows, offset, half, rows, local):
        def at(k, part):
            start = pl.multiple_of(((me.x + k + 4) % 4) * 128 + offset, 128)
            if by_rows:
                return target.at[me.core, pl.ds(start, 128), :].at[part]
            return target.at[me.core, part, pl.ds(start, 128)]

        self.ring = GatherRing(wires, base, at, source, me.along_x(1), me.along_x(-1), half, rows)
        self.keep = pltpu.make_async_copy(source, at(0, pl.ds(0, rows)), local)
        mine, other = target.at[me.core], target.at[1 - me.core]
        if not by_rows:
            mine, other = mine.at[:, pl.ds(offset, 512)], other.at[:, pl.ds(offset, 512)]
        self.pass_on = wires.copy(mine, mine, base + 4, me.sibling())
        self.passed = wires.copy(other, other, base + 4, me.sibling())

    def start(self):
        self.ring.start()
        self.keep.start()

    def forward(self):
        self.ring.forward(0)
        self.ring.forward(1)

    def finish(self):
        self.ring.wait_far()
        self.keep.wait()
        self.pass_on.start()

    def wait_sent(self):
        self.ring.wait_sent()
        self.pass_on.wait_send()


def expert_kernel(
    h_ref,
    g_ref,
    router,
    gate_in,
    up_in,
    down_in,
    dx_out,
    y_out,
    own_g_out,
    own_u_out,
    own_d_out,
    pair_g_out,
    pair_u_out,
    pair_d_out,
    wgu,
    wd,
    wr,
    buf,
    gbuf,
    acc_gu,
    acc_d,
    near,
    landing,
    near_f,
    landing_f,
    xb,
    gxb,
    yb,
    dxb,
    act,
    dgu,
    hot,
    hot_t,
    weight,
    dgate,
    ystage,
    a_send,
    a_recv,
    r_send,
    r_recv,
    e_send,
    e_recv,
    p_send,
    p_recv,
    local,
    g_local,
    y_local,
):
    me = Place()
    f_right, f_left, s_right, s_left = me.at(1, 0), me.at(-1, 0), me.at(0, 1), me.at(0, -1)
    a_wires, r_wires = Wires(a_send, a_recv), Wires(r_send, r_recv)
    e_wires, p_wires = Wires(e_send, e_recv), Wires(p_send, p_recv)
    own = buf.at[me.block(0, 0), pl.ds(0, ROWS)]
    fetches = [
        pltpu.make_async_copy(h_ref, own, local.at[0]),
        pltpu.make_async_copy(router.at[pl.ds(ROUTER_ROW, 32), :], wr, local.at[1]),
    ]
    for step in fetches:
        step.start()
    gate_weight = ColumnWeight(me, e_wires, 0, gate_in, wgu, False, 0, 512, 1024, local.at[2])
    up_weight = ColumnWeight(me, e_wires, 5, up_in, wgu, False, 512, 512, 1024, local.at[3])
    down_weight = ColumnWeight(me, e_wires, 10, down_in, wd, True, 0, 64, 128, local.at[4])
    weights = [gate_weight, up_weight, down_weight]
    greet([f_right, f_left, s_right, s_left, me.along_x(1), me.along_x(-1), me.sibling()])
    order = nth_place

    first = GatherRing(
        a_wires, 0, lambda k, rows: buf.at[me.block(k, 0), rows], own, f_right, f_left, HALF, ROWS
    )

    def second(i):
        fo = order(i)

        def at(k, rows):
            return buf.at[me.block(fo, k), rows]

        return GatherRing(a_wires, 4 + 4 * i, at, at(0, pl.ds(0, ROWS)), s_right, s_left, HALF, ROWS)

    def reduce_second(i):
        fo = order(i)
        return ReduceRing(
            r_wires,
            4 + 4 * i,
            lambda k, rows: buf.at[me.block(fo, k), rows],
            lambda rows: near.at[i, rows],
            lambda way: landing.at[i, way],
            s_right,
            s_left,
            HALF,
            BLOCK,
        )

    reduce_first = ReduceRing(
        r_wires,
        0,
        lambda k, rows: buf.at[me.block(k, 0), rows],
        lambda rows: near_f.at[rows],
        lambda way: landing_f.at[way],
        f_right,
        f_left,
        HALF,
        BLOCK,
    )

    def load_g(i):
        start = ((me.first + order(i)) % 4) * 4
        return pltpu.make_async_copy(g_ref.at[pl.ds(start, 4)], gbuf.at[i % 2], g_local.at[i % 2])

    def store_y(i, j):
        return pltpu.make_async_copy(ystage.at[j], y_out.at[((me.first + order(i)) % 4) * 4 + j], y_local.at[j])

    fetches[0].wait()
    first.start()
    gate_weight.start()
    up_weight.start()
    load_g(0).start()
    for acc in (acc_gu, acc_d):

        @pl.loop(0, acc.shape[1] // 32)
        def _(r):
            acc[:, pl.ds(pl.multiple_of(r * 32, 32), 32), :] = jnp.zeros((2, 32, acc.shape[2]), F32)

    first.forward(0)
    second(0).start()
    first.forward(1)
    gate_weight.forward()
    up_weight.forward()
    down_weight.start()
    fetches[1].wait()
    gate_weight.finish()
    second(0).forward(0)
    second(0).forward(1)
    second(1).start()
    down_weight.forward()
    up_weight.finish()
    first.wait_far()
    second(2).start()

    expert_row = lax.broadcasted_iota(jnp.int32, (32, 256), 0)
    slot_row = lax.broadcasted_iota(jnp.int32, (CAP, 256), 0).astype(F32)
    low_row = lax.broadcasted_iota(jnp.int32, (8, 1024), 0)
    quarter = lax.broadcasted_iota(jnp.int32, (8, 1024), 1) // 256
    my_quarter = quarter == me.chip // 4
    my_low = 2 * (me.chip % 4)

    def pick(table, e):
        return jnp.sum(jnp.where(expert_row == 2 * me.chip + e, table, 0.0), axis=0, keepdims=True)

    @pl.loop(0, 4)
    def _(i):
        base = ((me.first + order(i)) % 4) * 4
        slot = i % 2
        second(i).wait_far()

        @pl.when(i < 3)
        def _():
            load_g(i + 1).start()

        load_g(i).wait()

        @pl.loop(0, 4)
        def _(j):
            h = buf[base + j, pl.ds(0, ROWS), :]
            g = gbuf[slot, j, pl.ds(0, ROWS), :]
            packed = gbuf[slot, j, pl.ds(ROWS, 16), :].astype(F32)[0:8]
            places = jnp.concatenate([packed[:, q * 256 : (q + 1) * 256] for q in range(4)], axis=0)
            logits = dot(wr[...], h, NT)
            routed = places >= 0.0
            top = jnp.max(jnp.where(routed, logits, -1e30), axis=0, keepdims=True)
            terms = jnp.where(routed, jnp.exp(jnp.where(routed, logits - top, 0.0)), 0.0)
            gates = terms / jnp.sum(terms, axis=0, keepdims=True)
            for e in range(2):
                hit = pick(places, e) == slot_row
                rows = pl.ds(e * CAP, CAP)
                weight[j, rows, :] = jnp.sum(jnp.where(hit, pick(gates, e), 0.0), axis=1, keepdims=True)
                hot[j, rows, :] = hit.astype(F32).astype(BF)
            hot_t[j] = jnp.transpose(hot[j].astype(F32)).astype(BF)
            xb[j] = dot(hot[j], h).astype(BF)
            gx = dot(hot[j], g)
            gxb[j] = gx.astype(BF)

        @pl.when(i > 0)
        def _():
            reduce_second(i - 1).middle(0)
            reduce_second(i - 1).middle(1)


        @pl.when(i == 0)
        def _():
            second(1).forward(0)
            second(1).forward(1)
            down_weight.finish()
            second(2).forward(0)
            second(2).forward(1)
            second(3).start()
            for step in weights:
                step.passed.wait_recv()

        @pl.when(i == 1)
        def _():
            second(3).forward(0)
            second(3).forward(1)

        @pl.loop(0, 2)
        def _(e):
            rows = pl.ds(pl.multiple_of(e * CAP, 32), CAP)
            x = xb[:, rows, :].reshape(4 * CAP, 1024)
            gx = gxb[:, rows, :].reshape(4 * CAP, 1024)
            gate = weight[:, rows, :].reshape(4 * CAP, 1)
            dy = (gate * gx.astype(F32)).astype(BF)
            both = dot(x, wgu[e])
            gate_pre, up_pre = both[:, 0:512], both[:, 512:1024]
            grad_act = dot(dy, wd[e], NT)
            sig = 1.0 / (1.0 + jnp.exp(-gate_pre))
            silu = gate_pre * sig
            active = (silu * up_pre).astype(BF)
            grad_gate = (grad_act * up_pre * (sig * (1.0 + gate_pre * (1.0 - sig)))).astype(BF)
            grad_up = (grad_act * silu).astype(BF)
            act[:, rows, :] = active.reshape(4, CAP, 512)
            dgu[:, rows, pl.ds(0, 512)] = grad_gate.reshape(4, CAP, 512)
            dgu[:, rows, pl.ds(512, 512)] = grad_up.reshape(4, CAP, 512)
            out = dot(active, wd[e]).astype(BF).astype(F32)
            dgate[:, rows, :] = jnp.sum(gx.astype(F32) * out, axis=1, keepdims=True).reshape(4, CAP, 1)
            yb[:, rows, :] = (gate * out).astype(BF).reshape(4, CAP, 1024)

        second(i).wait_sent()

        @pl.when(i == 0)
        def _():
            first.on[0].wait_send()

        @pl.when(i == 1)
        def _():
            first.on[1].wait_send()

        @pl.when(i == 3)
        def _():
            for step in first.go:
                step.wait_send()

        @pl.loop(0, 2)
        def _(e):
            rows = pl.ds(pl.multiple_of(e * CAP, 32), CAP)
            grad_in = dot(dgu[:, rows, :].reshape(4 * CAP, 1024), wgu[e], NT)
            dxb[:, rows, :] = grad_in.astype(BF).reshape(4, CAP, 1024)

        @pl.loop(0, 4)
        def _(j):
            buf[base + j, pl.ds(0, ROWS), :] = dot(hot_t[j], dxb[j]).astype(BF)
            spots = hot[j].astype(F32) * dgate[j]
            grad_rows = [jnp.sum(spots[e * CAP : (e + 1) * CAP], axis=0, keepdims=True) for e in range(2)]
            wide = [jnp.concatenate([row] * 4, axis=1) for row in grad_rows]
            mine = jnp.where(low_row == my_low, wide[0], jnp.where(low_row == my_low + 1, wide[1], 0.0))
            mine = jnp.where(my_quarter, mine, 0.0)
            high = mine.astype(BF).astype(F32)
            buf[base + j, pl.ds(ROWS, 16), :] = jnp.concatenate([high, mine - high], axis=0).astype(BF)

        reduce_second(i).start()

        @pl.when(i > 0)
        def _():
            reduce_second(i - 1).finish()

        @pl.when(i == 3)
        def _():
            reduce_first.start()

        @pl.loop(0, 4)
        def _(j):
            @pl.when(i > 0)
            def _():
                store_y(i - 1, j).wait()

            ystage[j] = dot(hot_t[j], yb[j]).astype(BF)
            store_y(i, j).start()


        @pl.when(i == 3)
        def _():
            reduce_second(3).middle(0)
            reduce_second(3).middle(1)

        @pl.loop(0, 2)
        def _(e):
            rows = pl.ds(pl.multiple_of(e * CAP, 32), CAP)
            x = xb[:, rows, :].reshape(4 * CAP, 1024)
            gate = weight[:, rows, :].reshape(4 * CAP, 1)
            dy = (gate * gxb[:, rows, :].reshape(4 * CAP, 1024).astype(F32)).astype(BF)
            grad_pre = dgu[:, rows, :].reshape(4 * CAP, 1024)
            active = act[:, rows, :].reshape(4 * CAP, 512)
            acc_gu[e] += dot(x, grad_pre, TN)
            acc_d[e] += dot(active, dy, TN)


    reduce_first.middle(0)
    reduce_first.middle(1)
    for j in range(4):
        store_y(3, j).wait()

    leaving = [None] * 4
    number = 0
    for acc, offset, width, own_out, pair_out in (
        (acc_d, 0, 1024, own_d_out, pair_d_out),
        (acc_gu, 0, 512, own_g_out, pair_g_out),
        (acc_gu, 512, 512, own_u_out, pair_u_out),
    ):
        for n in range(acc.shape[1] // 256):
            rows = pl.ds(n * 256, 256)
            for stays in (False, True):
                slot = (2 * number + stays) % 4
                if leaving[slot] is not None:
                    leaving[slot]()
                stage = ystage.at[slot, :, pl.ds(0, width)]
                stage[...] = acc[me.core if stays else 1 - me.core, rows, pl.ds(offset, width)].astype(BF)
                if stays:
                    step = pltpu.make_async_copy(stage, own_out.at[rows, :], y_local.at[slot])
                    leaving[slot] = step.wait
                else:
                    step = p_wires.copy(stage, pair_out.at[rows, :], number, me.sibling())
                    leaving[slot] = step.wait_send
                step.start()
            number += 1
    reduce_second(3).finish()
    mine = me.block(0, 0)
    for step in reduce_first.mid:
        step.wait_recv()
    add_into(buf.at[mine], landing_f.at[0], landing_f.at[1])
    result = pltpu.make_async_copy(buf.at[mine], dx_out, local.at[0])
    result.start()
    for step in leaving:
        step()
    number = 0
    for pair_out in (pair_d_out, pair_g_out, pair_u_out):
        for n in range(pair_out.shape[0] // 256):
            here = pair_out.at[pl.ds(n * 256, 256), :]
            p_wires.copy(here, here, number, me.sibling()).wait_recv()
            number += 1
    for step in range(4):
        reduce_second(step).wait_sent()
    reduce_first.wait_sent()
    for step in weights:
        step.wait_sent()
    result.wait()


def expert_stage(*arrays):
    dma = pltpu.SemaphoreType.DMA
    s, v = jax.ShapeDtypeStruct, pltpu.VMEM
    return call(
        expert_kernel,
        (
            s((BLOCK, 1024), BF),
            s((16, ROWS, 1024), BF),
            s((1024, 512), BF),
            s((1024, 512), BF),
            s((512, 1024), BF),
            s((1024, 512), BF),
            s((1024, 512), BF),
            s((512, 1024), BF),
        ),
        [ANY] * 6,
        (ANY,) * 8,
        [
            v((2, 1024, 1024), BF),
            v((2, 512, 1024), BF),
            v((32, 1024), BF),
            v((16, BLOCK, 1024), BF),
            v((2, 4, BLOCK, 1024), BF),
            v((2, 1024, 1024), F32),
            v((2, 512, 1024), F32),
            v((4, BLOCK, 1024), BF),
            v((4, 2, BLOCK, 1024), BF),
            v((BLOCK, 1024), BF),
            v((2, BLOCK, 1024), BF),
            v((4, 2 * CAP, 1024), BF),
            v((4, 2 * CAP, 1024), BF),
            v((4, 2 * CAP, 1024), BF),
            v((4, 2 * CAP, 1024), BF),
            v((4, 2 * CAP, 512), BF),
            v((4, 2 * CAP, 1024), BF),
            v((4, 2 * CAP, 256), BF),
            v((4, 256, 2 * CAP), BF),
            v((4, 2 * CAP, 1), F32),
            v((4, 2 * CAP, 1), F32),
            v((4, ROWS, 1024), BF),
            dma((20,)),
            dma((20,)),
            dma((20,)),
            dma((20,)),
            dma((15,)),
            dma((15,)),
            dma((10,)),
            dma((10,)),
            dma((5,)),
            dma((2,)),
            dma((4,)),
        ],
        1,
        vmem=62,
    )(*arrays)


Y_ORDER = (2, 1, -1, 0)


class Sum:
    def __init__(self, me, wires, base, own, pair, part_f, part_s, part_x, total):
        self.me, self.own, self.pair = me, own, pair
        self.parts = (part_f, part_s, part_x)
        sibling = me.sibling()

        def half_of(core):
            return pl.ds(pl.multiple_of(core * HALF, HALF), HALF)

        def cols_of(k):
            return pl.ds(pl.multiple_of(((me.first + k + 4) % 4) * 256, 256), 256)

        def rows_of(k):
            return pl.ds(pl.multiple_of(me.core * HALF + ((me.second + k + 4) % 4) * 32, 32), 32)

        def shard(k):
            return (me.x + k + 4) % 4

        kept = half_of(me.core)
        steps = (1, 2, 3)
        self.shards = [shard(k) for k in range(4)]
        self.kept, self.cols, self.rows = kept, cols_of(0), rows_of(0)
        self.swap = wires.copy(own.at[:, half_of(1 - me.core), :], pair, base, sibling)
        self.out_f = [wires.copy(own.at[:, kept, cols_of(k)], part_f.at[k - 1], base + k, me.at(k, 0)) for k in steps]
        self.out_s = [
            wires.copy(own.at[:, rows_of(k), cols_of(0)], part_s.at[k - 1], base + 3 + k, me.at(0, k)) for k in steps
        ]
        self.out_x = [
            wires.copy(own.at[shard(k), rows_of(0), cols_of(0)], part_x.at[k - 1], base + 6 + k, me.along_x(k))
            for k in steps
        ]

        def back(rows, cols, number, device):
            here = total.at[rows, cols]
            return wires.copy(here, here, number, device)

        self.result = total.at[rows_of(0), cols_of(0)]
        self.back_s = [back(rows_of(0), cols_of(0), base + 9 + k, me.at(0, k)) for k in steps]
        self.came_s = [back(rows_of(-k), cols_of(0), base + 9 + k, me.at(0, k)) for k in steps]
        self.back_f = [back(kept, cols_of(0), base + 12 + k, me.at(k, 0)) for k in steps]
        self.came_f = [back(kept, cols_of(-k), base + 12 + k, me.at(k, 0)) for k in steps]
        here, there = total.at[kept], total.at[half_of(1 - me.core)]
        self.last = wires.copy(here, here, base + 16, sibling)
        self.last_came = wires.copy(there, there, base + 16, sibling)

    def step(self, number):
        own, (part_f, part_s, part_x) = self.own, self.parts
        if number == 0:
            self.swap.start()
        elif number == 1:
            self.swap.wait_recv()
            for k in range(4):
                add_into(own.at[k, self.kept], self.pair.at[k])
            for copy in self.out_f:
                copy.start()
        elif number == 2:
            for copy in self.out_f:
                copy.wait_recv()
            for k in range(4):
                add_into(own.at[k, self.kept, self.cols], *[part_f.at[n, k] for n in range(3)])
            for copy in self.out_s:
                copy.start()
        elif number == 3:
            for copy in self.out_s:
                copy.wait_recv()
            for k in range(4):
                add_into(own.at[k, self.rows, self.cols], *[part_s.at[n, k] for n in range(3)])
            for copy in self.out_x:
                copy.start()
        elif number == 4:
            for copy in self.out_x:
                copy.wait_recv()
            add_up(self.result, own.at[self.me.x, self.rows, self.cols], *[part_x.at[n] for n in range(3)])
            for copy in self.back_s:
                copy.start()
        elif number == 5:
            for copy in self.came_s:
                copy.wait_recv()
            for copy in self.back_f:
                copy.start()
        elif number == 6:
            for copy in self.came_f:
                copy.wait_recv()
            self.last.start()
        else:
            self.last_came.wait_recv()

    def wait_sent(self):
        for copy in [self.swap, self.last] + self.out_f + self.out_s + self.out_x + self.back_s + self.back_f:
            copy.wait_send()


LOADED = {
    "summed": ((BLOCK, 1024), BF),
    "h2": ((ROWS, 1024), BF),
    "middle": ((ROWS, 1024), F32),
    "cot": ((ROWS, 1024), BF),
    "tok": ((ROWS, 1024), BF),
    "mixed": ((ROWS, 1024), BF),
    "h1": ((ROWS, 1024), BF),
    "qpre": ((ROWS, 1024), F32),
    "kpre": ((ROWS, 512), F32),
    "qa": ((HEAD_PAIRS, 1024, 256), BF),
    "kv": ((4, ROWS, 1024), BF),
    "wk": ((1024, 512), BF),
    "wv": ((1024, 512), BF),
    "small": ((SMALL, 1024), BF),
    "rope": ((2, ROWS, 128), F32),
    "aug": ((ROWS + 1024, 128), BF),
    "places": ((32, ROWS), F32),
}


def backward_kernel(*refs):
    sources, refs = dict(zip(LOADED, refs)), refs[len(LOADED) :]
    wq, wo, gw, uw, dw, gp, up, dp, y, layer_out, tokens_out, total_out, small_out, g_out, u_out, d_out = refs[:16]
    refs = refs[16:]
    held, refs = dict(zip(LOADED, refs)), refs[len(LOADED) :]
    (
        doa,
        dqa,
        dkv,
        wbuf,
        parts,
        pair_w,
        part_f,
        part_s,
        part_x,
        total_w,
        near_k,
        land_k,
        own_g,
        own_u,
        own_d,
        pair_g,
        pair_u,
        pair_d,
        near_g,
        near_u,
        near_d,
        land_g,
        land_u,
        land_d,
        buf,
        y_sum,
        near_s,
        land_s,
        near_f,
        land_f,
        small_part,
        small_pair,
        small_x,
        small_f,
        small_s,
        layer,
        grad_middle,
        small_total,
        final_g,
        final_u,
        final_d,
        e_send,
        e_recv,
        w_send,
        w_recv,
        k_send,
        k_recv,
        y_send,
        y_recv,
        t_send,
        t_recv,
        local,
        fetched,
        leave,
    ) = refs
    summed, h2, middle, cot, tok, mixed, h1, qpre, kpre, qa, kv, wk, wv, small, rope, aug, places = held.values()
    me = Place()
    x, core = me.x, me.core
    right, left, sibling = me.along_x(1), me.along_x(-1), me.sibling()
    planes = [me.at(1, 0), me.at(-1, 0), me.at(2, 0), me.at(0, 1), me.at(0, -1), me.at(0, 2)]
    e_wires, w_wires, k_wires = Wires(e_send, e_recv), Wires(w_send, w_recv), Wires(k_send, k_recv)
    y_wires, t_wires = Wires(y_send, y_recv), Wires(t_send, t_recv)

    def shard(step):
        return (x + step + 4) % 4

    loads = {
        name: pltpu.make_async_copy(sources[name], held[name], fetched.at[n]) for n, name in enumerate(LOADED)
    }
    pulls = [
        pltpu.make_async_copy(source, target, local.at[n])
        for n, (source, target) in enumerate(
            ((gw, own_g), (uw, own_u), (dw, own_d), (gp, pair_g), (up, pair_u), (dp, pair_d), (wo, wbuf))
        )
    ]
    load_wq = pltpu.make_async_copy(wq, wbuf, local.at[7])

    def load_y(i):
        start = ((me.first + Y_ORDER[i] + 4) % 4) * 4
        return pltpu.make_async_copy(y.at[pl.ds(start, 4)], buf.at[i % 2], local.at[8 + i % 2])

    def ready(*names):
        for name in names:
            loads[name].wait()

    leaving = []

    def store(source, target):
        step = pltpu.make_async_copy(source, target, leave.at[len(leaving)])
        leaving.append(step)
        step.start()

    for step in pulls[:6]:
        step.start()
    load_y(0).start()
    for name in ("summed", "h2", "small", "places", "middle", "cot", "mixed"):
        loads[name].start()
    pulls[6].start()
    load_y(1).start()
    for name in ("aug", "qa", "kv", "rope", "qpre", "kpre", "h1", "wk", "wv", "tok"):
        loads[name].start()
    greet([right, left, me.along_x(2), sibling] + planes)

    def y_second(i):
        return ReduceRing(
            y_wires,
            4 + 4 * i,
            lambda k, rows: buf.at[i % 2, (me.second + k + 4) % 4, rows],
            lambda rows: near_s.at[i % 2, rows],
            lambda way: land_s.at[i % 2, way],
            me.at(0, 1),
            me.at(0, -1),
            HALF,
            ROWS,
        )

    y_first = ReduceRing(
        y_wires,
        0,
        lambda k, rows: y_sum.at[(me.first + k + 4) % 4, rows],
        lambda rows: near_f.at[rows],
        lambda way: land_f.at[way],
        me.at(1, 0),
        me.at(-1, 0),
        HALF,
        ROWS,
    )
    y_rings = [y_second(i) for i in range(4)]

    def y_start(i):
        load_y(i).wait()
        y_rings[i].start()

    def y_finish(i):
        y_rings[i].finish(y_sum.at[(me.first + Y_ORDER[i] + 4) % 4])
        y_rings[i].wait_sent()
        if i < 2:
            load_y(i + 2).start()

    def weight_sum(n, own):
        return Sum(
            me,
            w_wires,
            17 * n,
            own,
            pair_w.at[n % 2],
            part_f.at[n],
            part_s.at[n],
            part_x.at[n],
            total_w.at[n],
        )

    out_sum, query_sum, kv_sum = weight_sum(0, parts.at[0]), weight_sum(1, parts.at[1]), weight_sum(2, dkv)

    def weight_grad(target, left_rows, right_rows):
        for k in range(4):
            target[k] = dot(left_rows[:, k * ROWS : (k + 1) * ROWS], right_rows, TN).astype(BF)

    def slice_of(k):
        return pl.ds(pl.multiple_of(shard(k) * 128, 128), 128)

    def g_at(k, ref=None):
        return (own_g if ref is None else ref).at[:, slice_of(k)]

    def u_at(k, ref=None):
        return (own_u if ref is None else ref).at[:, slice_of(k)]

    def d_at(k, start=0, size=128, ref=None):
        return (own_d if ref is None else ref).at[pl.ds(pl.multiple_of(shard(k) * 128 + start, 64), size), :]

    e_far = [
        e_wires.copy(g_at(2), near_g, 3, right),
        e_wires.copy(d_at(2, 0, 64), near_d.at[0], 4, right),
        e_wires.copy(u_at(2), near_u, 5, left),
        e_wires.copy(d_at(2, 64, 64), near_d.at[1], 6, left),
    ]
    e_mid = [
        e_wires.copy(ref, land.at[way], 7 + way * 3 + i, device)
        for way, (k, device) in enumerate(((1, right), (-1, left)))
        for i, (ref, land) in enumerate(((g_at(k), land_g), (u_at(k), land_u), (d_at(k), land_d)))
    ]

    def add_pair(k):
        add_into(g_at(k), g_at(k, pair_g))
        add_into(u_at(k), u_at(k, pair_u))
        add_into(d_at(k), d_at(k, ref=pair_d))

    for step in pulls[:6]:
        step.wait()
    add_pair(2)
    for step in e_far:
        step.start()
    y_start(0)
    y_start(1)

    ready("summed", "h2", "small", "places")
    params = small[...].astype(F32)
    h2_rows = h2[...]
    numbers = summed[pl.ds(ROWS, 16), :].astype(F32)
    numbers = numbers[0:8] + numbers[8:16]
    grad_gates = jnp.concatenate([numbers[:, q * 256 : (q + 1) * 256] for q in range(4)], axis=0)
    logits = dot(small[pl.ds(ROUTER_ROW, 32), :], h2_rows, NT)
    routed = places[...] >= 0.0
    top = jnp.max(jnp.where(routed, logits, -1e30), axis=0, keepdims=True)
    terms = jnp.where(routed, jnp.exp(jnp.where(routed, logits - top, 0.0)), 0.0)
    gates = terms / jnp.sum(terms, axis=0, keepdims=True)
    grad_logits = gates * (grad_gates - jnp.sum(gates * grad_gates, axis=0, keepdims=True))
    grad_router = split_dot(grad_logits, h2_rows)
    for k in range(4):
        small_part[k, pl.ds(0, 32), :] = grad_router[:, k * ROWS : (k + 1) * ROWS]
        small_part[k, pl.ds(32, 16), :] = jnp.zeros((16, ROWS), F32)
    grad = summed[pl.ds(0, ROWS), :].astype(F32) + split_dot(grad_logits, small[pl.ds(ROUTER_ROW, 32), :], TN)

    def norm_back(v, gain, grad, row):
        scale = lax.rsqrt(jnp.mean(v * v, axis=1, keepdims=True) + EPS)
        normed = v * scale
        gained = gain * grad
        gain_grad = jnp.sum(grad * normed, axis=0, keepdims=True)
        for k in range(4):
            small_part[k, row : row + 1, :] = gain_grad[:, k * ROWS : (k + 1) * ROWS]
        return scale * (gained - normed * jnp.mean(gained * normed, axis=1, keepdims=True))

    ready("middle", "cot", "mixed")
    grad_middle[...] = cot[...].astype(F32) + norm_back(middle[...], params[1:2], grad, 33)
    grad_low = grad_middle[...].astype(BF)
    grad_low = grad_middle[...].astype(BF)
    ready("aug")
    live = aug[pl.ds(0, ROWS), 4:5].astype(F32) == 0.0
    pulls[6].wait()
    grad_mixed = jnp.where(live, dot(grad_low, wbuf[...], NT), 0.0).astype(BF).astype(F32)
    row_dots = split_dot(grad_mixed * mixed[...].astype(F32), head_map(1024))
    lane = lanes()
    for j in range(8):
        for n, head in enumerate(split_heads(grad_mixed[:, j * 128 : (j + 1) * 128], j % 2 == 1)):
            start = ((j % 2) * 2 + n) * ROWS
            marks = jnp.zeros((ROWS, 128), F32)
            for m, part in enumerate(three_parts(-row_dots[:, 2 * j + n : 2 * j + n + 1])):
                marks = jnp.where(lane == 5 + m, part, marks)
            doa[j // 2, pl.ds(start, ROWS), pl.ds(0, 128)] = head.astype(BF)
            doa[j // 2, pl.ds(start, ROWS), pl.ds(128, 128)] = marks.astype(BF)

    load_wq.start()
    ready("qa", "kv")

    def attend(k):
        there = shard(k)
        marks = aug[pl.ds(pl.multiple_of(there * ROWS + ROWS, ROWS), ROWS), :]

        @pl.loop(0, HEAD_PAIRS)
        def _(pair):
            start = pl.multiple_of(pair * 128, 128)
            keys = kv[there, :, pl.ds(start, 128)]
            keyed = jnp.concatenate([keys, marks], axis=1)
            valued = jnp.concatenate([kv[there, :, pl.ds(start + 512, 128)], marks], axis=1)
            p = jnp.exp(dot(qa[pair], keyed, NT))
            ds = (p * dot(doa[pair], valued, NT)).astype(BF)
            dkv[there, :, pl.ds(start + 512, 128)] = dot(p.astype(BF), doa[pair, :, pl.ds(0, 128)], TN).astype(BF)
            dkv[there, :, pl.ds(start, 128)] = dot(ds, qa[pair, :, pl.ds(0, 128)], TN).astype(BF)
            dq = dot(ds, keys)
            if k == 2:
                dqa[pair] = dq
            else:
                dqa[pair] += dq

    kv_ring = ReduceRing(
        k_wires,
        0,
        lambda k, rows: dkv.at[shard(k), rows],
        lambda rows: near_k.at[rows],
        lambda way: land_k.at[way],
        right,
        left,
        HALF,
        ROWS,
    )
    attend(2)
    kv_ring.start()
    y_rings[0].middle_both()
    y_rings[1].middle_both()
    weight_grad(parts.at[0], mixed[...], grad_low)
    out_sum.step(0)
    for k in (1, -1, 0):
        add_pair(k)
    attend(1)
    kv_ring.middle(0)
    out_sum.step(1)
    y_finish(0)
    y_finish(1)
    attend(-1)
    kv_ring.middle(1)
    y_first.start()
    y_start(2)
    y_start(3)
    e_far[0].wait_recv()
    add_into(g_at(1), near_g)
    e_far[1].wait_recv()
    add_into(d_at(1, 0, 64), near_d.at[0])
    e_far[2].wait_recv()
    add_into(u_at(-1), near_u)
    e_far[3].wait_recv()
    add_into(d_at(-1, 64, 64), near_d.at[1])
    for step in e_mid:
        step.start()
    attend(0)
    out_sum.step(2)
    y_rings[2].middle_both()
    y_rings[3].middle_both()

    def heads_back(pre, grads, gain, count):
        heads = head_map(count)
        scale = head_scale(pre, heads)
        normed = pre * scale
        gained = gain * grads
        mean = split_dot(split_dot(gained * normed, heads) * (1.0 / 64), heads, NT)
        gain_grad = jnp.sum(grads * normed, axis=0, keepdims=True)
        folded = sum(gain_grad[:, j * 128 : (j + 1) * 128] for j in range(count // 128))
        return scale * (gained - normed * mean), folded

    ready("rope", "qpre", "h1")
    blocks = []
    for j in range(8):
        pair, odd = j // 2, j % 2 == 1
        heads = [dqa[pair, pl.ds(((j % 2) * 2 + n) * ROWS, ROWS), :] for n in range(2)]
        blocks.append(turn(join_heads(heads[0], heads[1], odd) * 0.125, rope[0], -rope[1]))
    query_grad, query_gain_grad = heads_back(qpre[...], jnp.concatenate(blocks, axis=1), params[2:3], 1024)
    query_low = query_grad.astype(BF)
    weight_grad(parts.at[1], h1[...], query_low)
    query_sum.step(0)
    load_wq.wait()
    grad_h1 = dot(query_low, wbuf[...], NT)

    ready("kpre")
    kv_ring.finish()
    own_kv = dkv[x].astype(F32)
    blocks = [turn(own_kv[:, j * 128 : (j + 1) * 128], rope[0], -rope[1]) for j in range(4)]
    key_grad, key_gain_grad = heads_back(kpre[...], jnp.concatenate(blocks, axis=1), params[3:4, 0:512], 512)
    low = jnp.concatenate([key_grad.astype(BF), own_kv[:, 512:1024].astype(BF)], axis=1)
    kv_ring.wait_sent()
    weight_grad(dkv, h1[...], low)
    query_sum.step(1)
    kv_sum.step(0)
    ready("wk", "wv", "tok")
    grad_h1 = grad_h1 + dot(low[:, 0:512], wk[...], NT) + dot(low[:, 512:1024], wv[...], NT)
    grad_middle[...] += norm_back(tok[...].astype(F32), params[0:1], grad_h1, 32)
    store(grad_middle, tokens_out)
    for k in range(4):
        small_part[k, 34:35, pl.ds(0, 128)] = query_gain_grad
        small_part[k, 35:36, pl.ds(0, 128)] = key_gain_grad

    t_pair = t_wires.copy(small_part, small_pair, 0, sibling)
    t_pair.start()
    kv_sum.step(1)
    out_sum.step(3)
    y_finish(2)
    y_finish(3)
    y_first.middle_both()
    query_sum.step(2)
    t_pair.wait_recv()
    t_x = [t_wires.copy(small_part.at[shard(k)], small_x.at[k - 1], k, me.along_x(k)) for k in (1, 2, 3)]
    t_pair.wait_send()
    for k in range(4):
        small_part[k] += small_pair[k]
    for step in t_x:
        step.start()
    kv_sum.step(2)
    query_sum.step(3)
    kv_sum.step(3)
    out_sum.step(4)
    for step in t_x:
        step.wait_recv()
    small_f[0] = small_part[x] + small_x[0] + small_x[1] + small_x[2]
    t_f = [t_wires.copy(small_f.at[0], small_f.at[k], 3 + k, me.at(k, 0)) for k in (1, 2, 3)]
    for step in t_f:
        step.start()
    query_sum.step(4)
    kv_sum.step(4)
    out_sum.step(5)
    for step in t_f:
        step.wait_recv()
    small_s[0] = small_f[0] + small_f[1] + small_f[2] + small_f[3]
    t_s = [t_wires.copy(small_s.at[0], small_s.at[k], 6 + k, me.at(0, k)) for k in (1, 2, 3)]
    for step in t_s:
        step.start()
    query_sum.step(5)
    kv_sum.step(5)
    out_sum.step(6)
    for step in e_mid:
        step.wait_recv()
    for out, at, land, target in (
        (final_g, g_at, land_g, g_out),
        (final_u, u_at, land_u, u_out),
        (final_d, d_at, land_d, d_out),
    ):
        add_up(out, at(0), land.at[0], land.at[1])
        store(out, target)
    query_sum.step(6)
    kv_sum.step(6)
    for step in t_s:
        step.wait_recv()
    small_total[...] = small_s[0] + small_s[1] + small_s[2] + small_s[3]
    store(small_total, small_out)
    out_sum.step(7)
    store(total_w.at[0], total_out.at[0])
    y_first.finish()
    layer[...] = (middle[...] + y_sum[me.first].astype(F32)).astype(BF)
    store(layer, layer_out)
    query_sum.step(7)
    store(total_w.at[1], total_out.at[1])
    kv_sum.step(7)
    store(total_w.at[2], total_out.at[2])
    for step in e_far + e_mid + t_x + t_f + t_s:
        step.wait_send()
    for ring in [y_first, out_sum, query_sum, kv_sum]:
        ring.wait_sent()
    for step in leaving:
        step.wait()


def backward_stage(*arrays):
    dma = pltpu.SemaphoreType.DMA
    s, v = jax.ShapeDtypeStruct, pltpu.VMEM
    return call(
        backward_kernel,
        (
            s((ROWS, 1024), BF),
            s((ROWS, 1024), F32),
            s((3, ROWS, 1024), BF),
            s((SMALL, ROWS), F32),
            s((1024, 128), F32),
            s((1024, 128), F32),
            s((128, 1024), F32),
        ),
        [ANY] * (len(LOADED) + 9),
        (ANY,) * 7,
        [v(*one) for one in LOADED.values()]
        + [
            v((HEAD_PAIRS, 1024, 256), BF),
            v((HEAD_PAIRS, 1024, 128), F32),
            v((4, ROWS, 1024), BF),
            v((1024, 1024), BF),
            v((2, 4, ROWS, 1024), BF),
            v((2, 4, HALF, 1024), BF),
            v((3, 3, 4, HALF, 256), BF),
            v((3, 3, 4, 32, 256), BF),
            v((3, 3, 32, 256), BF),
            v((3, ROWS, 1024), BF),
            v((ROWS, 1024), BF),
            v((2, ROWS, 1024), BF),
            v((1024, 512), BF),
            v((1024, 512), BF),
            v((512, 1024), BF),
            v((1024, 512), BF),
            v((1024, 512), BF),
            v((512, 1024), BF),
            v((1024, 128), BF),
            v((1024, 128), BF),
            v((2, 64, 1024), BF),
            v((2, 1024, 128), BF),
            v((2, 1024, 128), BF),
            v((2, 128, 1024), BF),
            v((2, 4, ROWS, 1024), BF),
            v((4, ROWS, 1024), BF),
            v((2, ROWS, 1024), BF),
            v((2, 2, ROWS, 1024), BF),
            v((ROWS, 1024), BF),
            v((2, ROWS, 1024), BF),
            v((4, SMALL, ROWS), F32),
            v((4, SMALL, ROWS), F32),
            v((3, SMALL, ROWS), F32),
            v((4, SMALL, ROWS), F32),
            v((4, SMALL, ROWS), F32),
            v((ROWS, 1024), BF),
            v((ROWS, 1024), F32),
            v((SMALL, ROWS), F32),
            v((1024, 128), F32),
            v((1024, 128), F32),
            v((128, 1024), F32),
            dma((13,)),
            dma((13,)),
            dma((51,)),
            dma((51,)),
            dma((4,)),
            dma((4,)),
            dma((20,)),
            dma((20,)),
            dma((10,)),
            dma((10,)),
            dma((10,)),
            dma((len(LOADED),)),
            dma((9,)),
        ],
        2,
        vmem=63,
    )(*arrays)


def last_kernel(layer, tokens, totals, small, g, u, d, *rest):
    outs, (layer_v, tokens_v, totals_v, small_v, g_v, u_v, d_v), held, sem = rest[:13], rest[13:20], rest[20:24], rest[24]
    sources = (totals, small, tokens, layer, g, u, d)
    inside = (totals_v, small_v, tokens_v, layer_v, g_v, u_v, d_v)
    loads = [pltpu.make_async_copy(source, inner, sem.at[n]) for n, (source, inner) in enumerate(zip(sources, inside))]
    for step in loads:
        step.start()
    layer_out, tokens_out, g_out, u_out, d_out, wq, wk, wv, wo, first, second, heads, router = outs
    wq_v, wk_v, wv_v, wo_v = held
    stores = []

    def store(source, target):
        step = pltpu.make_async_copy(source, target, sem.at[7 + len(stores)])
        stores.append(step)
        step.start()

    loads[0].wait()
    wq_v[...] = totals_v[1].astype(F32)
    store(wq_v, wq)
    wo_v[...] = totals_v[0].astype(F32)
    store(wo_v, wo)
    wk_v[...] = totals_v[2, :, pl.ds(0, 512)].astype(F32)
    store(wk_v, wk)
    wv_v[...] = totals_v[2, :, pl.ds(512, 512)].astype(F32)
    store(wv_v, wv)
    loads[1].wait()
    first[...] = small_v[32:33, :]
    second[...] = small_v[33:34, :]
    both = small_v[34:36, 0:128]
    heads[...] = both + pltpu.roll(both, 64, 1)
    router[...] = small_v[0:32, :]
    for step, inner, target in zip(loads[2:], inside[2:], (tokens_out, layer_out, g_out, u_out, d_out)):
        step.wait()
        store(inner, target)
    for step in stores:
        step.wait()


def last_stage(*arrays):
    s, v = jax.ShapeDtypeStruct, pltpu.VMEM
    return pl.pallas_call(
        last_kernel,
        out_shape=(
            s((ROWS, 1024), BF),
            s((ROWS, 1024), F32),
            s((1024, 128), F32),
            s((1024, 128), F32),
            s((128, 1024), F32),
            s((ROWS, 1024), F32),
            s((ROWS, 512), F32),
            s((ROWS, 512), F32),
            s((ROWS, 1024), F32),
            s((1, ROWS), F32),
            s((1, ROWS), F32),
            s((2, 128), F32),
            s((32, ROWS), F32),
        ),
        in_specs=[ANY] * 7,
        out_specs=(ANY,) * 9 + (VMEM,) * 4,
        scratch_shapes=[
            v((ROWS, 1024), BF),
            v((ROWS, 1024), F32),
            v((3, ROWS, 1024), BF),
            v((SMALL, ROWS), F32),
            v((1024, 128), F32),
            v((1024, 128), F32),
            v((128, 1024), F32),
            v((ROWS, 1024), F32),
            v((ROWS, 512), F32),
            v((ROWS, 512), F32),
            v((ROWS, 1024), F32),
            pltpu.SemaphoreType.DMA((16,)),
        ],
        compiler_params=pltpu.CompilerParams(vmem_limit_bytes=62 * MIB),
    )(*arrays)


def body(
    tokens,
    lengths,
    routes,
    norm1_gain,
    w_query,
    w_key,
    w_value,
    query_gain,
    key_gain,
    w_out,
    norm2_gain,
    w_router,
    w_gate,
    w_up,
    w_down,
    cotangent,
):
    x = lax.axis_index("shard")
    frequency = (ROPE_BASE ** -((np.arange(128) % 32) / 32.0)).astype(np.float32)[None]
    gains = jnp.concatenate(
        [norm1_gain, norm2_gain, jnp.pad(query_gain, (0, ROWS - 16)), jnp.pad(key_gain, (0, ROWS - 16))]
    ).reshape(4, ROWS)
    (h2, middle, mixed, h1, qpre, kpre, qa, kv, wq, wk, wv, wo, small, rope, aug, places, g_all) = attention_forward(
        tokens,
        routes.T,
        lengths,
        gains,
        w_router.T,
        jnp.asarray(frequency),
        w_key,
        w_value,
        w_query,
        w_out,
        cotangent,
    )
    summed, y_part, *expert_grads = expert_stage(
        h2, g_all, small, w_gate[0], w_up[0], w_down[0]
    )
    results = backward_stage(
        summed,
        h2,
        middle,
        cotangent,
        tokens,
        mixed,
        h1,
        qpre,
        kpre,
        qa,
        kv,
        wk,
        wv,
        small,
        rope,
        aug,
        places,
        wq,
        wo,
        *expert_grads,
        y_part,
    )
    layer, tokens_grad, gate_grad, up_grad, down_grad, wq_g, wk_g, wv_g, wo_g, first, second, heads, router = last_stage(
        *results
    )
    heads = lax.dynamic_slice(heads, (0, x * 16), (2, 16))
    return (
        layer,
        tokens_grad,
        first[0],
        wq_g,
        wk_g,
        wv_g,
        heads[0],
        heads[1],
        wo_g,
        second[0],
        router.T,
        gate_grad[None],
        up_grad[None],
        down_grad[None],
    )


def solution(mesh):
    rows = P(("expert", "shard"), None)
    by_shard = P("shard", None)
    columns = P("expert", None, "shard")
    placed = (
        rows,
        P("expert", None),
        rows,
        P("shard"),
        by_shard,
        by_shard,
        by_shard,
        P("shard"),
        P("shard"),
        by_shard,
        P("shard"),
        by_shard,
        columns,
        columns,
        P("expert", "shard", None),
        rows,
    )
    return jax.shard_map(
        body,
        mesh=mesh,
        in_specs=placed,
        out_specs=(
            rows,
            rows,
            P("shard"),
            by_shard,
            by_shard,
            by_shard,
            P("shard"),
            P("shard"),
            by_shard,
            P("shard"),
            by_shard,
            columns,
            columns,
            P("expert", "shard", None),
        ),
        check_vma=False,
    )
```

```python
import math

import jax
import jax.numpy as jnp
import numpy as np
from jax import lax
from jax.experimental import pallas as pl
from jax.experimental.pallas import tpu as pltpu
from jax.sharding import PartitionSpec as P

CAP = 96
EPS = 1e-06
ROPE_BASE = 10000.0
BF = jnp.bfloat16
F32 = jnp.float32
MESH = pl.DeviceIdType.MESH
ANY = pl.BlockSpec(memory_space=pl.ANY)
VMEM = pl.BlockSpec(memory_space=pltpu.VMEM)
MIB = 1 << 20
W_COLS = 3328
W_HALF = W_COLS // 2
ROWS = 256
BLOCK = 272
HALF = 128


class Place:
    def __init__(self):
        self.expert = lax.axis_index("expert")
        self.x = lax.axis_index("shard")
        self.core = self.expert % 2
        self.chip = self.expert // 2
        y, z = self.chip % 4, self.chip // 4
        self.first = z + self.core * (y - z)
        self.second = y + self.core * (z - y)
        self.first_stride = 8 - 6 * self.core
        self.second_stride = 2 + 6 * self.core

    def block(self, first, second):
        return ((self.first + first + 4) % 4) * 4 + (self.second + second + 4) % 4

    def at(self, first, second):
        near = ((self.first + first + 4) % 4) * self.first_stride
        return {"expert": near + ((self.second + second + 4) % 4) * self.second_stride + self.core}

    def other_at(self, first, second):
        there = self.at(first, second)["expert"]
        return {"expert": there + 1 - 2 * self.core}

    def along_x(self, step):
        return {"shard": (self.x + step + 4) % 4}

    def sibling(self):
        return {"expert": self.expert + 1 - 2 * self.core}


def greet(devices):
    barrier = pltpu.get_barrier_semaphore()
    for device in devices:
        pl.semaphore_signal(barrier, inc=1, device_id=device, device_id_type=MESH)
    pl.semaphore_wait(barrier, len(devices))


class Copy:
    def __init__(self, *parts):
        self.parts = parts

    def made(self):
        return pltpu.make_async_remote_copy(*self.parts, device_id_type=MESH)

    def start(self):
        self.made().start()

    def wait_send(self):
        self.made().wait_send()

    def wait_recv(self):
        self.made().wait_recv()


class Wires:
    def __init__(self, send, recv):
        self.send, self.recv = send, recv

    def copy(self, source, target, number, device):
        return Copy(source, target, self.send.at[number], self.recv.at[number], device)


class GatherRing:
    def __init__(self, wires, base, at, own, right, left, half, rows):
        low, high, full = pl.ds(0, half), pl.ds(half, rows - half), pl.ds(0, rows)
        copy = wires.copy
        self.go = [copy(own, at(0, full), base, right), copy(own, at(0, full), base + 1, left)]
        self.came = [copy(at(-1, full), at(-1, full), base, right), copy(at(1, full), at(1, full), base + 1, left)]
        self.on = [copy(at(-1, low), at(-1, low), base + 2, right), copy(at(1, high), at(1, high), base + 3, left)]
        self.far = [copy(at(2, low), at(2, low), base + 2, right), copy(at(2, high), at(2, high), base + 3, left)]

    def start(self):
        for step in self.go:
            step.start()

    def forward(self, way):
        self.came[way].wait_recv()
        self.on[way].start()

    def wait_far(self):
        for step in self.far:
            step.wait_recv()

    def wait_sent(self):
        for step in self.go + self.on:
            step.wait_send()


class ReduceRing:
    def __init__(self, wires, base, at, near, landing, right, left, half, rows):
        low, high, full = pl.ds(0, half), pl.ds(half, rows - half), pl.ds(0, rows)
        copy = wires.copy
        self.at, self.near, self.landing = at, near, landing
        self.parts = [low, high, full]
        self.far = [copy(at(2, low), near(low), base, right), copy(at(2, high), near(high), base + 1, left)]
        self.mid = [copy(at(1, full), landing(0), base + 2, right), copy(at(-1, full), landing(1), base + 3, left)]

    def start(self):
        for step in self.far:
            step.start()

    def middle(self, way):
        self.far[way].wait_recv()
        side = 1 - 2 * way
        add_into(self.at(side, self.parts[way]), self.near(self.parts[way]))
        self.mid[way].start()

    def middle_both(self):
        for way in range(2):
            self.far[way].wait_recv()
        for way in range(2):
            add_into(self.at(1 - 2 * way, self.parts[way]), self.near(self.parts[way]))
        for way in range(2):
            self.mid[way].start()

    def finish(self, target=None):
        for step in self.mid:
            step.wait_recv()
        own = self.at(0, self.parts[2])
        if target is None:
            add_into(own, self.landing(0), self.landing(1))
        else:
            add_up(target, own, self.landing(0), self.landing(1))

    def wait_sent(self):
        for step in self.far + self.mid:
            step.wait_send()


def add_up(target, *terms):
    if len(target.shape) == 3:
        for k in range(target.shape[0]):
            add_up(target.at[k], *[term.at[k] for term in terms])
        return
    rows, columns = target.shape
    size = min(rows, 16 * max(1, 1024 // columns))

    @pl.loop(0, rows // size)
    def _(i):
        here = pl.ds(pl.multiple_of(i * size, 16), size)
        total = terms[0][here, :].astype(F32)
        for term in terms[1:]:
            total = total + term[here, :].astype(F32)
        target[here, :] = total.astype(target.dtype)


def add_into(target, *terms):
    add_up(target, target, *terms)


def dot(a, b, contract=((1,), (0,))):
    return lax.dot_general(a, b, (contract, ((), ())), preferred_element_type=F32)


NT = ((1,), (1,))
TN = ((0,), (0,))


def call(kernel, out_shape, in_specs, out_specs, scratch, ident, vmem=56):
    return pl.pallas_call(
        kernel,
        out_shape=out_shape,
        in_specs=in_specs,
        out_specs=out_specs,
        scratch_shapes=scratch,
        compiler_params=pltpu.CompilerParams(
            collective_id=ident, has_side_effects=True, vmem_limit_bytes=vmem * MIB
        ),
    )


HEAD_PAIRS = 4
NORM_ROW, QUERY_ROW = 0, 2
ROUTER_ROW = 16
SMALL = 48


def lanes(rows=ROWS, columns=128):
    return lax.broadcasted_iota(jnp.int32, (rows, columns), 1)


def head_map(columns):
    column = lax.broadcasted_iota(jnp.int32, (columns, 128), 0) // 64
    return (column == lax.broadcasted_iota(jnp.int32, (columns, 128), 1)).astype(F32).astype(BF)


def split_dot(a, exact, contract=((1,), (0,))):
    high = a.astype(BF)
    low = (a - high.astype(F32)).astype(BF)
    return dot(high, exact, contract) + dot(low, exact, contract)


def head_scale(v, heads):
    mean = split_dot(v * v, heads) * (1.0 / 64)
    return split_dot(lax.rsqrt(mean + EPS), heads, NT)


def turn(v, cosine, sine):
    lower = lanes() % 64 < 32
    swapped = jnp.where(lower, pltpu.roll(v, 96, 1), pltpu.roll(v, 32, 1))
    return v * cosine + swapped * sine


def split_heads(block, odd):
    keep = lanes() >= 64 if odd else lanes() < 64
    rolled = pltpu.roll(block, 64, 1)
    first, second = (rolled, block) if odd else (block, rolled)
    return jnp.where(keep, first, 0.0), jnp.where(keep, second, 0.0)


def join_heads(first, second, odd):
    low = pltpu.roll(first, 64, 1) if odd else first
    high = second if odd else pltpu.roll(second, 64, 1)
    return jnp.where(lanes() < 64, low, high)


def three_parts(v):
    high = v.astype(BF).astype(F32)
    middle = (v - high).astype(BF).astype(F32)
    return high, middle, v - high - middle


def passed_documents(lengths, rows, first):
    position = (lax.broadcasted_iota(jnp.int32, (rows, 128), 0) + first).astype(F32)
    end = jnp.zeros((1, 1), F32)
    number, start = jnp.zeros((rows, 128), F32), jnp.zeros((rows, 128), F32)
    for d in range(4):
        length = lengths[:, d : d + 1]
        end = end + length
        number = number + jnp.where(position >= end, 1.0, 0.0)
        start = start + jnp.where(position >= end, length, 0.0)
    return number, position - start


def attention_kernel(
    tok,
    routes,
    lengths,
    gains,
    router,
    frequency,
    wk_in,
    wv_in,
    wq_in,
    wo_in,
    g,
    h2_out,
    middle_out,
    mixed_out,
    h1_out,
    qpre_out,
    kpre_out,
    qa_out,
    kv_out,
    wq_out,
    wk_out,
    wv_out,
    wo_out,
    small_out,
    rope_out,
    aug_out,
    places_out,
    g_all,
    small,
    small_all,
    g_own,
    total,
    h2,
    middle,
    mixed,
    h1,
    qpre,
    kpre,
    qa,
    kv,
    wq,
    wk,
    wv,
    wo,
    params_low,
    rope,
    aug,
    places,
    local,
    leave,
    w_send,
    w_recv,
    k_send,
    k_recv,
    g_send,
    g_recv,
):
    me = Place()
    x, core = me.x, me.core
    right, left, sibling = me.along_x(1), me.along_x(-1), me.sibling()
    w_wires, k_wires, g_wires = Wires(w_send, w_recv), Wires(k_send, k_recv), Wires(g_send, g_recv)

    def shard(step):
        return (x + step + 4) % 4

    leaving = []

    def store(source, target):
        step = pltpu.make_async_copy(source, target, leave.at[len(leaving)])
        leaving.append(step)
        step.start()

    load_g = pltpu.make_async_copy(g, g_own.at[pl.ds(0, ROWS)], local.at[4])
    load_g.start()
    row = lax.broadcasted_iota(jnp.int32, (16, ROWS), 0)
    source = lax.broadcasted_iota(jnp.int32, (128, ROWS), 0)
    column = lanes(128, ROWS)
    spread = ((column % 16 == source) & ((column % 64) // 16 == x)).astype(F32).astype(BF)

    def tiled(gain):
        return dot(jnp.broadcast_to(gain, (16, 128)), spread)[0:1]

    block = jnp.zeros((16, ROWS), F32)
    parts = (gains[0:1, :].astype(F32), gains[1:2, :].astype(F32), tiled(gains[2:3, 0:128]), tiled(gains[3:4, 0:128]))
    for n, part in enumerate(parts):
        block = jnp.where(row == n, part, block)
    small[pl.ds(0, 16), :] = block.astype(BF)
    small[pl.ds(16, 32), :] = router[...]

    expert = lax.broadcasted_iota(jnp.int32, (32, ROWS), 0)
    hits = sum(jnp.where(routes[k : k + 1, :] == expert, 1.0, 0.0) for k in range(8))
    before = (lax.broadcasted_iota(jnp.int32, (ROWS, ROWS), 0) < lanes(ROWS, ROWS)).astype(F32).astype(BF)
    places[...] = jnp.where(hits > 0.0, dot(hits.astype(BF), before), -1.0)
    packed = jnp.concatenate([places[q * 8 : (q + 1) * 8] for q in range(4)], axis=1)
    g_own[pl.ds(ROWS, 16), :] = jnp.concatenate([packed, jnp.zeros((8, 1024), F32)], axis=0).astype(BF)
    load_g.wait()
    greet([right, left, sibling, me.at(1, 0), me.at(-1, 0), me.at(0, 1), me.at(0, -1)])
    small_ring = GatherRing(w_wires, 0, lambda k, rows: small_all.at[shard(k), rows], small, right, left, 32, SMALL)
    small_ring.start()

    class Weight:
        def __init__(self, source, target, base):
            def at(k, rows, half):
                start = pl.multiple_of(shard(k) * ROWS + half * HALF + rows.start, 64)
                return target.at[pl.ds(start, rows.size), :]

            own = source.at[pl.ds(pl.multiple_of(core * HALF, HALF), HALF), :]
            full = pl.ds(0, HALF)
            self.ring = GatherRing(w_wires, base, lambda k, rows: at(k, rows, core), own, right, left, 64, HALF)
            self.pass_on = [
                w_wires.copy(at(k, full, core), at(k, full, core), base + 4 + n, sibling) for n, k in enumerate((-1, 1, 2))
            ]
            self.passed = [
                w_wires.copy(at(k, full, 1 - core), at(k, full, 1 - core), base + 4 + n, sibling)
                for n, k in enumerate((-1, 1, 2))
            ]
            self.keep = pltpu.make_async_copy(
                source, target.at[pl.ds(pl.multiple_of(x * ROWS, ROWS), ROWS), :], local.at[base // 7]
            )

        def start(self):
            self.ring.start()

        def forward(self):
            for way in range(2):
                self.ring.forward(way)
                self.pass_on[way].start()

        def finish(self):
            self.ring.wait_far()
            self.pass_on[2].start()

        def ready(self):
            for step in self.passed:
                step.wait_recv()

        def wait_sent(self):
            self.ring.wait_sent()
            for step in self.pass_on:
                step.wait_send()

    key_weight, value_weight = Weight(wk_in, wk, 4), Weight(wv_in, wv, 11)
    query_weight, out_weight = Weight(wq_in, wq, 18), Weight(wo_in, wo, 25)
    weights = [key_weight, value_weight, query_weight, out_weight]
    key_weight.start()
    value_weight.start()
    query_weight.keep.start()
    out_weight.keep.start()

    def g_at(fo):
        return lambda k, rows: g_all.at[me.block(fo, k), rows]

    first = GatherRing(
        g_wires, 0, lambda k, rows: g_all.at[me.block(k, 0), rows], g_own, me.at(1, 0), me.at(-1, 0), HALF, BLOCK
    )
    seconds = [
        GatherRing(
            g_wires,
            4 + 4 * i,
            g_at(fo),
            g_own if fo == 0 else g_all.at[me.block(fo, 0)],
            me.at(0, 1),
            me.at(0, -1),
            HALF,
            BLOCK,
        )
        for i, fo in enumerate((-1, 1, 2, 0))
    ]
    first.start()
    own_copies = [
        pltpu.make_async_copy(g_own, g_all.at[me.block(0, 0)], local.at[4]),
        pltpu.make_async_copy(small, small_all.at[x], local.at[5]),
        key_weight.keep,
        value_weight.keep,
    ]
    for step in own_copies:
        step.start()

    ends = lengths[...].astype(F32)
    doc, since = passed_documents(ends, ROWS, x * ROWS)
    lane = lanes()
    aug[pl.ds(0, ROWS), :] = jnp.where(
        lane.astype(F32) == doc, 16.0, jnp.where(lane == 8, -128.0, 0.0)
    ).astype(BF)
    angles = since * frequency[...]
    rope[0] = jnp.cos(angles)
    sine_table = jnp.sin(angles)
    rope[1] = jnp.where(lane % 64 < 32, -sine_table, sine_table)
    doc = passed_documents(ends, 1024, 0)[0]
    lane = lanes(1024)
    aug[pl.ds(ROWS, 1024), :] = jnp.where(
        lane.astype(F32) == doc, 8.0, jnp.where((lane >= 5) & (lane < 9), 1.0, 0.0)
    ).astype(BF)
    store(rope, rope_out)
    store(aug, aug_out)
    store(places, places_out)
    tokens = tok[...].astype(F32)
    tokens = tokens * lax.rsqrt(jnp.mean(tokens * tokens, axis=1, keepdims=True) + EPS)

    for way in range(2):
        small_ring.forward(way)
    key_weight.forward()
    value_weight.forward()
    query_weight.start()
    first.forward(0)
    first.forward(1)
    seconds[3].start()
    seconds[0].start()
    seconds[1].start()
    small_ring.wait_far()
    own_copies[1].wait()
    shares = [small_all[k].astype(F32) for k in range(4)]
    params = jnp.concatenate(shares, axis=1)
    by_head = jnp.concatenate([shares[0] + shares[1] + shares[2] + shares[3]] * 4, axis=1)
    row = lax.broadcasted_iota(jnp.int32, (SMALL, 1024), 0)
    params = jnp.where((row == 2) | (row == 3), by_head, params)
    params_low[...] = params.astype(BF)
    store(params_low, small_out)
    h1[...] = (tokens * params[0:1]).astype(BF)
    store(h1, h1_out)
    key_weight.finish()
    value_weight.finish()
    key_weight.ready()
    key_weight.keep.wait()
    kpre[...] = dot(h1[...], wk[...])
    value_weight.ready()
    value_weight.keep.wait()
    kv[x, :, pl.ds(512, 512)] = dot(h1[...], wv[...]).astype(BF)
    keys = kpre[...]
    keys = keys * head_scale(keys, head_map(512)) * params[3:4, 0:512]
    for j in range(4):
        block = keys[:, j * 128 : (j + 1) * 128]
        kv[x, :, pl.ds(j * 128, 128)] = turn(block, rope[0], rope[1]).astype(BF)
    kv_ring = GatherRing(k_wires, 0, lambda k, rows: kv.at[shard(k), rows], kv.at[x], right, left, HALF, ROWS)
    query_weight.forward()
    kv_ring.start()
    store(kpre, kpre_out)
    store(wk, wk_out)
    store(wv, wv_out)
    first.wait_far()
    seconds[2].start()
    query_weight.finish()
    query_weight.ready()
    query_weight.keep.wait()
    qpre[...] = dot(h1[...], wq[...])
    store(qpre, qpre_out)
    store(wq, wq_out)
    queries = qpre[...]
    queries = queries * head_scale(queries, head_map(1024)) * params[2:3]
    for j in range(8):
        block = turn(queries[:, j * 128 : (j + 1) * 128], rope[0], rope[1]) * 0.125
        for n, head in enumerate(split_heads(block, j % 2 == 1)):
            start = ((j % 2) * 2 + n) * ROWS
            qa[j // 2, pl.ds(start, ROWS), pl.ds(0, 128)] = head.astype(BF)
            qa[j // 2, pl.ds(start, ROWS), pl.ds(128, 128)] = aug[pl.ds(0, ROWS), :]

    def attend(k):
        there = shard(k)
        marks = aug[pl.ds(pl.multiple_of(there * ROWS + ROWS, ROWS), ROWS), :]

        @pl.loop(0, HEAD_PAIRS)
        def _(pair):
            start = pl.multiple_of(pair * 128, 128)
            keyed = jnp.concatenate([kv[there, :, pl.ds(start, 128)], marks], axis=1)
            valued = jnp.concatenate([kv[there, :, pl.ds(start + 512, 128)], marks], axis=1)
            p = jnp.exp(dot(qa[pair], keyed, NT)).astype(BF)
            weighted = dot(p, valued)
            if k == 0:
                total[pair] = weighted
            else:
                total[pair] += weighted

    attend(0)
    kv_ring.forward(0)
    kv_ring.forward(1)
    out_weight.start()
    seconds[3].forward(0)
    seconds[3].forward(1)
    attend(-1)
    attend(1)
    for ring in seconds[0:2]:
        ring.forward(0)
        ring.forward(1)
    kv_ring.wait_far()
    attend(2)
    store(kv, kv_out)
    out_weight.forward()
    seconds[2].forward(0)
    seconds[2].forward(1)

    live = aug[pl.ds(0, ROWS), 4:5].astype(F32) == 0.0
    lane = lanes(1024)

    @pl.loop(0, HEAD_PAIRS)
    def _(pair):
        weighted = total[pair]
        mass = weighted[:, 133:134]
        heads = weighted[:, 0:128] / mass
        parts = three_parts(-jnp.log(mass))
        marks = qa[pair, :, pl.ds(128, 128)].astype(F32)
        for n, part in enumerate(parts):
            marks = jnp.where(lane == 5 + n, part, marks)
        qa[pair, :, pl.ds(128, 128)] = marks.astype(BF)
        heads = [heads[n * ROWS : (n + 1) * ROWS] for n in range(4)]
        for odd in range(2):
            joined = join_heads(heads[2 * odd], heads[2 * odd + 1], odd == 1)
            start = pl.multiple_of(pair * 256 + odd * 128, 128)
            mixed[:, pl.ds(start, 128)] = jnp.where(live, joined, 0.0).astype(BF)

    store(qa, qa_out)
    store(mixed, mixed_out)
    out_weight.finish()
    out_weight.ready()
    out_weight.keep.wait()
    store(wo, wo_out)
    middle[...] = tok[...].astype(F32) + dot(mixed[...], wo[...])
    store(middle, middle_out)
    scale = lax.rsqrt(jnp.mean(middle[...] * middle[...], axis=1, keepdims=True) + EPS)
    h2[...] = (middle[...] * scale * params_low[1:2, :].astype(F32)).astype(BF)
    store(h2, h2_out)
    for ring in [small_ring, kv_ring, first] + weights:
        ring.wait_sent()
    own_copies[0].wait()
    for ring in seconds:
        ring.wait_far()
    for ring in seconds:
        ring.wait_sent()
    for step in leaving:
        step.wait()


def attention_forward(*arrays):
    dma = pltpu.SemaphoreType.DMA
    s, v = jax.ShapeDtypeStruct, pltpu.VMEM
    stored = (
        ((ROWS, 1024), BF),
        ((ROWS, 1024), F32),
        ((ROWS, 1024), BF),
        ((ROWS, 1024), BF),
        ((ROWS, 1024), F32),
        ((ROWS, 512), F32),
        ((HEAD_PAIRS, 1024, 256), BF),
        ((4, ROWS, 1024), BF),
        ((1024, 1024), BF),
        ((1024, 512), BF),
        ((1024, 512), BF),
        ((1024, 1024), BF),
        ((SMALL, 1024), BF),
        ((2, ROWS, 128), F32),
        ((ROWS + 1024, 128), BF),
        ((32, ROWS), F32),
    )
    return call(
        attention_kernel,
        tuple(s(*one) for one in stored) + (s((16, BLOCK, 1024), BF),),
        [VMEM] * 6 + [ANY] * 5,
        (ANY,) * 17,
        [v((SMALL, ROWS), BF), v((4, SMALL, ROWS), BF), v((BLOCK, 1024), BF), v((HEAD_PAIRS, 1024, 256), F32)]
        + [v(*one) for one in stored]
        + [
            dma((6,)),
            dma((16,)),
            dma((32,)),
            dma((32,)),
            dma((4,)),
            dma((4,)),
            dma((20,)),
            dma((20,)),
        ],
        0,
        vmem=56,
    )(*arrays)


ORDER = (-1, 2, 1, 0)


def nth_place(i):
    return 3 - i


class ColumnWeight:
    def __init__(self, me, wires, base, source, target, offset, half, rows, local):
        def at(k, part):
            return target.at[me.core, (me.x + k + 4) % 4 + offset, part]

        self.ring = GatherRing(wires, base, at, source, me.along_x(1), me.along_x(-1), half, rows)
        self.keep = pltpu.make_async_copy(source, at(0, pl.ds(0, rows)), local)
        mine, other = target.at[me.core, pl.ds(offset, 4)], target.at[1 - me.core, pl.ds(offset, 4)]
        self.pass_on = wires.copy(mine, mine, base + 4, me.sibling())
        self.passed = wires.copy(other, other, base + 4, me.sibling())

    def start(self):
        self.ring.start()
        self.keep.start()

    def forward(self):
        self.ring.forward(0)
        self.ring.forward(1)

    def finish(self):
        self.ring.wait_far()
        self.keep.wait()
        self.pass_on.start()

    def wait_sent(self):
        self.ring.wait_sent()
        self.pass_on.wait_send()


def expert_kernel(
    h_ref,
    g_ref,
    router,
    gate_in,
    up_in,
    down_in,
    dx_out,
    y_out,
    y_near,
    own_g_out,
    own_u_out,
    own_d_out,
    pair_g_out,
    pair_u_out,
    pair_d_out,
    wgu,
    wd,
    wr,
    buf,
    gbuf,
    near,
    landing,
    near_f,
    landing_f,
    xb,
    gxb,
    yb,
    dxb,
    act,
    dgu,
    hot,
    hot_t,
    weight,
    dgate,
    ystage,
    a_send,
    a_recv,
    r_send,
    r_recv,
    e_send,
    e_recv,
    p_send,
    p_recv,
    y_send,
    y_recv,
    local,
    g_local,
    y_local,
):
    me = Place()
    f_right, f_left, s_right, s_left = me.at(1, 0), me.at(-1, 0), me.at(0, 1), me.at(0, -1)
    a_wires, r_wires = Wires(a_send, a_recv), Wires(r_send, r_recv)
    e_wires, p_wires, y_wires = Wires(e_send, e_recv), Wires(p_send, p_recv), Wires(y_send, y_recv)
    own = buf.at[me.block(0, 0), pl.ds(0, ROWS)]
    fetches = [
        pltpu.make_async_copy(h_ref, own, local.at[0]),
        pltpu.make_async_copy(router.at[pl.ds(ROUTER_ROW, 32), :], wr, local.at[1]),
    ]
    for step in fetches:
        step.start()
    gate_weight = ColumnWeight(me, e_wires, 0, gate_in, wgu, 0, 512, 1024, local.at[2])
    up_weight = ColumnWeight(me, e_wires, 5, up_in, wgu, 4, 512, 1024, local.at[3])
    down_weight = ColumnWeight(me, e_wires, 10, down_in, wd, 0, 64, 128, local.at[4])
    weights = [gate_weight, up_weight, down_weight]
    greet([f_right, f_left, s_right, s_left, me.along_x(1), me.along_x(-1), me.sibling()])
    order = nth_place

    first = GatherRing(
        a_wires, 0, lambda k, rows: buf.at[me.block(k, 0), rows], own, f_right, f_left, HALF, ROWS
    )

    def second(i):
        fo = order(i)

        def at(k, rows):
            return buf.at[me.block(fo, k), rows]

        return GatherRing(a_wires, 4 + 4 * i, at, at(0, pl.ds(0, ROWS)), s_right, s_left, HALF, ROWS)

    def reduce_second(i):
        fo = order(i)
        return ReduceRing(
            r_wires,
            4 + 4 * i,
            lambda k, rows: buf.at[me.block(fo, k), rows],
            lambda rows: near.at[i, rows],
            lambda way: landing.at[i, way],
            s_right,
            s_left,
            HALF,
            BLOCK,
        )

    reduce_first = ReduceRing(
        r_wires,
        0,
        lambda k, rows: buf.at[me.block(k, 0), rows],
        lambda rows: near_f.at[rows],
        lambda way: landing_f.at[way],
        f_right,
        f_left,
        HALF,
        BLOCK,
    )

    def load_g(i):
        start = ((me.first + order(i)) % 4) * 4
        return pltpu.make_async_copy(g_ref.at[pl.ds(start, 4)], gbuf.at[i % 2], g_local.at[i % 2])

    def store_y(i, j):
        return pltpu.make_async_copy(ystage.at[j], y_out.at[((me.first + order(i)) % 4) * 4 + j], y_local.at[j])

    def far_y(i):
        block = ystage.at[(me.second + 2) % 4]
        low, high = pl.ds(0, HALF), pl.ds(HALF, HALF)
        return [
            y_wires.copy(block.at[low], y_near.at[i, low], 2 * i, s_right),
            y_wires.copy(block.at[high], y_near.at[i, high], 2 * i + 1, s_left),
        ]

    fetches[0].wait()
    first.start()
    gate_weight.start()
    up_weight.start()
    load_g(0).start()
    first.forward(0)
    second(0).start()
    first.forward(1)
    gate_weight.forward()
    up_weight.forward()
    down_weight.start()
    fetches[1].wait()
    gate_weight.finish()
    second(0).forward(0)
    second(0).forward(1)
    first.wait_far()
    second(1).start()
    down_weight.forward()
    up_weight.finish()
    second(2).start()

    expert_row = lax.broadcasted_iota(jnp.int32, (32, 256), 0)
    slot_row = lax.broadcasted_iota(jnp.int32, (CAP, 256), 0).astype(F32)
    low_row = lax.broadcasted_iota(jnp.int32, (8, 1024), 0)
    quarter = lax.broadcasted_iota(jnp.int32, (8, 1024), 1) // 256
    my_quarter = quarter == me.chip // 4
    my_low = 2 * (me.chip % 4)

    def pick(table, e):
        return jnp.sum(jnp.where(expert_row == 2 * me.chip + e, table, 0.0), axis=0, keepdims=True)

    @pl.loop(0, 4)
    def _(i):
        base = ((me.first + order(i)) % 4) * 4
        slot = i % 2
        second(i).wait_far()

        @pl.when(i < 3)
        def _():
            load_g(i + 1).start()

        load_g(i).wait()

        @pl.loop(0, 4)
        def _(j):
            h = buf[base + j, pl.ds(0, ROWS), :]
            g = gbuf[slot, j, pl.ds(0, ROWS), :]
            packed = gbuf[slot, j, pl.ds(ROWS, 16), :].astype(F32)[0:8]
            places = jnp.concatenate([packed[:, q * 256 : (q + 1) * 256] for q in range(4)], axis=0)
            logits = dot(wr[...], h, NT)
            routed = places >= 0.0
            top = jnp.max(jnp.where(routed, logits, -1e30), axis=0, keepdims=True)
            terms = jnp.where(routed, jnp.exp(jnp.where(routed, logits - top, 0.0)), 0.0)
            gates = terms / jnp.sum(terms, axis=0, keepdims=True)
            for e in range(2):
                hit = pick(places, e) == slot_row
                rows = pl.ds(e * CAP, CAP)
                weight[j, rows, :] = jnp.sum(jnp.where(hit, pick(gates, e), 0.0), axis=1, keepdims=True)
                hot[j, rows, :] = hit.astype(F32).astype(BF)
            hot_t[j] = jnp.transpose(hot[j].astype(F32)).astype(BF)
            xb[i, j] = dot(hot[j], h).astype(BF)
            gxb[i, j] = dot(hot[j], g).astype(BF)


        @pl.when(i > 1)
        def _():
            reduce_second(i - 2).finish()

        @pl.when(i == 3)
        def _():
            reduce_first.start()


        @pl.when(i == 0)
        def _():
            second(1).forward(0)
            second(1).forward(1)
            down_weight.finish()
            second(2).forward(0)
            second(2).forward(1)
            second(3).start()
            for step in weights:
                step.passed.wait_recv()

        @pl.when(i == 1)
        def _():
            second(3).forward(0)
            second(3).forward(1)

        @pl.loop(0, 2)
        def _(e):
            rows = pl.ds(pl.multiple_of(e * CAP, 32), CAP)
            x = xb[i, :, rows, :].reshape(4 * CAP, 1024)
            gx = gxb[i, :, rows, :].reshape(4 * CAP, 1024)
            gate = weight[:, rows, :].reshape(4 * CAP, 1)
            dy = (gate * gx.astype(F32)).astype(BF)
            gxb[i, :, rows, :] = dy.reshape(4, CAP, 1024)
            gate_up = jnp.concatenate([wgu[e, n] for n in range(8)], axis=1)
            down = wd[e].reshape(512, 1024)
            both = dot(x, gate_up)
            gate_pre, up_pre = both[:, 0:512], both[:, 512:1024]
            grad_act = dot(dy, down, NT)
            sig = 1.0 / (1.0 + jnp.exp(-gate_pre))
            silu = gate_pre * sig
            active = (silu * up_pre).astype(BF)
            grad_gate = (grad_act * up_pre * (sig * (1.0 + gate_pre * (1.0 - sig)))).astype(BF)
            grad_up = (grad_act * silu).astype(BF)
            act[i, :, rows, :] = active.reshape(4, CAP, 512)
            dgu[i, :, rows, pl.ds(0, 512)] = grad_gate.reshape(4, CAP, 512)
            dgu[i, :, rows, pl.ds(512, 512)] = grad_up.reshape(4, CAP, 512)
            out = dot(active, down).astype(BF).astype(F32)
            dgate[:, rows, :] = jnp.sum(gx.astype(F32) * out, axis=1, keepdims=True).reshape(4, CAP, 1)
            yb[:, rows, :] = (gate * out).astype(BF).reshape(4, CAP, 1024)


        @pl.when(i > 0)
        def _():
            reduce_second(i - 1).middle(0)
            reduce_second(i - 1).middle(1)

        second(i).wait_sent()

        @pl.when(i == 0)
        def _():
            first.on[0].wait_send()

        @pl.when(i == 2)
        def _():
            first.on[1].wait_send()

        @pl.when(i == 3)
        def _():
            for step in first.go:
                step.wait_send()

        @pl.loop(0, 2)
        def _(e):
            rows = pl.ds(pl.multiple_of(e * CAP, 32), CAP)
            gate_up = jnp.concatenate([wgu[e, n] for n in range(8)], axis=1)
            grad_in = dot(dgu[i, :, rows, :].reshape(4 * CAP, 1024), gate_up, NT)
            dxb[:, rows, :] = grad_in.astype(BF).reshape(4, CAP, 1024)

        @pl.loop(0, 4)
        def _(j):
            buf[base + j, pl.ds(0, ROWS), :] = dot(hot_t[j], dxb[j]).astype(BF)
            spots = hot[j].astype(F32) * dgate[j]
            grad_rows = [jnp.sum(spots[e * CAP : (e + 1) * CAP], axis=0, keepdims=True) for e in range(2)]
            wide = [jnp.concatenate([row] * 4, axis=1) for row in grad_rows]
            mine = jnp.where(low_row == my_low, wide[0], jnp.where(low_row == my_low + 1, wide[1], 0.0))
            mine = jnp.where(my_quarter, mine, 0.0)
            high = mine.astype(BF).astype(F32)
            buf[base + j, pl.ds(ROWS, 16), :] = jnp.concatenate([high, mine - high], axis=0).astype(BF)

        reduce_second(i).start()

        @pl.loop(0, 4)
        def _(j):
            @pl.when(i > 0)
            def _():
                store_y(i - 1, j).wait()

            @pl.when((i > 0) & (j == (me.second + 2) % 4))
            def _():
                for step in far_y(i - 1):
                    step.wait_send()

            ystage[j] = dot(hot_t[j], yb[j]).astype(BF)
            store_y(i, j).start()

        @pl.when(i < 3)
        def _():
            for step in far_y(i):
                step.start()


    for j in range(4):
        store_y(3, j).wait()

    leaving = [None] * 4

    def weight_chunk(number):
        stays, n = number >= 6, number % 6
        expert = me.core if stays else 1 - me.core
        rows = pl.ds(pl.multiple_of(expert * CAP, 32), CAP)
        slot = number % 4
        if leaving[slot] is not None:
            for step in leaving[slot]:
                step()
        if n < 2:
            inner = act[:, :, rows, pl.ds(n * 256, 256)].reshape(16 * CAP, 256)
            outer = gxb[:, :, rows, :].reshape(16 * CAP, 1024)
            parts = [(ystage.at[slot], own_d_out if stays else pair_d_out, n)]
        else:
            n = n - 2
            inner = xb[:, :, rows, pl.ds(n * 256, 256)].reshape(16 * CAP, 256)
            outer = dgu[:, :, rows, :].reshape(16 * CAP, 1024)
            parts = [
                (ystage.at[slot, :, pl.ds(0, 512)], own_g_out if stays else pair_g_out, n),
                (ystage.at[slot, :, pl.ds(512, 512)], own_u_out if stays else pair_u_out, n),
            ]
        ystage[slot] = dot(inner, outer, TN).astype(BF)
        leaving[slot] = []
        for part, (stage, out, n) in enumerate(parts):
            target = out.at[pl.ds(n * 256, 256), :]
            if stays:
                step = pltpu.make_async_copy(stage, target, y_local.at[2 * slot + part])
                leaving[slot].append(step.wait)
            else:
                step = p_wires.copy(stage, target, 2 * number + part, me.sibling())
                leaving[slot].append(step.wait_send)
            step.start()

    for number in range(3):
        weight_chunk(number)
    reduce_first.middle(1)
    reduce_second(3).middle(0)
    reduce_second(3).middle(1)
    reduce_second(2).finish()
    reduce_first.middle(0)
    for number in range(3, 12):
        weight_chunk(number)
    reduce_second(3).finish()
    mine = me.block(0, 0)
    for step in reduce_first.mid:
        step.wait_recv()
    add_into(buf.at[mine], landing_f.at[0], landing_f.at[1])
    result = pltpu.make_async_copy(buf.at[mine], dx_out, local.at[0])
    result.start()
    for steps in leaving:
        for step in steps:
            step()
    for number in range(6):
        outs = (pair_d_out,) if number < 2 else (pair_g_out, pair_u_out)
        for part, out in enumerate(outs):
            here = out.at[pl.ds((number if number < 2 else number - 2) * 256, 256), :]
            p_wires.copy(here, here, 2 * number + part, me.sibling()).wait_recv()
    for step in range(4):
        reduce_second(step).wait_sent()
    reduce_first.wait_sent()
    for step in weights:
        step.wait_sent()
    for i in range(3):
        for step in far_y(i):
            step.wait_recv()
    result.wait()


def expert_stage(*arrays):
    dma = pltpu.SemaphoreType.DMA
    s, v = jax.ShapeDtypeStruct, pltpu.VMEM
    return call(
        expert_kernel,
        (
            s((BLOCK, 1024), BF),
            s((16, ROWS, 1024), BF),
            s((3, ROWS, 1024), BF),
            s((1024, 512), BF),
            s((1024, 512), BF),
            s((512, 1024), BF),
            s((1024, 512), BF),
            s((1024, 512), BF),
            s((512, 1024), BF),
        ),
        [ANY] * 6,
        (ANY,) * 9,
        [
            v((2, 8, 1024, 128), BF),
            v((2, 4, 128, 1024), BF),
            v((32, 1024), BF),
            v((16, BLOCK, 1024), BF),
            v((2, 4, BLOCK, 1024), BF),
            v((4, BLOCK, 1024), BF),
            v((4, 2, BLOCK, 1024), BF),
            v((BLOCK, 1024), BF),
            v((2, BLOCK, 1024), BF),
            v((4, 4, 2 * CAP, 1024), BF),
            v((4, 4, 2 * CAP, 1024), BF),
            v((4, 2 * CAP, 1024), BF),
            v((4, 2 * CAP, 1024), BF),
            v((4, 4, 2 * CAP, 512), BF),
            v((4, 4, 2 * CAP, 1024), BF),
            v((4, 2 * CAP, 256), BF),
            v((4, 256, 2 * CAP), BF),
            v((4, 2 * CAP, 1), F32),
            v((4, 2 * CAP, 1), F32),
            v((4, ROWS, 1024), BF),
            dma((20,)),
            dma((20,)),
            dma((20,)),
            dma((20,)),
            dma((15,)),
            dma((15,)),
            dma((12,)),
            dma((12,)),
            dma((6,)),
            dma((6,)),
            dma((5,)),
            dma((2,)),
            dma((8,)),
        ],
        1,
        vmem=62,
    )(*arrays)


class Sum:
    def __init__(self, me, wires, base, own, pair, part_f, part_x, part_s, part_o, total):
        self.pair, self.part_f, self.part_x, self.part_s, self.part_o = pair, part_f, part_x, part_s, part_o

        def half_of(core):
            return pl.ds(pl.multiple_of(core * HALF, HALF), HALF)

        def cols_of(place):
            return pl.ds(pl.multiple_of(((place + 4) % 4) * 256, 256), 256)

        def there(rows, cols, number, device):
            return wires.copy(total.at[rows, cols], total.at[rows, cols], base + number, device)

        other, first, second = 1 - me.core, me.first, me.second
        kept, steps = half_of(me.core), (1, 2, 3)
        cols = cols_of(first)
        self.kept = own.at[:, kept]
        self.mine_f, self.mine_x = own.at[:, kept, cols], own.at[me.x, kept, cols]
        self.swap = wires.copy(own.at[:, half_of(other), :], pair, base, me.sibling())
        self.out_f = [
            wires.copy(own.at[:, kept, cols_of(first + k)], part_f.at[k - 1], base + k, me.at(k, 0)) for k in steps
        ]
        self.out_x = [
            wires.copy(own.at[(me.x + k) % 4, kept, cols], part_x.at[k - 1], base + 3 + k, me.along_x(k)) for k in steps
        ]
        self.out_s = [wires.copy(part_s.at[0], part_s.at[k], base + 6 + k, me.at(0, k)) for k in steps]
        self.out_s += [wires.copy(part_s.at[0], part_o.at[k], base + 10 + k, me.other_at(0, k)) for k in range(4)]
        self.result, self.result_other = total.at[kept, cols], total.at[half_of(other), cols_of(second)]
        self.back = [there(kept, cols, 13 + k, me.at(k, 0)) for k in steps]
        self.back += [there(kept, cols, 16 + k, me.other_at(k, 0)) for k in steps]
        self.came = [there(kept, cols_of(first - k), 13 + k, me.at(k, 0)) for k in steps]
        self.came += [there(half_of(other), cols_of(second - k), 16 + k, me.at(1, 0)) for k in steps]

    def step(self, number):
        if number == 0:
            self.swap.start()
        elif number == 1:
            self.swap.wait_recv()
            add_into(self.kept, self.pair)
            for copy in self.out_f:
                copy.start()
        elif number == 2:
            for copy in self.out_f:
                copy.wait_recv()
            add_into(self.mine_f, *[self.part_f.at[n] for n in range(3)])
            for copy in self.out_x:
                copy.start()
        elif number == 3:
            for copy in self.out_x:
                copy.wait_recv()
            add_up(self.part_s.at[0], self.mine_x, *[self.part_x.at[n] for n in range(3)])
            for copy in self.out_s:
                copy.start()
        elif number == 4:
            for copy in self.out_s:
                copy.wait_recv()
            add_up(self.result, *[self.part_s.at[n] for n in range(4)])
            add_up(self.result_other, *[self.part_o.at[n] for n in range(4)])
            for copy in self.back:
                copy.start()
        else:
            for copy in self.came:
                copy.wait_recv()

    def wait_sent(self):
        for copy in [self.swap] + self.out_f + self.out_x + self.out_s + self.back:
            copy.wait_send()


LOADED = {
    "summed": ((BLOCK, 1024), BF),
    "h2": ((ROWS, 1024), BF),
    "middle": ((ROWS, 1024), F32),
    "cot": ((ROWS, 1024), BF),
    "tok": ((ROWS, 1024), BF),
    "mixed": ((ROWS, 1024), BF),
    "h1": ((ROWS, 1024), BF),
    "qpre": ((ROWS, 1024), F32),
    "kpre": ((ROWS, 512), F32),
    "qa": ((HEAD_PAIRS, 1024, 256), BF),
    "kv": ((4, ROWS, 1024), BF),
    "wk": ((1024, 512), BF),
    "wv": ((1024, 512), BF),
    "small": ((SMALL, 1024), BF),
    "rope": ((2, ROWS, 128), F32),
    "aug": ((ROWS + 1024, 128), BF),
    "places": ((32, ROWS), F32),
}


def backward_kernel(*refs):
    sources, refs = dict(zip(LOADED, refs)), refs[len(LOADED) :]
    wq, wo, gw, uw, dw, gp, up, dp, y, y_near = refs[:10]
    layer_out, tokens_out, total_out, small_out, g_out, u_out, d_out, y_land = refs[10:18]
    refs = refs[18:]
    held, refs = dict(zip(LOADED, refs)), refs[len(LOADED) :]
    (
        doa,
        dqa,
        dkv,
        wbuf,
        parts,
        pair_w,
        part_f,
        part_x,
        part_s,
        part_o,
        total_w,
        near_k,
        land_k,
        own_g,
        own_u,
        own_d,
        pair_g,
        pair_u,
        pair_d,
        near_g,
        near_u,
        near_d,
        land_g,
        land_u,
        land_d,
        buf,
        y_sum,
        near_y,
        near_last,
        far_block,
        near_f,
        land_f,
        small_part,
        small_pair,
        small_x,
        small_f,
        small_s,
        layer,
        grad_middle,
        small_total,
        final_g,
        final_u,
        final_d,
        e_send,
        e_recv,
        w_send,
        w_recv,
        k_send,
        k_recv,
        y_send,
        y_recv,
        t_send,
        t_recv,
        local,
        fetched,
        leave,
    ) = refs
    summed, h2, middle, cot, tok, mixed, h1, qpre, kpre, qa, kv, wk, wv, small, rope, aug, places = held.values()
    me = Place()
    x, core = me.x, me.core
    right, left, sibling = me.along_x(1), me.along_x(-1), me.sibling()
    planes = [me.at(k, 0) for k in (1, 2, 3)] + [me.at(0, k) for k in (1, 2, 3)] + [me.along_x(k) for k in (1, 2, 3)]
    planes += [me.other_at(0, 0)] + [me.other_at(k, 0) for k in (1, 2, 3)] + [me.other_at(0, k) for k in (1, 2, 3)]
    e_wires, w_wires, k_wires = Wires(e_send, e_recv), Wires(w_send, w_recv), Wires(k_send, k_recv)
    y_wires, t_wires = Wires(y_send, y_recv), Wires(t_send, t_recv)

    def shard(step):
        return (x + step + 4) % 4

    loads = {
        name: pltpu.make_async_copy(sources[name], held[name], fetched.at[n]) for n, name in enumerate(LOADED)
    }
    pulls = [
        pltpu.make_async_copy(source, target, local.at[n])
        for n, (source, target) in enumerate(
            ((gw, own_g), (uw, own_u), (dw, own_d), (gp, pair_g), (up, pair_u), (dp, pair_d), (wo, wbuf))
        )
    ]
    load_wq = pltpu.make_async_copy(wq, wbuf, local.at[7])

    def place_y(i, k):
        return ((me.first + ORDER[i] + 4) % 4) * 4 + (me.second + k + 4) % 4

    load_sides = [
        pltpu.make_async_copy(y.at[place_y(i, 1 - 2 * way)], buf.at[i, way], local.at[8 + 2 * i + way])
        for i in range(4)
        for way in range(2)
    ]
    load_near = pltpu.make_async_copy(y_near, near_y, local.at[16])
    load_far = pltpu.make_async_copy(y.at[place_y(3, 2)], far_block, local.at[17])
    load_own = [
        pltpu.make_async_copy(y.at[place_y(i, 0)], y_sum.at[(me.first + ORDER[i] + 4) % 4], local.at[18 + i])
        for i in range(4)
    ]

    def ready(*names):
        for name in names:
            loads[name].wait()

    leaving = []

    def store(source, target):
        step = pltpu.make_async_copy(source, target, leave.at[len(leaving)])
        leaving.append(step)
        step.start()

    load_far.start()
    for step in pulls[:6]:
        step.start()
    for name in ("summed", "h2", "small", "places", "middle", "cot", "mixed", "aug"):
        loads[name].start()
    pulls[6].start()
    load_near.start()
    for step in load_sides + load_own:
        step.start()
    for name in ("qa", "kv", "rope", "qpre", "kpre", "h1", "wk", "wv", "tok"):
        loads[name].start()
    greet(planes)

    low, high = pl.ds(0, HALF), pl.ds(HALF, HALF)
    s_right, s_left = me.at(0, 1), me.at(0, -1)
    far_y = [
        y_wires.copy(far_block.at[low], near_last.at[low], 4, s_right),
        y_wires.copy(far_block.at[high], near_last.at[high], 5, s_left),
    ]
    mid_y = [
        [
            y_wires.copy(buf.at[i, way], y_land.at[i, way], 6 + 2 * i + way, (s_right, s_left)[way])
            for way in range(2)
        ]
        for i in range(4)
    ]
    load_land = [pltpu.make_async_copy(y_land.at[i], buf.at[i], local.at[8 + i]) for i in range(4)]

    def y_middle(i):
        near = near_last if i == 3 else near_y.at[i]
        add_into(buf.at[i, 0, low], near.at[low])
        add_into(buf.at[i, 1, high], near.at[high])
        for step in mid_y[i]:
            step.start()

    def y_fetch(i):
        for step in mid_y[i]:
            step.wait_recv()
            step.wait_send()
        load_land[i].start()

    def y_finish(i):
        load_land[i].wait()
        add_into(y_sum.at[(me.first + ORDER[i] + 4) % 4], buf.at[i, 0], buf.at[i, 1])

    y_first = ReduceRing(
        y_wires,
        0,
        lambda k, rows: y_sum.at[(me.first + k + 4) % 4, rows],
        lambda rows: near_f.at[rows],
        lambda way: land_f.at[way],
        me.at(1, 0),
        me.at(-1, 0),
        HALF,
        ROWS,
    )
    def weight_sum(n, own):
        return Sum(
            me,
            w_wires,
            20 * n,
            own,
            pair_w.at[n % 2],
            part_f.at[n],
            part_x.at[n],
            part_s.at[n],
            part_o.at[n],
            total_w.at[n],
        )

    out_sum, query_sum, kv_sum = weight_sum(0, parts.at[0]), weight_sum(1, parts.at[1]), weight_sum(2, dkv)

    def weight_grad(target, left_rows, right_rows):
        for k in range(4):
            target[k] = dot(left_rows[:, k * ROWS : (k + 1) * ROWS], right_rows, TN).astype(BF)

    def slice_of(k):
        return pl.ds(pl.multiple_of(shard(k) * 128, 128), 128)

    def g_at(k, ref=None):
        return (own_g if ref is None else ref).at[:, slice_of(k)]

    def u_at(k, ref=None):
        return (own_u if ref is None else ref).at[:, slice_of(k)]

    def d_at(k, start=0, size=128, ref=None):
        return (own_d if ref is None else ref).at[pl.ds(pl.multiple_of(shard(k) * 128 + start, 64), size), :]

    e_far = [
        e_wires.copy(g_at(2), near_g, 3, right),
        e_wires.copy(d_at(2, 0, 64), near_d.at[0], 4, right),
        e_wires.copy(u_at(2), near_u, 5, left),
        e_wires.copy(d_at(2, 64, 64), near_d.at[1], 6, left),
    ]
    e_mid = [
        e_wires.copy(ref, land.at[way], 7 + way * 3 + i, device)
        for way, (k, device) in enumerate(((1, right), (-1, left)))
        for i, (ref, land) in enumerate(((g_at(k), land_g), (u_at(k), land_u), (d_at(k), land_d)))
    ]

    def add_pair(k):
        add_into(g_at(k), g_at(k, pair_g))
        add_into(u_at(k), u_at(k, pair_u))
        add_into(d_at(k), d_at(k, ref=pair_d))

    load_far.wait()
    for step in far_y:
        step.start()
    for step in pulls[:6]:
        step.wait()
    add_pair(2)
    for step in e_far:
        step.start()
    ready("summed", "h2", "small", "places")
    params = small[...].astype(F32)
    h2_rows = h2[...]
    numbers = summed[pl.ds(ROWS, 16), :].astype(F32)
    numbers = numbers[0:8] + numbers[8:16]
    grad_gates = jnp.concatenate([numbers[:, q * 256 : (q + 1) * 256] for q in range(4)], axis=0)
    logits = dot(small[pl.ds(ROUTER_ROW, 32), :], h2_rows, NT)
    routed = places[...] >= 0.0
    top = jnp.max(jnp.where(routed, logits, -1e30), axis=0, keepdims=True)
    terms = jnp.where(routed, jnp.exp(jnp.where(routed, logits - top, 0.0)), 0.0)
    gates = terms / jnp.sum(terms, axis=0, keepdims=True)
    grad_logits = gates * (grad_gates - jnp.sum(gates * grad_gates, axis=0, keepdims=True))
    grad_router = split_dot(grad_logits, h2_rows)
    for k in range(4):
        small_part[k, pl.ds(0, 32), :] = grad_router[:, k * ROWS : (k + 1) * ROWS]
        small_part[k, pl.ds(32, 16), :] = jnp.zeros((16, ROWS), F32)
    grad = summed[pl.ds(0, ROWS), :].astype(F32) + split_dot(grad_logits, small[pl.ds(ROUTER_ROW, 32), :], TN)

    def norm_back(v, gain, grad, row):
        scale = lax.rsqrt(jnp.mean(v * v, axis=1, keepdims=True) + EPS)
        normed = v * scale
        gained = gain * grad
        gain_grad = jnp.sum(grad * normed, axis=0, keepdims=True)
        for k in range(4):
            small_part[k, row : row + 1, :] = gain_grad[:, k * ROWS : (k + 1) * ROWS]
        return scale * (gained - normed * jnp.mean(gained * normed, axis=1, keepdims=True))

    ready("middle", "cot", "mixed")
    grad_middle[...] = cot[...].astype(F32) + norm_back(middle[...], params[1:2], grad, 33)
    grad_low = grad_middle[...].astype(BF)
    weight_grad(parts.at[0], mixed[...], grad_low)
    out_sum.step(0)
    grad_low = grad_middle[...].astype(BF)
    ready("aug")
    live = aug[pl.ds(0, ROWS), 4:5].astype(F32) == 0.0
    pulls[6].wait()
    grad_mixed = jnp.where(live, dot(grad_low, wbuf[...], NT), 0.0).astype(BF).astype(F32)
    row_dots = split_dot(grad_mixed * mixed[...].astype(F32), head_map(1024))
    lane = lanes()
    for j in range(8):
        for n, head in enumerate(split_heads(grad_mixed[:, j * 128 : (j + 1) * 128], j % 2 == 1)):
            start = ((j % 2) * 2 + n) * ROWS
            marks = jnp.zeros((ROWS, 128), F32)
            for m, part in enumerate(three_parts(-row_dots[:, 2 * j + n : 2 * j + n + 1])):
                marks = jnp.where(lane == 5 + m, part, marks)
            doa[j // 2, pl.ds(start, ROWS), pl.ds(0, 128)] = head.astype(BF)
            doa[j // 2, pl.ds(start, ROWS), pl.ds(128, 128)] = marks.astype(BF)

    load_wq.start()
    for step in [load_near] + load_sides + load_own:
        step.wait()
    for i in range(3):
        y_middle(i)
    ready("qa", "kv")

    def attend(k):
        there = shard(k)
        marks = aug[pl.ds(pl.multiple_of(there * ROWS + ROWS, ROWS), ROWS), :]

        @pl.loop(0, HEAD_PAIRS)
        def _(pair):
            start = pl.multiple_of(pair * 128, 128)
            keys = kv[there, :, pl.ds(start, 128)]
            keyed = jnp.concatenate([keys, marks], axis=1)
            valued = jnp.concatenate([kv[there, :, pl.ds(start + 512, 128)], marks], axis=1)
            p = jnp.exp(dot(qa[pair], keyed, NT))
            ds = (p * dot(doa[pair], valued, NT)).astype(BF)
            dkv[there, :, pl.ds(start + 512, 128)] = dot(p.astype(BF), doa[pair, :, pl.ds(0, 128)], TN).astype(BF)
            dkv[there, :, pl.ds(start, 128)] = dot(ds, qa[pair, :, pl.ds(0, 128)], TN).astype(BF)
            dq = dot(ds, keys)
            if k == 2:
                dqa[pair] = dq
            else:
                dqa[pair] += dq

    kv_ring = ReduceRing(
        k_wires,
        0,
        lambda k, rows: dkv.at[shard(k), rows],
        lambda rows: near_k.at[rows],
        lambda way: land_k.at[way],
        right,
        left,
        HALF,
        ROWS,
    )
    attend(2)
    kv_ring.start()
    out_sum.step(1)
    attend(1)
    for step in far_y:
        step.wait_recv()
    y_middle(3)
    attend(-1)
    kv_ring.middle(0)
    kv_ring.middle(1)
    attend(0)

    def heads_back(pre, grads, gain, count):
        heads = head_map(count)
        scale = head_scale(pre, heads)
        normed = pre * scale
        gained = gain * grads
        mean = split_dot(split_dot(gained * normed, heads) * (1.0 / 64), heads, NT)
        gain_grad = jnp.sum(grads * normed, axis=0, keepdims=True)
        folded = sum(gain_grad[:, j * 128 : (j + 1) * 128] for j in range(count // 128))
        return scale * (gained - normed * mean), folded + pltpu.roll(folded, 64, 1)

    ready("rope", "qpre", "h1")
    blocks = []
    for j in range(8):
        pair, odd = j // 2, j % 2 == 1
        heads = [dqa[pair, pl.ds(((j % 2) * 2 + n) * ROWS, ROWS), :] for n in range(2)]
        blocks.append(turn(join_heads(heads[0], heads[1], odd) * 0.125, rope[0], -rope[1]))
    query_grad, query_gain_grad = heads_back(qpre[...], jnp.concatenate(blocks, axis=1), params[2:3], 1024)
    query_low = query_grad.astype(BF)
    weight_grad(parts.at[1], h1[...], query_low)
    query_sum.step(0)
    for k in (1, -1, 0):
        add_pair(k)
    e_far[0].wait_recv()
    add_into(g_at(1), near_g)
    e_far[1].wait_recv()
    add_into(d_at(1, 0, 64), near_d.at[0])
    e_far[2].wait_recv()
    add_into(u_at(-1), near_u)
    e_far[3].wait_recv()
    add_into(d_at(-1, 64, 64), near_d.at[1])
    out_sum.step(2)
    query_sum.step(1)
    y_fetch(1)
    load_wq.wait()
    grad_h1 = dot(query_low, wbuf[...], NT)
    ready("kpre")
    y_finish(1)
    y_first.start()

    kv_ring.finish()
    for step in e_mid[0:2] + e_mid[3:5]:
        step.start()
    own_kv = dkv[x].astype(F32)
    blocks = [turn(own_kv[:, j * 128 : (j + 1) * 128], rope[0], -rope[1]) for j in range(4)]
    key_grad, key_gain_grad = heads_back(kpre[...], jnp.concatenate(blocks, axis=1), params[3:4, 0:512], 512)
    low = jnp.concatenate([key_grad.astype(BF), own_kv[:, 512:1024].astype(BF)], axis=1)
    kv_ring.wait_sent()
    weight_grad(dkv, h1[...], low)
    kv_sum.step(0)
    ready("wk", "wv", "tok")
    grad_h1 = grad_h1 + dot(low[:, 0:512], wk[...], NT) + dot(low[:, 512:1024], wv[...], NT)
    grad_middle[...] += norm_back(tok[...].astype(F32), params[0:1], grad_h1, 32)
    store(grad_middle, tokens_out)
    for k in range(4):
        for row, folded in ((34, query_gain_grad), (35, key_gain_grad)):
            small_part[k, row : row + 1, pl.ds(0, 128)] = pltpu.roll(folded, (128 - 16 * k) % 128, 1)

    t_pair = t_wires.copy(small_part, small_pair, 0, sibling)
    t_pair.start()
    kv_sum.step(1)
    out_sum.step(3)
    y_fetch(0)
    y_fetch(2)
    y_finish(0)
    y_finish(2)
    query_sum.step(2)
    y_first.middle_both()
    y_fetch(3)
    t_pair.wait_recv()
    t_x = [t_wires.copy(small_part.at[shard(k)], small_x.at[k - 1], k, me.along_x(k)) for k in (1, 2, 3)]
    t_pair.wait_send()
    for k in range(4):
        small_part[k] += small_pair[k]
    for step in t_x:
        step.start()
    y_finish(3)
    out_sum.step(4)
    kv_sum.step(2)
    e_mid[2].start()
    e_mid[5].start()
    query_sum.step(3)
    kv_sum.step(3)
    query_sum.step(4)
    for step in t_x:
        step.wait_recv()
    small_f[0] = small_part[x] + small_x[0] + small_x[1] + small_x[2]
    t_f = [t_wires.copy(small_f.at[0], small_f.at[k], 3 + k, me.at(k, 0)) for k in (1, 2, 3)]
    for step in t_f:
        step.start()
    kv_sum.step(4)
    y_first.finish()
    layer[...] = (middle[...] + y_sum[me.first].astype(F32)).astype(BF)
    store(layer, layer_out)
    for step in t_f:
        step.wait_recv()
    small_s[0] = small_f[0] + small_f[1] + small_f[2] + small_f[3]
    t_s = [t_wires.copy(small_s.at[0], small_s.at[k], 6 + k, me.at(0, k)) for k in (1, 2, 3)]
    for step in t_s:
        step.start()
    for step in e_mid:
        step.wait_recv()
    for out, at, land, target in (
        (final_g, g_at, land_g, g_out),
        (final_u, u_at, land_u, u_out),
        (final_d, d_at, land_d, d_out),
    ):
        add_up(out, at(0), land.at[0], land.at[1])
        store(out, target)
    out_sum.step(5)
    store(total_w.at[0], total_out.at[0])
    query_sum.step(5)
    store(total_w.at[1], total_out.at[1])
    kv_sum.step(5)
    store(total_w.at[2], total_out.at[2])
    for step in t_s:
        step.wait_recv()
    small_total[...] = small_s[0] + small_s[1] + small_s[2] + small_s[3]
    store(small_total, small_out)
    for step in e_far + e_mid + t_x + t_f + t_s + far_y:
        step.wait_send()
    for ring in [y_first, out_sum, query_sum, kv_sum]:
        ring.wait_sent()
    for step in leaving:
        step.wait()


def backward_stage(*arrays):
    dma = pltpu.SemaphoreType.DMA
    s, v = jax.ShapeDtypeStruct, pltpu.VMEM
    return call(
        backward_kernel,
        (
            s((ROWS, 1024), BF),
            s((ROWS, 1024), F32),
            s((3, ROWS, 1024), BF),
            s((SMALL, ROWS), F32),
            s((1024, 128), F32),
            s((1024, 128), F32),
            s((128, 1024), F32),
            s((4, 2, ROWS, 1024), BF),
        ),
        [ANY] * (len(LOADED) + 10),
        (ANY,) * 8,
        [v(*one) for one in LOADED.values()]
        + [
            v((HEAD_PAIRS, 1024, 256), BF),
            v((HEAD_PAIRS, 1024, 128), F32),
            v((4, ROWS, 1024), BF),
            v((1024, 1024), BF),
            v((2, 4, ROWS, 1024), BF),
            v((2, 4, HALF, 1024), BF),
            v((3, 3, 4, HALF, 256), BF),
            v((3, 3, HALF, 256), BF),
            v((3, 4, HALF, 256), BF),
            v((3, 4, HALF, 256), BF),
            v((3, ROWS, 1024), BF),
            v((ROWS, 1024), BF),
            v((2, ROWS, 1024), BF),
            v((1024, 512), BF),
            v((1024, 512), BF),
            v((512, 1024), BF),
            v((1024, 512), BF),
            v((1024, 512), BF),
            v((512, 1024), BF),
            v((1024, 128), BF),
            v((1024, 128), BF),
            v((2, 64, 1024), BF),
            v((2, 1024, 128), BF),
            v((2, 1024, 128), BF),
            v((2, 128, 1024), BF),
            v((4, 2, ROWS, 1024), BF),
            v((4, ROWS, 1024), BF),
            v((3, ROWS, 1024), BF),
            v((ROWS, 1024), BF),
            v((ROWS, 1024), BF),
            v((ROWS, 1024), BF),
            v((2, ROWS, 1024), BF),
            v((4, SMALL, ROWS), F32),
            v((4, SMALL, ROWS), F32),
            v((3, SMALL, ROWS), F32),
            v((4, SMALL, ROWS), F32),
            v((4, SMALL, ROWS), F32),
            v((ROWS, 1024), BF),
            v((ROWS, 1024), F32),
            v((SMALL, ROWS), F32),
            v((1024, 128), F32),
            v((1024, 128), F32),
            v((128, 1024), F32),
            dma((13,)),
            dma((13,)),
            dma((60,)),
            dma((60,)),
            dma((4,)),
            dma((4,)),
            dma((14,)),
            dma((14,)),
            dma((10,)),
            dma((10,)),
            dma((22,)),
            dma((len(LOADED),)),
            dma((9,)),
        ],
        2,
        vmem=63,
    )(*arrays)


def last_kernel(layer, tokens, totals, small, g, u, d, *rest):
    outs, (layer_v, tokens_v, totals_v, small_v, g_v, u_v, d_v), held, sem = rest[:13], rest[13:20], rest[20:24], rest[24]
    sources = (totals, small, tokens, layer, g, u, d)
    inside = (totals_v, small_v, tokens_v, layer_v, g_v, u_v, d_v)
    loads = [pltpu.make_async_copy(source, inner, sem.at[n]) for n, (source, inner) in enumerate(zip(sources, inside))]
    for step in loads:
        step.start()
    layer_out, tokens_out, g_out, u_out, d_out, wq, wk, wv, wo, first, second, heads, router = outs
    wq_v, wk_v, wv_v, wo_v = held
    stores = []

    def store(source, target):
        step = pltpu.make_async_copy(source, target, sem.at[7 + len(stores)])
        stores.append(step)
        step.start()

    loads[0].wait()
    wq_v[...] = totals_v[1].astype(F32)
    store(wq_v, wq)
    wo_v[...] = totals_v[0].astype(F32)
    store(wo_v, wo)
    wk_v[...] = totals_v[2, :, pl.ds(0, 512)].astype(F32)
    store(wk_v, wk)
    wv_v[...] = totals_v[2, :, pl.ds(512, 512)].astype(F32)
    store(wv_v, wv)
    loads[1].wait()
    first[...] = small_v[32:33, :]
    second[...] = small_v[33:34, :]
    heads[...] = small_v[34:36, 0:16]
    router[...] = small_v[0:32, :]
    for step, inner, target in zip(loads[2:], inside[2:], (tokens_out, layer_out, g_out, u_out, d_out)):
        step.wait()
        store(inner, target)
    for step in stores:
        step.wait()


def last_stage(*arrays):
    s, v = jax.ShapeDtypeStruct, pltpu.VMEM
    return pl.pallas_call(
        last_kernel,
        out_shape=(
            s((ROWS, 1024), BF),
            s((ROWS, 1024), F32),
            s((1024, 128), F32),
            s((1024, 128), F32),
            s((128, 1024), F32),
            s((ROWS, 1024), F32),
            s((ROWS, 512), F32),
            s((ROWS, 512), F32),
            s((ROWS, 1024), F32),
            s((1, ROWS), F32),
            s((1, ROWS), F32),
            s((2, 16), F32),
            s((32, ROWS), F32),
        ),
        in_specs=[ANY] * 7,
        out_specs=(ANY,) * 9 + (VMEM,) * 4,
        scratch_shapes=[
            v((ROWS, 1024), BF),
            v((ROWS, 1024), F32),
            v((3, ROWS, 1024), BF),
            v((SMALL, ROWS), F32),
            v((1024, 128), F32),
            v((1024, 128), F32),
            v((128, 1024), F32),
            v((ROWS, 1024), F32),
            v((ROWS, 512), F32),
            v((ROWS, 512), F32),
            v((ROWS, 1024), F32),
            pltpu.SemaphoreType.DMA((16,)),
        ],
        compiler_params=pltpu.CompilerParams(vmem_limit_bytes=62 * MIB),
    )(*arrays)


def body(
    tokens,
    lengths,
    routes,
    norm1_gain,
    w_query,
    w_key,
    w_value,
    query_gain,
    key_gain,
    w_out,
    norm2_gain,
    w_router,
    w_gate,
    w_up,
    w_down,
    cotangent,
):
    frequency = (ROPE_BASE ** -((np.arange(128) % 32) / 32.0)).astype(np.float32)[None]
    gains = jnp.concatenate(
        [norm1_gain, norm2_gain, jnp.pad(query_gain, (0, ROWS - 16)), jnp.pad(key_gain, (0, ROWS - 16))]
    ).reshape(4, ROWS)
    (h2, middle, mixed, h1, qpre, kpre, qa, kv, wq, wk, wv, wo, small, rope, aug, places, g_all) = attention_forward(
        tokens,
        routes.T,
        lengths,
        gains,
        w_router.T,
        jnp.asarray(frequency),
        w_key,
        w_value,
        w_query,
        w_out,
        cotangent,
    )
    summed, y_part, y_near, *expert_grads = expert_stage(
        h2, g_all, small, w_gate[0], w_up[0], w_down[0]
    )
    results = backward_stage(
        summed,
        h2,
        middle,
        cotangent,
        tokens,
        mixed,
        h1,
        qpre,
        kpre,
        qa,
        kv,
        wk,
        wv,
        small,
        rope,
        aug,
        places,
        wq,
        wo,
        *expert_grads,
        y_part,
        y_near,
    )
    layer, tokens_grad, gate_grad, up_grad, down_grad, wq_g, wk_g, wv_g, wo_g, first, second, heads, router = last_stage(
        *results[:7]
    )
    return (
        layer,
        tokens_grad,
        first[0],
        wq_g,
        wk_g,
        wv_g,
        heads[0],
        heads[1],
        wo_g,
        second[0],
        router.T,
        gate_grad[None],
        up_grad[None],
        down_grad[None],
    )


def solution(mesh):
    rows = P(("expert", "shard"), None)
    by_shard = P("shard", None)
    columns = P("expert", None, "shard")
    placed = (
        rows,
        P("expert", None),
        rows,
        P("shard"),
        by_shard,
        by_shard,
        by_shard,
        P("shard"),
        P("shard"),
        by_shard,
        P("shard"),
        by_shard,
        columns,
        columns,
        P("expert", "shard", None),
        rows,
    )
    return jax.shard_map(
        body,
        mesh=mesh,
        in_specs=placed,
        out_specs=(
            rows,
            rows,
            P("shard"),
            by_shard,
            by_shard,
            by_shard,
            P("shard"),
            P("shard"),
            by_shard,
            P("shard"),
            by_shard,
            columns,
            columns,
            P("expert", "shard", None),
        ),
        check_vma=False,
    )
```

```python
import math

import jax
import jax.numpy as jnp
import numpy as np
from jax import lax
from jax.experimental import pallas as pl
from jax.experimental.pallas import tpu as pltpu
from jax.sharding import PartitionSpec as P

CAP = 96
EPS = 1e-06
ROPE_BASE = 10000.0
BF = jnp.bfloat16
F32 = jnp.float32
MESH = pl.DeviceIdType.MESH
ANY = pl.BlockSpec(memory_space=pl.ANY)
VMEM = pl.BlockSpec(memory_space=pltpu.VMEM)
MIB = 1 << 20
W_COLS = 3328
W_HALF = W_COLS // 2
ROWS = 256
BLOCK = 272
HALF = 128


class Place:
    def __init__(self):
        self.expert = lax.axis_index("expert")
        self.x = lax.axis_index("shard")
        self.core = self.expert % 2
        self.chip = self.expert // 2
        y, z = self.chip % 4, self.chip // 4
        self.first = z + self.core * (y - z)
        self.second = y + self.core * (z - y)
        self.first_stride = 8 - 6 * self.core
        self.second_stride = 2 + 6 * self.core

    def block(self, first, second):
        return ((self.first + first + 4) % 4) * 4 + (self.second + second + 4) % 4

    def at(self, first, second):
        near = ((self.first + first + 4) % 4) * self.first_stride
        return {"expert": near + ((self.second + second + 4) % 4) * self.second_stride + self.core}

    def other_at(self, first, second):
        there = self.at(first, second)["expert"]
        return {"expert": there + 1 - 2 * self.core}

    def along_x(self, step):
        return {"shard": (self.x + step + 4) % 4}

    def sibling(self):
        return {"expert": self.expert + 1 - 2 * self.core}


def greet(devices, wait=True):
    barrier = pltpu.get_barrier_semaphore()
    for device in devices:
        pl.semaphore_signal(barrier, inc=1, device_id=device, device_id_type=MESH)
    if wait:
        wait_for(devices)


def wait_for(devices):
    pl.semaphore_wait(pltpu.get_barrier_semaphore(), len(devices))


class Copy:
    def __init__(self, *parts):
        self.parts = parts

    def made(self):
        return pltpu.make_async_remote_copy(*self.parts, device_id_type=MESH)

    def start(self):
        self.made().start()

    def wait_send(self):
        self.made().wait_send()

    def wait_recv(self):
        self.made().wait_recv()


class Wires:
    def __init__(self, send, recv):
        self.send, self.recv = send, recv

    def copy(self, source, target, number, device):
        return Copy(source, target, self.send.at[number], self.recv.at[number], device)


class GatherRing:
    def __init__(self, wires, base, at, own, right, left, half, rows):
        low, high, full = pl.ds(0, half), pl.ds(half, rows - half), pl.ds(0, rows)
        copy = wires.copy
        self.go = [copy(own, at(0, full), base, right), copy(own, at(0, full), base + 1, left)]
        self.came = [copy(at(-1, full), at(-1, full), base, right), copy(at(1, full), at(1, full), base + 1, left)]
        self.on = [copy(at(-1, low), at(-1, low), base + 2, right), copy(at(1, high), at(1, high), base + 3, left)]
        self.far = [copy(at(2, low), at(2, low), base + 2, right), copy(at(2, high), at(2, high), base + 3, left)]

    def start(self):
        for step in self.go:
            step.start()

    def forward(self, way):
        self.came[way].wait_recv()
        self.on[way].start()

    def wait_far(self):
        for step in self.far:
            step.wait_recv()

    def wait_sent(self):
        for step in self.go + self.on:
            step.wait_send()


class ReduceRing:
    def __init__(self, wires, base, at, near, landing, right, left, half, rows):
        low, high, full = pl.ds(0, half), pl.ds(half, rows - half), pl.ds(0, rows)
        copy = wires.copy
        self.at, self.near, self.landing = at, near, landing
        self.parts = [low, high, full]
        self.far = [copy(at(2, low), near(low), base, right), copy(at(2, high), near(high), base + 1, left)]
        self.mid = [copy(at(1, full), landing(0), base + 2, right), copy(at(-1, full), landing(1), base + 3, left)]

    def start(self):
        for step in self.far:
            step.start()

    def middle(self, way):
        self.far[way].wait_recv()
        side = 1 - 2 * way
        add_into(self.at(side, self.parts[way]), self.near(self.parts[way]))
        self.mid[way].start()

    def middle_both(self):
        for way in range(2):
            self.far[way].wait_recv()
        for way in range(2):
            add_into(self.at(1 - 2 * way, self.parts[way]), self.near(self.parts[way]))
        for way in range(2):
            self.mid[way].start()

    def finish(self, target=None):
        for step in self.mid:
            step.wait_recv()
        own = self.at(0, self.parts[2])
        if target is None:
            add_into(own, self.landing(0), self.landing(1))
        else:
            add_up(target, own, self.landing(0), self.landing(1))

    def wait_sent(self):
        for step in self.far + self.mid:
            step.wait_send()


def add_up(target, *terms):
    if len(target.shape) == 3:
        for k in range(target.shape[0]):
            add_up(target.at[k], *[term.at[k] for term in terms])
        return
    rows, columns = target.shape
    size = min(rows, 16 * max(1, 1024 // columns))

    @pl.loop(0, rows // size)
    def _(i):
        here = pl.ds(pl.multiple_of(i * size, 16), size)
        total = terms[0][here, :].astype(F32)
        for term in terms[1:]:
            total = total + term[here, :].astype(F32)
        target[here, :] = total.astype(target.dtype)


def add_into(target, *terms):
    add_up(target, target, *terms)


def dot(a, b, contract=((1,), (0,))):
    return lax.dot_general(a, b, (contract, ((), ())), preferred_element_type=F32)


NT = ((1,), (1,))
TN = ((0,), (0,))


def call(kernel, out_shape, in_specs, out_specs, scratch, ident, vmem=56):
    return pl.pallas_call(
        kernel,
        out_shape=out_shape,
        in_specs=in_specs,
        out_specs=out_specs,
        scratch_shapes=scratch,
        compiler_params=pltpu.CompilerParams(
            collective_id=ident, has_side_effects=True, vmem_limit_bytes=vmem * MIB
        ),
    )


HEAD_PAIRS = 4
NORM_ROW, QUERY_ROW = 0, 2
ROUTER_ROW = 16
SMALL = 48


def lanes(rows=ROWS, columns=128):
    return lax.broadcasted_iota(jnp.int32, (rows, columns), 1)


def head_map(columns):
    column = lax.broadcasted_iota(jnp.int32, (columns, 128), 0) // 64
    return (column == lax.broadcasted_iota(jnp.int32, (columns, 128), 1)).astype(F32).astype(BF)


def split_dot(a, exact, contract=((1,), (0,))):
    high = a.astype(BF)
    low = (a - high.astype(F32)).astype(BF)
    return dot(high, exact, contract) + dot(low, exact, contract)


def head_scale(v, heads):
    mean = split_dot(v * v, heads) * (1.0 / 64)
    return split_dot(lax.rsqrt(mean + EPS), heads, NT)


def turn(v, cosine, sine):
    lower = lanes() % 64 < 32
    swapped = jnp.where(lower, pltpu.roll(v, 96, 1), pltpu.roll(v, 32, 1))
    return v * cosine + swapped * sine


def split_heads(block, odd):
    keep = lanes() >= 64 if odd else lanes() < 64
    rolled = pltpu.roll(block, 64, 1)
    first, second = (rolled, block) if odd else (block, rolled)
    return jnp.where(keep, first, 0.0), jnp.where(keep, second, 0.0)


def join_heads(first, second, odd):
    low = pltpu.roll(first, 64, 1) if odd else first
    high = second if odd else pltpu.roll(second, 64, 1)
    return jnp.where(lanes() < 64, low, high)


def three_parts(v):
    high = v.astype(BF).astype(F32)
    middle = (v - high).astype(BF).astype(F32)
    return high, middle, v - high - middle


def passed_documents(lengths, rows, first):
    position = (lax.broadcasted_iota(jnp.int32, (rows, 128), 0) + first).astype(F32)
    end = jnp.zeros((1, 1), F32)
    number, start = jnp.zeros((rows, 128), F32), jnp.zeros((rows, 128), F32)
    for d in range(4):
        length = lengths[:, d : d + 1]
        end = end + length
        number = number + jnp.where(position >= end, 1.0, 0.0)
        start = start + jnp.where(position >= end, length, 0.0)
    return number, position - start


def attention_kernel(
    tok,
    routes,
    lengths,
    gains,
    router,
    frequency,
    wk_in,
    wv_in,
    wq_in,
    wo_in,
    g,
    h2_out,
    middle_out,
    mixed_out,
    h1_out,
    qpre_out,
    kpre_out,
    qa_out,
    kv_out,
    wq_out,
    wk_out,
    wv_out,
    wo_out,
    small_out,
    rope_out,
    aug_out,
    places_out,
    g_all,
    small,
    small_all,
    g_own,
    total,
    h2,
    middle,
    mixed,
    h1,
    qpre,
    kpre,
    qa,
    kv,
    wq,
    wk,
    wv,
    wo,
    params_low,
    rope,
    aug,
    places,
    local,
    leave,
    w_send,
    w_recv,
    k_send,
    k_recv,
    g_send,
    g_recv,
):
    me = Place()
    x, core = me.x, me.core
    right, left, sibling = me.along_x(1), me.along_x(-1), me.sibling()
    partners = [right, left, sibling, me.at(1, 0), me.at(-1, 0), me.at(0, 1), me.at(0, -1)]
    greet(partners, wait=False)
    w_wires, k_wires, g_wires = Wires(w_send, w_recv), Wires(k_send, k_recv), Wires(g_send, g_recv)

    def shard(step):
        return (x + step + 4) % 4

    leaving = []

    def store(source, target):
        step = pltpu.make_async_copy(source, target, leave.at[len(leaving)])
        leaving.append(step)
        step.start()

    load_g = pltpu.make_async_copy(g, g_own.at[pl.ds(0, ROWS)], local.at[4])
    load_g.start()
    row = lax.broadcasted_iota(jnp.int32, (16, ROWS), 0)
    source = lax.broadcasted_iota(jnp.int32, (128, ROWS), 0)
    column = lanes(128, ROWS)
    spread = ((column % 16 == source) & ((column % 64) // 16 == x)).astype(F32).astype(BF)

    def tiled(gain):
        return dot(jnp.broadcast_to(gain, (16, 128)), spread)[0:1]

    block = jnp.zeros((16, ROWS), F32)
    parts = (gains[0:1, :].astype(F32), gains[1:2, :].astype(F32), tiled(gains[2:3, 0:128]), tiled(gains[3:4, 0:128]))
    for n, part in enumerate(parts):
        block = jnp.where(row == n, part, block)
    small[pl.ds(0, 16), :] = block.astype(BF)
    small[pl.ds(16, 32), :] = router[...]

    expert = lax.broadcasted_iota(jnp.int32, (32, ROWS), 0)
    hits = sum(jnp.where(routes[k : k + 1, :] == expert, 1.0, 0.0) for k in range(8))
    before = (lax.broadcasted_iota(jnp.int32, (ROWS, ROWS), 0) < lanes(ROWS, ROWS)).astype(F32).astype(BF)
    places[...] = jnp.where(hits > 0.0, dot(hits.astype(BF), before), -1.0)
    packed = jnp.concatenate([places[q * 8 : (q + 1) * 8] for q in range(4)], axis=1)
    g_own[pl.ds(ROWS, 16), :] = jnp.concatenate([packed, jnp.zeros((8, 1024), F32)], axis=0).astype(BF)
    load_g.wait()
    wait_for(partners)
    small_ring = GatherRing(w_wires, 0, lambda k, rows: small_all.at[shard(k), rows], small, right, left, 32, SMALL)
    small_ring.start()

    class Weight:
        def __init__(self, source, target, base):
            def at(k, rows, half):
                start = pl.multiple_of(shard(k) * ROWS + half * HALF + rows.start, 64)
                return target.at[pl.ds(start, rows.size), :]

            own = source.at[pl.ds(pl.multiple_of(core * HALF, HALF), HALF), :]
            full = pl.ds(0, HALF)
            self.ring = GatherRing(w_wires, base, lambda k, rows: at(k, rows, core), own, right, left, 64, HALF)
            self.pass_on = [
                w_wires.copy(at(k, full, core), at(k, full, core), base + 4 + n, sibling) for n, k in enumerate((-1, 1, 2))
            ]
            self.passed = [
                w_wires.copy(at(k, full, 1 - core), at(k, full, 1 - core), base + 4 + n, sibling)
                for n, k in enumerate((-1, 1, 2))
            ]
            self.keep = pltpu.make_async_copy(
                source, target.at[pl.ds(pl.multiple_of(x * ROWS, ROWS), ROWS), :], local.at[base // 7]
            )

        def start(self):
            self.ring.start()

        def forward(self):
            for way in range(2):
                self.ring.forward(way)
                self.pass_on[way].start()

        def finish(self):
            self.ring.wait_far()
            self.pass_on[2].start()

        def ready(self):
            for step in self.passed:
                step.wait_recv()

        def wait_sent(self):
            self.ring.wait_sent()
            for step in self.pass_on:
                step.wait_send()

    key_weight, value_weight = Weight(wk_in, wk, 4), Weight(wv_in, wv, 11)
    query_weight, out_weight = Weight(wq_in, wq, 18), Weight(wo_in, wo, 25)
    weights = [key_weight, value_weight, query_weight, out_weight]
    key_weight.start()
    value_weight.start()
    query_weight.keep.start()
    out_weight.keep.start()

    def g_at(fo):
        return lambda k, rows: g_all.at[me.block(fo, k), rows]

    first = GatherRing(
        g_wires, 0, lambda k, rows: g_all.at[me.block(k, 0), rows], g_own, me.at(1, 0), me.at(-1, 0), HALF, BLOCK
    )
    seconds = [
        GatherRing(
            g_wires,
            4 + 4 * i,
            g_at(fo),
            g_own if fo == 0 else g_all.at[me.block(fo, 0)],
            me.at(0, 1),
            me.at(0, -1),
            HALF,
            BLOCK,
        )
        for i, fo in enumerate((-1, 1, 2, 0))
    ]
    first.start()
    own_copies = [
        pltpu.make_async_copy(g_own, g_all.at[me.block(0, 0)], local.at[4]),
        pltpu.make_async_copy(small, small_all.at[x], local.at[5]),
        key_weight.keep,
        value_weight.keep,
    ]
    for step in own_copies:
        step.start()

    ends = lengths[...].astype(F32)
    doc, since = passed_documents(ends, ROWS, x * ROWS)
    lane = lanes()
    aug[pl.ds(0, ROWS), :] = jnp.where(
        lane.astype(F32) == doc, 16.0, jnp.where(lane == 8, -128.0, 0.0)
    ).astype(BF)
    angles = since * frequency[...]
    rope[0] = jnp.cos(angles)
    sine_table = jnp.sin(angles)
    rope[1] = jnp.where(lane % 64 < 32, -sine_table, sine_table)
    doc = passed_documents(ends, 1024, 0)[0]
    lane = lanes(1024)
    aug[pl.ds(ROWS, 1024), :] = jnp.where(
        lane.astype(F32) == doc, 8.0, jnp.where((lane >= 5) & (lane < 9), 1.0, 0.0)
    ).astype(BF)
    store(rope, rope_out)
    store(aug, aug_out)
    store(places, places_out)
    tokens = tok[...].astype(F32)
    tokens = tokens * lax.rsqrt(jnp.mean(tokens * tokens, axis=1, keepdims=True) + EPS)

    for way in range(2):
        small_ring.forward(way)
    key_weight.forward()
    value_weight.forward()
    query_weight.start()
    first.forward(0)
    first.forward(1)
    seconds[3].start()
    seconds[0].start()
    seconds[1].start()
    small_ring.wait_far()
    own_copies[1].wait()
    shares = [small_all[k].astype(F32) for k in range(4)]
    params = jnp.concatenate(shares, axis=1)
    by_head = jnp.concatenate([shares[0] + shares[1] + shares[2] + shares[3]] * 4, axis=1)
    row = lax.broadcasted_iota(jnp.int32, (SMALL, 1024), 0)
    params = jnp.where((row == 2) | (row == 3), by_head, params)
    params_low[...] = params.astype(BF)
    store(params_low, small_out)
    h1[...] = (tokens * params[0:1]).astype(BF)
    store(h1, h1_out)
    key_weight.finish()
    value_weight.finish()
    key_weight.ready()
    key_weight.keep.wait()
    kpre[...] = dot(h1[...], wk[...])
    value_weight.ready()
    value_weight.keep.wait()
    kv[x, :, pl.ds(512, 512)] = dot(h1[...], wv[...]).astype(BF)
    keys = kpre[...]
    keys = keys * head_scale(keys, head_map(512)) * params[3:4, 0:512]
    for j in range(4):
        block = keys[:, j * 128 : (j + 1) * 128]
        kv[x, :, pl.ds(j * 128, 128)] = turn(block, rope[0], rope[1]).astype(BF)
    kv_ring = GatherRing(k_wires, 0, lambda k, rows: kv.at[shard(k), rows], kv.at[x], right, left, HALF, ROWS)
    query_weight.forward()
    kv_ring.start()
    store(kpre, kpre_out)
    store(wk, wk_out)
    store(wv, wv_out)
    first.wait_far()
    seconds[2].start()
    query_weight.finish()
    query_weight.ready()
    query_weight.keep.wait()
    qpre[...] = dot(h1[...], wq[...])
    store(qpre, qpre_out)
    store(wq, wq_out)
    queries = qpre[...]
    queries = queries * head_scale(queries, head_map(1024)) * params[2:3]
    for j in range(8):
        block = turn(queries[:, j * 128 : (j + 1) * 128], rope[0], rope[1]) * 0.125
        for n, head in enumerate(split_heads(block, j % 2 == 1)):
            start = ((j % 2) * 2 + n) * ROWS
            qa[j // 2, pl.ds(start, ROWS), pl.ds(0, 128)] = head.astype(BF)
            qa[j // 2, pl.ds(start, ROWS), pl.ds(128, 128)] = aug[pl.ds(0, ROWS), :]

    def attend(k):
        there = shard(k)
        marks = aug[pl.ds(pl.multiple_of(there * ROWS + ROWS, ROWS), ROWS), :]

        @pl.loop(0, HEAD_PAIRS)
        def _(pair):
            start = pl.multiple_of(pair * 128, 128)
            keyed = jnp.concatenate([kv[there, :, pl.ds(start, 128)], marks], axis=1)
            valued = jnp.concatenate([kv[there, :, pl.ds(start + 512, 128)], marks], axis=1)
            p = jnp.exp(dot(qa[pair], keyed, NT)).astype(BF)
            weighted = dot(p, valued)
            if k == 0:
                total[pair] = weighted
            else:
                total[pair] += weighted

    attend(0)
    kv_ring.forward(0)
    kv_ring.forward(1)
    out_weight.start()
    seconds[3].forward(0)
    seconds[3].forward(1)
    attend(-1)
    attend(1)
    for ring in seconds[0:2]:
        ring.forward(0)
        ring.forward(1)
    kv_ring.wait_far()
    attend(2)
    store(kv, kv_out)
    out_weight.forward()
    seconds[2].forward(0)
    seconds[2].forward(1)

    live = aug[pl.ds(0, ROWS), 4:5].astype(F32) == 0.0
    lane = lanes(1024)

    @pl.loop(0, HEAD_PAIRS)
    def _(pair):
        weighted = total[pair]
        mass = weighted[:, 133:134]
        heads = weighted[:, 0:128] / mass
        parts = three_parts(-jnp.log(mass))
        marks = qa[pair, :, pl.ds(128, 128)].astype(F32)
        for n, part in enumerate(parts):
            marks = jnp.where(lane == 5 + n, part, marks)
        qa[pair, :, pl.ds(128, 128)] = marks.astype(BF)
        heads = [heads[n * ROWS : (n + 1) * ROWS] for n in range(4)]
        for odd in range(2):
            joined = join_heads(heads[2 * odd], heads[2 * odd + 1], odd == 1)
            start = pl.multiple_of(pair * 256 + odd * 128, 128)
            mixed[:, pl.ds(start, 128)] = jnp.where(live, joined, 0.0).astype(BF)

    store(qa, qa_out)
    store(mixed, mixed_out)
    out_weight.finish()
    out_weight.ready()
    out_weight.keep.wait()
    store(wo, wo_out)
    middle[...] = tok[...].astype(F32) + dot(mixed[...], wo[...])
    store(middle, middle_out)
    scale = lax.rsqrt(jnp.mean(middle[...] * middle[...], axis=1, keepdims=True) + EPS)
    h2[...] = (middle[...] * scale * params_low[1:2, :].astype(F32)).astype(BF)
    store(h2, h2_out)
    for ring in [small_ring, kv_ring, first] + weights:
        ring.wait_sent()
    own_copies[0].wait()
    for ring in seconds:
        ring.wait_far()
    for ring in seconds:
        ring.wait_sent()
    for step in leaving:
        step.wait()


def attention_forward(*arrays):
    dma = pltpu.SemaphoreType.DMA
    s, v = jax.ShapeDtypeStruct, pltpu.VMEM
    stored = (
        ((ROWS, 1024), BF),
        ((ROWS, 1024), F32),
        ((ROWS, 1024), BF),
        ((ROWS, 1024), BF),
        ((ROWS, 1024), F32),
        ((ROWS, 512), F32),
        ((HEAD_PAIRS, 1024, 256), BF),
        ((4, ROWS, 1024), BF),
        ((1024, 1024), BF),
        ((1024, 512), BF),
        ((1024, 512), BF),
        ((1024, 1024), BF),
        ((SMALL, 1024), BF),
        ((2, ROWS, 128), F32),
        ((ROWS + 1024, 128), BF),
        ((32, ROWS), F32),
    )
    return call(
        attention_kernel,
        tuple(s(*one) for one in stored) + (s((16, BLOCK, 1024), BF),),
        [VMEM] * 6 + [ANY] * 5,
        (ANY,) * 17,
        [v((SMALL, ROWS), BF), v((4, SMALL, ROWS), BF), v((BLOCK, 1024), BF), v((HEAD_PAIRS, 1024, 256), F32)]
        + [v(*one) for one in stored]
        + [
            dma((6,)),
            dma((16,)),
            dma((32,)),
            dma((32,)),
            dma((4,)),
            dma((4,)),
            dma((20,)),
            dma((20,)),
        ],
        0,
        vmem=56,
    )(*arrays)


ORDER = (-1, 2, 1, 0)


def nth_place(i):
    return 3 - i


class ColumnWeight:
    def __init__(self, me, wires, base, source, target, offset, half, rows, local):
        def at(k, part):
            return target.at[me.core, (me.x + k + 4) % 4 + offset, part]

        self.ring = GatherRing(wires, base, at, source, me.along_x(1), me.along_x(-1), half, rows)
        self.keep = pltpu.make_async_copy(source, at(0, pl.ds(0, rows)), local)
        mine, other = target.at[me.core, pl.ds(offset, 4)], target.at[1 - me.core, pl.ds(offset, 4)]
        self.pass_on = wires.copy(mine, mine, base + 4, me.sibling())
        self.passed = wires.copy(other, other, base + 4, me.sibling())

    def start(self):
        self.ring.start()
        self.keep.start()

    def forward(self):
        self.ring.forward(0)
        self.ring.forward(1)

    def finish(self):
        self.ring.wait_far()
        self.keep.wait()
        self.pass_on.start()

    def wait_sent(self):
        self.ring.wait_sent()
        self.pass_on.wait_send()


def expert_kernel(
    h_ref,
    g_ref,
    router,
    gate_in,
    up_in,
    down_in,
    dx_out,
    y_out,
    y_near,
    own_g_out,
    own_u_out,
    own_d_out,
    pair_g_out,
    pair_u_out,
    pair_d_out,
    wgu,
    wd,
    wr,
    buf,
    gbuf,
    near,
    landing,
    near_f,
    landing_f,
    xb,
    gxb,
    yb,
    dxb,
    act,
    dgu,
    hot,
    hot_t,
    weight,
    dgate,
    ystage,
    a_send,
    a_recv,
    r_send,
    r_recv,
    e_send,
    e_recv,
    p_send,
    p_recv,
    y_send,
    y_recv,
    local,
    g_local,
    y_local,
):
    me = Place()
    f_right, f_left, s_right, s_left = me.at(1, 0), me.at(-1, 0), me.at(0, 1), me.at(0, -1)
    a_wires, r_wires = Wires(a_send, a_recv), Wires(r_send, r_recv)
    e_wires, p_wires, y_wires = Wires(e_send, e_recv), Wires(p_send, p_recv), Wires(y_send, y_recv)
    own = buf.at[me.block(0, 0), pl.ds(0, ROWS)]
    fetches = [
        pltpu.make_async_copy(h_ref, own, local.at[0]),
        pltpu.make_async_copy(router.at[pl.ds(ROUTER_ROW, 32), :], wr, local.at[1]),
    ]
    for step in fetches:
        step.start()
    gate_weight = ColumnWeight(me, e_wires, 0, gate_in, wgu, 0, 512, 1024, local.at[2])
    up_weight = ColumnWeight(me, e_wires, 5, up_in, wgu, 4, 512, 1024, local.at[3])
    down_weight = ColumnWeight(me, e_wires, 10, down_in, wd, 0, 64, 128, local.at[4])
    weights = [gate_weight, up_weight, down_weight]
    greet([f_right, f_left, s_right, s_left, me.along_x(1), me.along_x(-1), me.sibling()])
    order = nth_place

    first = GatherRing(
        a_wires, 0, lambda k, rows: buf.at[me.block(k, 0), rows], own, f_right, f_left, HALF, ROWS
    )

    def second(i):
        fo = order(i)

        def at(k, rows):
            return buf.at[me.block(fo, k), rows]

        return GatherRing(a_wires, 4 + 4 * i, at, at(0, pl.ds(0, ROWS)), s_right, s_left, HALF, ROWS)

    def reduce_second(i):
        fo = order(i)
        return ReduceRing(
            r_wires,
            4 + 4 * i,
            lambda k, rows: buf.at[me.block(fo, k), rows],
            lambda rows: near.at[i, rows],
            lambda way: landing.at[i, way],
            s_right,
            s_left,
            HALF,
            BLOCK,
        )

    reduce_first = ReduceRing(
        r_wires,
        0,
        lambda k, rows: buf.at[me.block(k, 0), rows],
        lambda rows: near_f.at[rows],
        lambda way: landing_f.at[way],
        f_right,
        f_left,
        HALF,
        BLOCK,
    )

    def load_g(i):
        start = ((me.first + order(i)) % 4) * 4
        return pltpu.make_async_copy(g_ref.at[pl.ds(start, 4)], gbuf.at[i % 2], g_local.at[i % 2])

    def store_y(i, j):
        return pltpu.make_async_copy(ystage.at[j], y_out.at[((me.first + order(i)) % 4) * 4 + j], y_local.at[j])

    def far_y(i):
        block = ystage.at[(me.second + 2) % 4]
        low, high = pl.ds(0, HALF), pl.ds(HALF, HALF)
        return [
            y_wires.copy(block.at[low], y_near.at[i, low], 2 * i, s_right),
            y_wires.copy(block.at[high], y_near.at[i, high], 2 * i + 1, s_left),
        ]

    fetches[0].wait()
    first.start()
    gate_weight.start()
    up_weight.start()
    load_g(0).start()
    first.forward(0)
    second(0).start()
    first.forward(1)
    gate_weight.forward()
    up_weight.forward()
    down_weight.start()
    fetches[1].wait()
    gate_weight.finish()
    second(0).forward(0)
    second(0).forward(1)
    first.wait_far()
    second(1).start()
    down_weight.forward()
    up_weight.finish()
    second(2).start()

    expert_row = lax.broadcasted_iota(jnp.int32, (32, 256), 0)
    slot_row = lax.broadcasted_iota(jnp.int32, (CAP, 256), 0).astype(F32)
    low_row = lax.broadcasted_iota(jnp.int32, (8, 1024), 0)
    quarter = lax.broadcasted_iota(jnp.int32, (8, 1024), 1) // 256
    my_quarter = quarter == me.chip // 4
    my_low = 2 * (me.chip % 4)

    def pick(table, e):
        return jnp.sum(jnp.where(expert_row == 2 * me.chip + e, table, 0.0), axis=0, keepdims=True)

    @pl.loop(0, 4)
    def _(i):
        base = ((me.first + order(i)) % 4) * 4
        slot = i % 2
        second(i).wait_far()

        @pl.when(i < 3)
        def _():
            load_g(i + 1).start()

        load_g(i).wait()

        @pl.loop(0, 4)
        def _(j):
            h = buf[base + j, pl.ds(0, ROWS), :]
            g = gbuf[slot, j, pl.ds(0, ROWS), :]
            packed = gbuf[slot, j, pl.ds(ROWS, 16), :].astype(F32)[0:8]
            places = jnp.concatenate([packed[:, q * 256 : (q + 1) * 256] for q in range(4)], axis=0)
            logits = dot(wr[...], h, NT)
            routed = places >= 0.0
            top = jnp.max(jnp.where(routed, logits, -1e30), axis=0, keepdims=True)
            terms = jnp.where(routed, jnp.exp(jnp.where(routed, logits - top, 0.0)), 0.0)
            gates = terms / jnp.sum(terms, axis=0, keepdims=True)
            for e in range(2):
                hit = pick(places, e) == slot_row
                rows = pl.ds(e * CAP, CAP)
                weight[j, rows, :] = jnp.sum(jnp.where(hit, pick(gates, e), 0.0), axis=1, keepdims=True)
                hot[j, rows, :] = hit.astype(F32).astype(BF)
            hot_t[j] = jnp.transpose(hot[j].astype(F32)).astype(BF)
            xb[i, j] = dot(hot[j], h).astype(BF)
            gxb[i, j] = dot(hot[j], g).astype(BF)


        @pl.when(i > 1)
        def _():
            reduce_second(i - 2).finish()

        @pl.when(i == 3)
        def _():
            reduce_first.start()


        @pl.when(i == 0)
        def _():
            second(1).forward(0)
            second(1).forward(1)
            down_weight.finish()
            second(2).forward(0)
            second(2).forward(1)
            second(3).start()
            for step in weights:
                step.passed.wait_recv()

        @pl.when(i == 1)
        def _():
            second(3).forward(0)
            second(3).forward(1)

        @pl.loop(0, 2)
        def _(e):
            rows = pl.ds(pl.multiple_of(e * CAP, 32), CAP)
            x = xb[i, :, rows, :].reshape(4 * CAP, 1024)
            gx = gxb[i, :, rows, :].reshape(4 * CAP, 1024)
            gate = weight[:, rows, :].reshape(4 * CAP, 1)
            dy = (gate * gx.astype(F32)).astype(BF)
            gxb[i, :, rows, :] = dy.reshape(4, CAP, 1024)
            gate_up = jnp.concatenate([wgu[e, n] for n in range(8)], axis=1)
            down = wd[e].reshape(512, 1024)
            both = dot(x, gate_up)
            gate_pre, up_pre = both[:, 0:512], both[:, 512:1024]
            grad_act = dot(dy, down, NT)
            sig = 1.0 / (1.0 + jnp.exp(-gate_pre))
            silu = gate_pre * sig
            active = (silu * up_pre).astype(BF)
            grad_gate = (grad_act * up_pre * (sig * (1.0 + gate_pre * (1.0 - sig)))).astype(BF)
            grad_up = (grad_act * silu).astype(BF)
            act[i, :, rows, :] = active.reshape(4, CAP, 512)
            dgu[i, :, rows, pl.ds(0, 512)] = grad_gate.reshape(4, CAP, 512)
            dgu[i, :, rows, pl.ds(512, 512)] = grad_up.reshape(4, CAP, 512)
            out = dot(active, down).astype(BF).astype(F32)
            dgate[:, rows, :] = jnp.sum(gx.astype(F32) * out, axis=1, keepdims=True).reshape(4, CAP, 1)
            yb[:, rows, :] = (gate * out).astype(BF).reshape(4, CAP, 1024)


        @pl.when(i > 0)
        def _():
            reduce_second(i - 1).middle(0)
            reduce_second(i - 1).middle(1)

        second(i).wait_sent()

        @pl.when(i == 0)
        def _():
            first.on[0].wait_send()

        @pl.when(i == 2)
        def _():
            first.on[1].wait_send()

        @pl.when(i == 3)
        def _():
            for step in first.go:
                step.wait_send()

        @pl.loop(0, 2)
        def _(e):
            rows = pl.ds(pl.multiple_of(e * CAP, 32), CAP)
            gate_up = jnp.concatenate([wgu[e, n] for n in range(8)], axis=1)
            grad_in = dot(dgu[i, :, rows, :].reshape(4 * CAP, 1024), gate_up, NT)
            dxb[:, rows, :] = grad_in.astype(BF).reshape(4, CAP, 1024)

        @pl.loop(0, 4)
        def _(j):
            buf[base + j, pl.ds(0, ROWS), :] = dot(hot_t[j], dxb[j]).astype(BF)
            spots = hot[j].astype(F32) * dgate[j]
            grad_rows = [jnp.sum(spots[e * CAP : (e + 1) * CAP], axis=0, keepdims=True) for e in range(2)]
            wide = [jnp.concatenate([row] * 4, axis=1) for row in grad_rows]
            mine = jnp.where(low_row == my_low, wide[0], jnp.where(low_row == my_low + 1, wide[1], 0.0))
            mine = jnp.where(my_quarter, mine, 0.0)
            high = mine.astype(BF).astype(F32)
            buf[base + j, pl.ds(ROWS, 16), :] = jnp.concatenate([high, mine - high], axis=0).astype(BF)

        reduce_second(i).start()

        @pl.loop(0, 4)
        def _(j):
            @pl.when(i > 0)
            def _():
                store_y(i - 1, j).wait()

            @pl.when((i > 0) & (j == (me.second + 2) % 4))
            def _():
                for step in far_y(i - 1):
                    step.wait_send()

            ystage[j] = dot(hot_t[j], yb[j]).astype(BF)
            store_y(i, j).start()

        @pl.when(i < 3)
        def _():
            for step in far_y(i):
                step.start()


    for j in range(4):
        store_y(3, j).wait()

    leaving = [None] * 4

    def weight_chunk(number):
        stays, n = number >= 6, number % 6
        expert = me.core if stays else 1 - me.core
        rows = pl.ds(pl.multiple_of(expert * CAP, 32), CAP)
        slot = number % 4
        if leaving[slot] is not None:
            for step in leaving[slot]:
                step()
        if n < 2:
            inner = act[:, :, rows, pl.ds(n * 256, 256)].reshape(16 * CAP, 256)
            outer = gxb[:, :, rows, :].reshape(16 * CAP, 1024)
            parts = [(ystage.at[slot], own_d_out if stays else pair_d_out, n)]
        else:
            n = n - 2
            inner = xb[:, :, rows, pl.ds(n * 256, 256)].reshape(16 * CAP, 256)
            outer = dgu[:, :, rows, :].reshape(16 * CAP, 1024)
            parts = [
                (ystage.at[slot, :, pl.ds(0, 512)], own_g_out if stays else pair_g_out, n),
                (ystage.at[slot, :, pl.ds(512, 512)], own_u_out if stays else pair_u_out, n),
            ]
        ystage[slot] = dot(inner, outer, TN).astype(BF)
        leaving[slot] = []
        for part, (stage, out, n) in enumerate(parts):
            target = out.at[pl.ds(n * 256, 256), :]
            if stays:
                step = pltpu.make_async_copy(stage, target, y_local.at[2 * slot + part])
                leaving[slot].append(step.wait)
            else:
                step = p_wires.copy(stage, target, 2 * number + part, me.sibling())
                leaving[slot].append(step.wait_send)
            step.start()

    for number in range(3):
        weight_chunk(number)
    reduce_first.middle(1)
    reduce_second(3).middle(0)
    reduce_second(3).middle(1)
    reduce_second(2).finish()
    reduce_first.middle(0)
    for number in range(3, 12):
        weight_chunk(number)
    reduce_second(3).finish()
    mine = me.block(0, 0)
    for step in reduce_first.mid:
        step.wait_recv()
    add_into(buf.at[mine], landing_f.at[0], landing_f.at[1])
    result = pltpu.make_async_copy(buf.at[mine], dx_out, local.at[0])
    result.start()
    for steps in leaving:
        for step in steps:
            step()
    for number in range(6):
        outs = (pair_d_out,) if number < 2 else (pair_g_out, pair_u_out)
        for part, out in enumerate(outs):
            here = out.at[pl.ds((number if number < 2 else number - 2) * 256, 256), :]
            p_wires.copy(here, here, 2 * number + part, me.sibling()).wait_recv()
    for step in range(4):
        reduce_second(step).wait_sent()
    reduce_first.wait_sent()
    for step in weights:
        step.wait_sent()
    for i in range(3):
        for step in far_y(i):
            step.wait_recv()
    result.wait()


def expert_stage(*arrays):
    dma = pltpu.SemaphoreType.DMA
    s, v = jax.ShapeDtypeStruct, pltpu.VMEM
    return call(
        expert_kernel,
        (
            s((BLOCK, 1024), BF),
            s((16, ROWS, 1024), BF),
            s((3, ROWS, 1024), BF),
            s((1024, 512), BF),
            s((1024, 512), BF),
            s((512, 1024), BF),
            s((1024, 512), BF),
            s((1024, 512), BF),
            s((512, 1024), BF),
        ),
        [ANY] * 6,
        (ANY,) * 9,
        [
            v((2, 8, 1024, 128), BF),
            v((2, 4, 128, 1024), BF),
            v((32, 1024), BF),
            v((16, BLOCK, 1024), BF),
            v((2, 4, BLOCK, 1024), BF),
            v((4, BLOCK, 1024), BF),
            v((4, 2, BLOCK, 1024), BF),
            v((BLOCK, 1024), BF),
            v((2, BLOCK, 1024), BF),
            v((4, 4, 2 * CAP, 1024), BF),
            v((4, 4, 2 * CAP, 1024), BF),
            v((4, 2 * CAP, 1024), BF),
            v((4, 2 * CAP, 1024), BF),
            v((4, 4, 2 * CAP, 512), BF),
            v((4, 4, 2 * CAP, 1024), BF),
            v((4, 2 * CAP, 256), BF),
            v((4, 256, 2 * CAP), BF),
            v((4, 2 * CAP, 1), F32),
            v((4, 2 * CAP, 1), F32),
            v((4, ROWS, 1024), BF),
            dma((20,)),
            dma((20,)),
            dma((20,)),
            dma((20,)),
            dma((15,)),
            dma((15,)),
            dma((12,)),
            dma((12,)),
            dma((6,)),
            dma((6,)),
            dma((5,)),
            dma((2,)),
            dma((8,)),
        ],
        1,
        vmem=62,
    )(*arrays)


class Sum:
    def __init__(self, me, wires, base, own, pair, part_f, part_x, part_s, part_o, total):
        self.pair, self.part_f, self.part_x, self.part_s, self.part_o = pair, part_f, part_x, part_s, part_o

        def half_of(core):
            return pl.ds(pl.multiple_of(core * HALF, HALF), HALF)

        def cols_of(place):
            return pl.ds(pl.multiple_of(((place + 4) % 4) * 256, 256), 256)

        def there(rows, cols, number, device):
            return wires.copy(total.at[rows, cols], total.at[rows, cols], base + number, device)

        other, first, second = 1 - me.core, me.first, me.second
        kept, steps = half_of(me.core), (1, 2, 3)
        cols = cols_of(first)
        self.kept = own.at[:, kept]
        self.mine_f, self.mine_x = own.at[:, kept, cols], own.at[me.x, kept, cols]
        self.swap = wires.copy(own.at[:, half_of(other), :], pair, base, me.sibling())
        self.out_f = [
            wires.copy(own.at[:, kept, cols_of(first + k)], part_f.at[k - 1], base + k, me.at(k, 0)) for k in steps
        ]
        self.out_x = [
            wires.copy(own.at[(me.x + k) % 4, kept, cols], part_x.at[k - 1], base + 3 + k, me.along_x(k)) for k in steps
        ]
        self.out_s = [wires.copy(part_s.at[0], part_s.at[k], base + 6 + k, me.at(0, k)) for k in steps]
        self.out_s += [wires.copy(part_s.at[0], part_o.at[k], base + 10 + k, me.other_at(0, k)) for k in range(4)]
        self.result, self.result_other = total.at[kept, cols], total.at[half_of(other), cols_of(second)]
        self.back = [there(kept, cols, 13 + k, me.at(k, 0)) for k in steps]
        self.back += [there(kept, cols, 16 + k, me.other_at(k, 0)) for k in steps]
        self.came = [there(kept, cols_of(first - k), 13 + k, me.at(k, 0)) for k in steps]
        self.came += [there(half_of(other), cols_of(second - k), 16 + k, me.at(1, 0)) for k in steps]

    def step(self, number):
        if number == 0:
            self.swap.start()
        elif number == 1:
            self.swap.wait_recv()
            add_into(self.kept, self.pair)
            for copy in self.out_f:
                copy.start()
        elif number == 2:
            for copy in self.out_f:
                copy.wait_recv()
            add_into(self.mine_f, *[self.part_f.at[n] for n in range(3)])
            for copy in self.out_x:
                copy.start()
        elif number == 3:
            for copy in self.out_x:
                copy.wait_recv()
            add_up(self.part_s.at[0], self.mine_x, *[self.part_x.at[n] for n in range(3)])
            for copy in self.out_s:
                copy.start()
        elif number == 4:
            for copy in self.out_s:
                copy.wait_recv()
            add_up(self.result, *[self.part_s.at[n] for n in range(4)])
            add_up(self.result_other, *[self.part_o.at[n] for n in range(4)])
            for copy in self.back:
                copy.start()
        else:
            for copy in self.came:
                copy.wait_recv()

    def wait_sent(self):
        for copy in [self.swap] + self.out_f + self.out_x + self.out_s + self.back:
            copy.wait_send()


class SumByX:
    def __init__(self, me, wires, base, own, pair, near, landing, part_f, part_s, part_o, total):
        self.pair, self.part_f, self.part_s, self.part_o = pair, part_f, part_s, part_o

        def half_of(core):
            return pl.ds(pl.multiple_of(core * HALF, HALF), HALF)

        def cols_of(place):
            return pl.ds(pl.multiple_of(((place + 4) % 4) * 256, 256), 256)

        def there(rows, cols, number, device):
            return wires.copy(total.at[rows, cols], total.at[rows, cols], base + number, device)

        other, first, second = 1 - me.core, me.first, me.second
        kept, steps = half_of(me.core), (1, 2, 3)
        cols = cols_of(first)
        self.kept, self.mine_f = own.at[:, kept], own.at[me.x, kept, cols]
        self.swap = wires.copy(own.at[:, half_of(other), :], pair, base, me.sibling())
        self.ring = ReduceRing(
            wires,
            base + 1,
            lambda k, part: own.at[(me.x + k + 4) % 4, kept].at[part],
            lambda part: near.at[part],
            lambda way: landing.at[way],
            me.along_x(1),
            me.along_x(-1),
            64,
            HALF,
        )
        self.out_f = [
            wires.copy(own.at[me.x, kept, cols_of(first + k)], part_f.at[k - 1], base + 4 + k, me.at(k, 0)) for k in steps
        ]
        self.out_s = [wires.copy(part_s.at[0], part_s.at[k], base + 7 + k, me.at(0, k)) for k in steps]
        self.out_s += [wires.copy(part_s.at[0], part_o.at[k], base + 11 + k, me.other_at(0, k)) for k in range(4)]
        self.result, self.result_other = total.at[kept, cols], total.at[half_of(other), cols_of(second)]
        self.back = [there(kept, cols, 14 + k, me.at(k, 0)) for k in steps]
        self.back += [there(kept, cols, 17 + k, me.other_at(k, 0)) for k in steps]
        self.came = [there(kept, cols_of(first - k), 14 + k, me.at(k, 0)) for k in steps]
        self.came += [there(half_of(other), cols_of(second - k), 17 + k, me.at(1, 0)) for k in steps]

    def step(self, number):
        if number == 0:
            self.swap.start()
        elif number == 1:
            self.swap.wait_recv()
            add_into(self.kept, self.pair)
            self.ring.start()
        elif number == 2:
            self.ring.middle(0)
            self.ring.middle(1)
        elif number == 3:
            self.ring.finish()
            for copy in self.out_f:
                copy.start()
        elif number == 4:
            for copy in self.out_f:
                copy.wait_recv()
            add_up(self.part_s.at[0], self.mine_f, *[self.part_f.at[n] for n in range(3)])
            for copy in self.out_s:
                copy.start()
        elif number == 5:
            for copy in self.out_s:
                copy.wait_recv()
            add_up(self.result, *[self.part_s.at[n] for n in range(4)])
            add_up(self.result_other, *[self.part_o.at[n] for n in range(4)])
            for copy in self.back:
                copy.start()
        else:
            for copy in self.came:
                copy.wait_recv()

    def wait_sent(self):
        self.ring.wait_sent()
        for copy in [self.swap] + self.out_f + self.out_s + self.back:
            copy.wait_send()


LOADED = {
    "summed": ((BLOCK, 1024), BF),
    "h2": ((ROWS, 1024), BF),
    "middle": ((ROWS, 1024), F32),
    "cot": ((ROWS, 1024), BF),
    "tok": ((ROWS, 1024), BF),
    "mixed": ((ROWS, 1024), BF),
    "h1": ((ROWS, 1024), BF),
    "qpre": ((ROWS, 1024), F32),
    "kpre": ((ROWS, 512), F32),
    "qa": ((HEAD_PAIRS, 1024, 256), BF),
    "kv": ((4, ROWS, 1024), BF),
    "wk": ((1024, 512), BF),
    "wv": ((1024, 512), BF),
    "small": ((SMALL, 1024), BF),
    "rope": ((2, ROWS, 128), F32),
    "aug": ((ROWS + 1024, 128), BF),
    "places": ((32, ROWS), F32),
}


def backward_kernel(*refs):
    sources, refs = dict(zip(LOADED, refs)), refs[len(LOADED) :]
    wq, wo, gw, uw, dw, gp, up, dp, y, y_near = refs[:10]
    layer_out, tokens_out, total_out, small_out, g_out, u_out, d_out, y_land = refs[10:18]
    refs = refs[18:]
    held, refs = dict(zip(LOADED, refs)), refs[len(LOADED) :]
    (
        doa,
        dqa,
        dkv,
        wbuf,
        parts,
        pair_w,
        part_f,
        part_x,
        part_s,
        part_o,
        near_w,
        land_w,
        out_part_f,
        out_part_s,
        out_part_o,
        total_w,
        near_k,
        land_k,
        own_g,
        own_u,
        own_d,
        pair_g,
        pair_u,
        pair_d,
        near_g,
        near_u,
        near_d,
        land_g,
        land_u,
        land_d,
        buf,
        y_sum,
        near_y,
        near_last,
        far_block,
        near_f,
        land_f,
        small_part,
        small_pair,
        small_x,
        small_f,
        small_s,
        layer,
        grad_middle,
        small_total,
        final_g,
        final_u,
        final_d,
        e_send,
        e_recv,
        w_send,
        w_recv,
        k_send,
        k_recv,
        y_send,
        y_recv,
        t_send,
        t_recv,
        local,
        fetched,
        leave,
    ) = refs
    summed, h2, middle, cot, tok, mixed, h1, qpre, kpre, qa, kv, wk, wv, small, rope, aug, places = held.values()
    me = Place()
    x, core = me.x, me.core
    right, left, sibling = me.along_x(1), me.along_x(-1), me.sibling()
    planes = [me.at(k, 0) for k in (1, 2, 3)] + [me.at(0, k) for k in (1, 2, 3)] + [me.along_x(k) for k in (1, 2, 3)]
    planes += [me.other_at(0, 0)] + [me.other_at(k, 0) for k in (1, 2, 3)] + [me.other_at(0, k) for k in (1, 2, 3)]
    greet(planes, wait=False)
    e_wires, w_wires, k_wires = Wires(e_send, e_recv), Wires(w_send, w_recv), Wires(k_send, k_recv)
    y_wires, t_wires = Wires(y_send, y_recv), Wires(t_send, t_recv)

    def shard(step):
        return (x + step + 4) % 4

    loads = {
        name: pltpu.make_async_copy(sources[name], held[name], fetched.at[n]) for n, name in enumerate(LOADED)
    }
    pulls = [
        pltpu.make_async_copy(source, target, local.at[n])
        for n, (source, target) in enumerate(
            ((gw, own_g), (uw, own_u), (dw, own_d), (gp, pair_g), (up, pair_u), (dp, pair_d), (wo, wbuf))
        )
    ]
    load_wq = pltpu.make_async_copy(wq, wbuf, local.at[7])

    def place_y(i, k):
        return ((me.first + ORDER[i] + 4) % 4) * 4 + (me.second + k + 4) % 4

    load_sides = [
        pltpu.make_async_copy(y.at[place_y(i, 1 - 2 * way)], buf.at[i, way], local.at[8 + 2 * i + way])
        for i in range(4)
        for way in range(2)
    ]
    load_near = pltpu.make_async_copy(y_near, near_y, local.at[16])
    load_far = pltpu.make_async_copy(y.at[place_y(3, 2)], far_block, local.at[17])
    load_own = [
        pltpu.make_async_copy(y.at[place_y(i, 0)], y_sum.at[(me.first + ORDER[i] + 4) % 4], local.at[18 + i])
        for i in range(4)
    ]

    def ready(*names):
        for name in names:
            loads[name].wait()

    leaving = []

    def store(source, target):
        step = pltpu.make_async_copy(source, target, leave.at[len(leaving)])
        leaving.append(step)
        step.start()

    for name in ("summed", "h2", "small", "places", "middle", "cot"):
        loads[name].start()

    low, high = pl.ds(0, HALF), pl.ds(HALF, HALF)
    s_right, s_left = me.at(0, 1), me.at(0, -1)
    far_y = [
        y_wires.copy(far_block.at[low], near_last.at[low], 4, s_right),
        y_wires.copy(far_block.at[high], near_last.at[high], 5, s_left),
    ]
    mid_y = [
        [
            y_wires.copy(buf.at[i, way], y_land.at[i, way], 6 + 2 * i + way, (s_right, s_left)[way])
            for way in range(2)
        ]
        for i in range(4)
    ]
    load_land = [pltpu.make_async_copy(y_land.at[i], buf.at[i], local.at[8 + i]) for i in range(4)]

    def y_middle(i):
        near = near_last if i == 3 else near_y.at[i]
        add_into(buf.at[i, 0, low], near.at[low])
        add_into(buf.at[i, 1, high], near.at[high])
        for step in mid_y[i]:
            step.start()

    def y_fetch(i):
        for step in mid_y[i]:
            step.wait_recv()
            step.wait_send()
        load_land[i].start()

    def y_finish(i):
        load_land[i].wait()
        add_into(y_sum.at[(me.first + ORDER[i] + 4) % 4], buf.at[i, 0], buf.at[i, 1])

    y_first = ReduceRing(
        y_wires,
        0,
        lambda k, rows: y_sum.at[(me.first + k + 4) % 4, rows],
        lambda rows: near_f.at[rows],
        lambda way: land_f.at[way],
        me.at(1, 0),
        me.at(-1, 0),
        HALF,
        ROWS,
    )
    def weight_sum(n, own):
        return Sum(
            me,
            w_wires,
            20 * n,
            own,
            pair_w.at[n % 2],
            part_f.at[n - 1],
            part_x.at[n - 1],
            part_s.at[n - 1],
            part_o.at[n - 1],
            total_w.at[n],
        )

    out_sum = SumByX(
        me, w_wires, 60, parts.at[0], pair_w.at[0], near_w, land_w, out_part_f, out_part_s, out_part_o, total_w.at[0]
    )
    query_sum, kv_sum = weight_sum(1, parts.at[1]), weight_sum(2, dkv)

    def weight_grad(target, left_rows, right_rows):
        for k in range(4):
            target[k] = dot(left_rows[:, k * ROWS : (k + 1) * ROWS], right_rows, TN).astype(BF)

    def slice_of(k):
        return pl.ds(pl.multiple_of(shard(k) * 128, 128), 128)

    def g_at(k, ref=None):
        return (own_g if ref is None else ref).at[:, slice_of(k)]

    def u_at(k, ref=None):
        return (own_u if ref is None else ref).at[:, slice_of(k)]

    def d_at(k, start=0, size=128, ref=None):
        return (own_d if ref is None else ref).at[pl.ds(pl.multiple_of(shard(k) * 128 + start, 64), size), :]

    e_far = [
        e_wires.copy(g_at(2), near_g, 3, right),
        e_wires.copy(d_at(2, 0, 64), near_d.at[0], 4, right),
        e_wires.copy(u_at(2), near_u, 5, left),
        e_wires.copy(d_at(2, 64, 64), near_d.at[1], 6, left),
    ]
    e_mid = [
        e_wires.copy(ref, land.at[way], 7 + way * 3 + i, device)
        for way, (k, device) in enumerate(((1, right), (-1, left)))
        for i, (ref, land) in enumerate(((g_at(k), land_g), (u_at(k), land_u), (d_at(k), land_d)))
    ]

    def add_pair(k):
        add_into(g_at(k), g_at(k, pair_g))
        add_into(u_at(k), u_at(k, pair_u))
        add_into(d_at(k), d_at(k, ref=pair_d))

    ready("summed", "h2", "small", "places")
    load_far.start()
    for step in pulls[:6]:
        step.start()
    for name in ("mixed", "aug"):
        loads[name].start()
    pulls[6].start()
    params = small[...].astype(F32)
    h2_rows = h2[...]
    numbers = summed[pl.ds(ROWS, 16), :].astype(F32)
    numbers = numbers[0:8] + numbers[8:16]
    grad_gates = jnp.concatenate([numbers[:, q * 256 : (q + 1) * 256] for q in range(4)], axis=0)
    logits = dot(small[pl.ds(ROUTER_ROW, 32), :], h2_rows, NT)
    routed = places[...] >= 0.0
    top = jnp.max(jnp.where(routed, logits, -1e30), axis=0, keepdims=True)
    terms = jnp.where(routed, jnp.exp(jnp.where(routed, logits - top, 0.0)), 0.0)
    gates = terms / jnp.sum(terms, axis=0, keepdims=True)
    grad_logits = gates * (grad_gates - jnp.sum(gates * grad_gates, axis=0, keepdims=True))
    grad_router = split_dot(grad_logits, h2_rows)
    for k in range(4):
        small_part[k, pl.ds(0, 32), :] = grad_router[:, k * ROWS : (k + 1) * ROWS]
        small_part[k, pl.ds(32, 16), :] = jnp.zeros((16, ROWS), F32)
    grad = summed[pl.ds(0, ROWS), :].astype(F32) + split_dot(grad_logits, small[pl.ds(ROUTER_ROW, 32), :], TN)

    def norm_back(v, gain, grad, row):
        scale = lax.rsqrt(jnp.mean(v * v, axis=1, keepdims=True) + EPS)
        normed = v * scale
        gained = gain * grad
        gain_grad = jnp.sum(grad * normed, axis=0, keepdims=True)
        for k in range(4):
            small_part[k, row : row + 1, :] = gain_grad[:, k * ROWS : (k + 1) * ROWS]
        return scale * (gained - normed * jnp.mean(gained * normed, axis=1, keepdims=True))

    ready("middle", "cot", "mixed")
    grad_middle[...] = cot[...].astype(F32) + norm_back(middle[...], params[1:2], grad, 33)
    grad_low = grad_middle[...].astype(BF)
    load_near.start()
    for step in load_sides + load_own:
        step.start()
    for name in ("qa", "kv"):
        loads[name].start()
    wait_for(planes)
    load_far.wait()
    for step in far_y:
        step.start()
    for step in pulls[:6]:
        step.wait()
    add_pair(2)
    for step in e_far:
        step.start()
    weight_grad(parts.at[0], mixed[...], grad_low)
    out_sum.step(0)
    grad_low = grad_middle[...].astype(BF)
    ready("aug")
    live = aug[pl.ds(0, ROWS), 4:5].astype(F32) == 0.0
    pulls[6].wait()
    grad_mixed = jnp.where(live, dot(grad_low, wbuf[...], NT), 0.0).astype(BF).astype(F32)
    row_dots = split_dot(grad_mixed * mixed[...].astype(F32), head_map(1024))
    lane = lanes()
    for j in range(8):
        for n, head in enumerate(split_heads(grad_mixed[:, j * 128 : (j + 1) * 128], j % 2 == 1)):
            start = ((j % 2) * 2 + n) * ROWS
            marks = jnp.zeros((ROWS, 128), F32)
            for m, part in enumerate(three_parts(-row_dots[:, 2 * j + n : 2 * j + n + 1])):
                marks = jnp.where(lane == 5 + m, part, marks)
            doa[j // 2, pl.ds(start, ROWS), pl.ds(0, 128)] = head.astype(BF)
            doa[j // 2, pl.ds(start, ROWS), pl.ds(128, 128)] = marks.astype(BF)

    load_wq.start()
    for step in [load_near] + load_sides + load_own:
        step.wait()
    for i in range(3):
        y_middle(i)
    for name in ("rope", "qpre", "kpre", "h1", "wk", "wv", "tok"):
        loads[name].start()
    ready("qa", "kv")

    def attend(k):
        there = shard(k)
        marks = aug[pl.ds(pl.multiple_of(there * ROWS + ROWS, ROWS), ROWS), :]

        @pl.loop(0, HEAD_PAIRS)
        def _(pair):
            start = pl.multiple_of(pair * 128, 128)
            keys = kv[there, :, pl.ds(start, 128)]
            keyed = jnp.concatenate([keys, marks], axis=1)
            valued = jnp.concatenate([kv[there, :, pl.ds(start + 512, 128)], marks], axis=1)
            p = jnp.exp(dot(qa[pair], keyed, NT))
            ds = (p * dot(doa[pair], valued, NT)).astype(BF)
            dkv[there, :, pl.ds(start + 512, 128)] = dot(p.astype(BF), doa[pair, :, pl.ds(0, 128)], TN).astype(BF)
            dkv[there, :, pl.ds(start, 128)] = dot(ds, qa[pair, :, pl.ds(0, 128)], TN).astype(BF)
            dq = dot(ds, keys)
            if k == 2:
                dqa[pair] = dq
            else:
                dqa[pair] += dq

    kv_ring = ReduceRing(
        k_wires,
        0,
        lambda k, rows: dkv.at[shard(k), rows],
        lambda rows: near_k.at[rows],
        lambda way: land_k.at[way],
        right,
        left,
        HALF,
        ROWS,
    )
    attend(2)
    kv_ring.start()
    out_sum.step(1)
    attend(1)
    for step in far_y:
        step.wait_recv()
    y_middle(3)
    attend(-1)
    kv_ring.middle(0)
    kv_ring.middle(1)
    attend(0)

    def heads_back(pre, grads, gain, count):
        heads = head_map(count)
        scale = head_scale(pre, heads)
        normed = pre * scale
        gained = gain * grads
        mean = split_dot(split_dot(gained * normed, heads) * (1.0 / 64), heads, NT)
        gain_grad = jnp.sum(grads * normed, axis=0, keepdims=True)
        folded = sum(gain_grad[:, j * 128 : (j + 1) * 128] for j in range(count // 128))
        return scale * (gained - normed * mean), folded + pltpu.roll(folded, 64, 1)

    ready("rope", "qpre", "h1")
    blocks = []
    for j in range(8):
        pair, odd = j // 2, j % 2 == 1
        heads = [dqa[pair, pl.ds(((j % 2) * 2 + n) * ROWS, ROWS), :] for n in range(2)]
        blocks.append(turn(join_heads(heads[0], heads[1], odd) * 0.125, rope[0], -rope[1]))
    query_grad, query_gain_grad = heads_back(qpre[...], jnp.concatenate(blocks, axis=1), params[2:3], 1024)
    query_low = query_grad.astype(BF)
    weight_grad(parts.at[1], h1[...], query_low)
    query_sum.step(0)
    for k in (1, -1, 0):
        add_pair(k)
    e_far[0].wait_recv()
    add_into(g_at(1), near_g)
    e_far[1].wait_recv()
    add_into(d_at(1, 0, 64), near_d.at[0])
    e_far[2].wait_recv()
    add_into(u_at(-1), near_u)
    e_far[3].wait_recv()
    add_into(d_at(-1, 64, 64), near_d.at[1])
    query_sum.step(1)
    y_fetch(1)
    load_wq.wait()
    grad_h1 = dot(query_low, wbuf[...], NT)
    ready("kpre")
    y_finish(1)
    y_first.start()

    kv_ring.finish()
    out_sum.step(2)
    own_kv = dkv[x].astype(F32)
    blocks = [turn(own_kv[:, j * 128 : (j + 1) * 128], rope[0], -rope[1]) for j in range(4)]
    key_grad, key_gain_grad = heads_back(kpre[...], jnp.concatenate(blocks, axis=1), params[3:4, 0:512], 512)
    low = jnp.concatenate([key_grad.astype(BF), own_kv[:, 512:1024].astype(BF)], axis=1)
    kv_ring.wait_sent()
    weight_grad(dkv, h1[...], low)
    kv_sum.step(0)
    ready("wk", "wv", "tok")
    grad_h1 = grad_h1 + dot(low[:, 0:512], wk[...], NT) + dot(low[:, 512:1024], wv[...], NT)
    grad_middle[...] += norm_back(tok[...].astype(F32), params[0:1], grad_h1, 32)
    store(grad_middle, tokens_out)
    for k in range(4):
        for row, folded in ((34, query_gain_grad), (35, key_gain_grad)):
            small_part[k, row : row + 1, pl.ds(0, 128)] = pltpu.roll(folded, (128 - 16 * k) % 128, 1)

    t_pair = t_wires.copy(small_part, small_pair, 0, sibling)
    t_pair.start()
    kv_sum.step(1)
    y_fetch(0)
    y_fetch(2)
    y_finish(0)
    y_finish(2)
    query_sum.step(2)
    y_first.middle_both()
    y_fetch(3)
    t_pair.wait_recv()
    t_x = [t_wires.copy(small_part.at[shard(k)], small_x.at[k - 1], k, me.along_x(k)) for k in (1, 2, 3)]
    t_pair.wait_send()
    for k in range(4):
        small_part[k] += small_pair[k]
    for step in t_x:
        step.start()
    y_finish(3)
    query_sum.step(3)
    out_sum.step(3)
    kv_sum.step(2)
    for step in e_mid:
        step.start()
    kv_sum.step(3)
    query_sum.step(4)
    for step in t_x:
        step.wait_recv()
    small_f[0] = small_part[x] + small_x[0] + small_x[1] + small_x[2]
    t_f = [t_wires.copy(small_f.at[0], small_f.at[k], 3 + k, me.at(k, 0)) for k in (1, 2, 3)]
    for step in t_f:
        step.start()
    kv_sum.step(4)
    out_sum.step(4)
    y_first.finish()
    layer[...] = (middle[...] + y_sum[me.first].astype(F32)).astype(BF)
    store(layer, layer_out)
    for step in t_f:
        step.wait_recv()
    small_s[0] = small_f[0] + small_f[1] + small_f[2] + small_f[3]
    t_s = [t_wires.copy(small_s.at[0], small_s.at[k], 6 + k, me.at(0, k)) for k in (1, 2, 3)]
    for step in t_s:
        step.start()
    kv_sum.step(5)
    store(total_w.at[2], total_out.at[2])
    out_sum.step(5)
    query_sum.step(5)
    store(total_w.at[1], total_out.at[1])
    for step in e_mid:
        step.wait_recv()
    for out, at, land, target in (
        (final_g, g_at, land_g, g_out),
        (final_u, u_at, land_u, u_out),
        (final_d, d_at, land_d, d_out),
    ):
        add_up(out, at(0), land.at[0], land.at[1])
        store(out, target)
    out_sum.step(6)
    store(total_w.at[0], total_out.at[0])
    for step in t_s:
        step.wait_recv()
    small_total[...] = small_s[0] + small_s[1] + small_s[2] + small_s[3]
    store(small_total, small_out)
    for step in e_far + e_mid + t_x + t_f + t_s + far_y:
        step.wait_send()
    for ring in [y_first, out_sum, query_sum, kv_sum]:
        ring.wait_sent()
    for step in leaving:
        step.wait()


def backward_stage(*arrays):
    dma = pltpu.SemaphoreType.DMA
    s, v = jax.ShapeDtypeStruct, pltpu.VMEM
    return call(
        backward_kernel,
        (
            s((ROWS, 1024), BF),
            s((ROWS, 1024), F32),
            s((3, ROWS, 1024), BF),
            s((SMALL, ROWS), F32),
            s((1024, 128), F32),
            s((1024, 128), F32),
            s((128, 1024), F32),
            s((4, 2, ROWS, 1024), BF),
        ),
        [ANY] * (len(LOADED) + 10),
        (ANY,) * 8,
        [v(*one) for one in LOADED.values()]
        + [
            v((HEAD_PAIRS, 1024, 256), BF),
            v((HEAD_PAIRS, 1024, 128), F32),
            v((4, ROWS, 1024), BF),
            v((1024, 1024), BF),
            v((2, 4, ROWS, 1024), BF),
            v((2, 4, HALF, 1024), BF),
            v((2, 3, 4, HALF, 256), BF),
            v((2, 3, HALF, 256), BF),
            v((2, 4, HALF, 256), BF),
            v((2, 4, HALF, 256), BF),
            v((HALF, 1024), BF),
            v((2, HALF, 1024), BF),
            v((3, HALF, 256), BF),
            v((4, HALF, 256), BF),
            v((4, HALF, 256), BF),
            v((3, ROWS, 1024), BF),
            v((ROWS, 1024), BF),
            v((2, ROWS, 1024), BF),
            v((1024, 512), BF),
            v((1024, 512), BF),
            v((512, 1024), BF),
            v((1024, 512), BF),
            v((1024, 512), BF),
            v((512, 1024), BF),
            v((1024, 128), BF),
            v((1024, 128), BF),
            v((2, 64, 1024), BF),
            v((2, 1024, 128), BF),
            v((2, 1024, 128), BF),
            v((2, 128, 1024), BF),
            v((4, 2, ROWS, 1024), BF),
            v((4, ROWS, 1024), BF),
            v((3, ROWS, 1024), BF),
            v((ROWS, 1024), BF),
            v((ROWS, 1024), BF),
            v((ROWS, 1024), BF),
            v((2, ROWS, 1024), BF),
            v((4, SMALL, ROWS), F32),
            v((4, SMALL, ROWS), F32),
            v((3, SMALL, ROWS), F32),
            v((4, SMALL, ROWS), F32),
            v((4, SMALL, ROWS), F32),
            v((ROWS, 1024), BF),
            v((ROWS, 1024), F32),
            v((SMALL, ROWS), F32),
            v((1024, 128), F32),
            v((1024, 128), F32),
            v((128, 1024), F32),
            dma((13,)),
            dma((13,)),
            dma((81,)),
            dma((81,)),
            dma((4,)),
            dma((4,)),
            dma((14,)),
            dma((14,)),
            dma((10,)),
            dma((10,)),
            dma((22,)),
            dma((len(LOADED),)),
            dma((9,)),
        ],
        2,
        vmem=63,
    )(*arrays)


def last_kernel(layer, tokens, totals, small, g, u, d, *rest):
    outs, (layer_v, tokens_v, totals_v, small_v, g_v, u_v, d_v), held, sem = rest[:14], rest[14:21], rest[21:25], rest[25]
    sources = (totals, small, tokens, layer, g, u, d)
    inside = (totals_v, small_v, tokens_v, layer_v, g_v, u_v, d_v)
    loads = [pltpu.make_async_copy(source, inner, sem.at[n]) for n, (source, inner) in enumerate(zip(sources, inside))]
    for step in loads:
        step.start()
    layer_out, tokens_out, g_out, u_out, d_out, wq, wk, wv, wo, first, second, head_q, head_k, router = outs
    wq_v, wk_v, wv_v, wo_v = held
    stores = []

    def store(source, target):
        step = pltpu.make_async_copy(source, target, sem.at[7 + len(stores)])
        stores.append(step)
        step.start()

    loads[0].wait()
    wq_v[...] = totals_v[1].astype(F32)
    store(wq_v, wq)
    wo_v[...] = totals_v[0].astype(F32)
    store(wo_v, wo)
    wk_v[...] = totals_v[2, :, pl.ds(0, 512)].astype(F32)
    store(wk_v, wk)
    wv_v[...] = totals_v[2, :, pl.ds(512, 512)].astype(F32)
    store(wv_v, wv)
    loads[1].wait()
    first[...] = small_v[32:33, :]
    second[...] = small_v[33:34, :]
    head_q[...] = small_v[34:35, 0:16]
    head_k[...] = small_v[35:36, 0:16]
    router[...] = small_v[0:32, :]
    for step, inner, target in zip(loads[2:], inside[2:], (tokens_out, layer_out, g_out, u_out, d_out)):
        step.wait()
        store(inner, target)
    for step in stores:
        step.wait()


def last_stage(*arrays):
    s, v = jax.ShapeDtypeStruct, pltpu.VMEM
    return pl.pallas_call(
        last_kernel,
        out_shape=(
            s((ROWS, 1024), BF),
            s((ROWS, 1024), F32),
            s((1024, 128), F32),
            s((1024, 128), F32),
            s((128, 1024), F32),
            s((ROWS, 1024), F32),
            s((ROWS, 512), F32),
            s((ROWS, 512), F32),
            s((ROWS, 1024), F32),
            s((1, ROWS), F32),
            s((1, ROWS), F32),
            s((1, 16), F32),
            s((1, 16), F32),
            s((32, ROWS), F32),
        ),
        in_specs=[ANY] * 7,
        out_specs=(ANY,) * 9 + (VMEM,) * 5,
        scratch_shapes=[
            v((ROWS, 1024), BF),
            v((ROWS, 1024), F32),
            v((3, ROWS, 1024), BF),
            v((SMALL, ROWS), F32),
            v((1024, 128), F32),
            v((1024, 128), F32),
            v((128, 1024), F32),
            v((ROWS, 1024), F32),
            v((ROWS, 512), F32),
            v((ROWS, 512), F32),
            v((ROWS, 1024), F32),
            pltpu.SemaphoreType.DMA((16,)),
        ],
        compiler_params=pltpu.CompilerParams(vmem_limit_bytes=62 * MIB),
    )(*arrays)


def body(
    tokens,
    lengths,
    routes,
    norm1_gain,
    w_query,
    w_key,
    w_value,
    query_gain,
    key_gain,
    w_out,
    norm2_gain,
    w_router,
    w_gate,
    w_up,
    w_down,
    cotangent,
):
    frequency = (ROPE_BASE ** -((np.arange(128) % 32) / 32.0)).astype(np.float32)[None]
    gains = jnp.concatenate(
        [norm1_gain, norm2_gain, jnp.pad(query_gain, (0, ROWS - 16)), jnp.pad(key_gain, (0, ROWS - 16))]
    ).reshape(4, ROWS)
    (h2, middle, mixed, h1, qpre, kpre, qa, kv, wq, wk, wv, wo, small, rope, aug, places, g_all) = attention_forward(
        tokens,
        routes.T,
        lengths,
        gains,
        w_router.T,
        jnp.asarray(frequency),
        w_key,
        w_value,
        w_query,
        w_out,
        cotangent,
    )
    summed, y_part, y_near, *expert_grads = expert_stage(
        h2, g_all, small, w_gate[0], w_up[0], w_down[0]
    )
    results = backward_stage(
        summed,
        h2,
        middle,
        cotangent,
        tokens,
        mixed,
        h1,
        qpre,
        kpre,
        qa,
        kv,
        wk,
        wv,
        small,
        rope,
        aug,
        places,
        wq,
        wo,
        *expert_grads,
        y_part,
        y_near,
    )
    layer, tokens_grad, gate_grad, up_grad, down_grad, wq_g, wk_g, wv_g, wo_g, first, second, head_q, head_k, router = last_stage(
        *results[:7]
    )
    return (
        layer,
        tokens_grad,
        first[0],
        wq_g,
        wk_g,
        wv_g,
        head_q[0],
        head_k[0],
        wo_g,
        second[0],
        router.T,
        gate_grad[None],
        up_grad[None],
        down_grad[None],
    )


def solution(mesh):
    rows = P(("expert", "shard"), None)
    by_shard = P("shard", None)
    columns = P("expert", None, "shard")
    placed = (
        rows,
        P("expert", None),
        rows,
        P("shard"),
        by_shard,
        by_shard,
        by_shard,
        P("shard"),
        P("shard"),
        by_shard,
        P("shard"),
        by_shard,
        columns,
        columns,
        P("expert", "shard", None),
        rows,
    )
    return jax.shard_map(
        body,
        mesh=mesh,
        in_specs=placed,
        out_specs=(
            rows,
            rows,
            P("shard"),
            by_shard,
            by_shard,
            by_shard,
            P("shard"),
            P("shard"),
            by_shard,
            P("shard"),
            by_shard,
            columns,
            columns,
            P("expert", "shard", None),
        ),
        check_vma=False,
    )
```

```python
import math

import jax
import jax.numpy as jnp
import numpy as np
from jax import lax
from jax.experimental import pallas as pl
from jax.experimental.pallas import tpu as pltpu
from jax.sharding import PartitionSpec as P

CAP = 96
EPS = 1e-06
ROPE_BASE = 10000.0
BF = jnp.bfloat16
F32 = jnp.float32
MESH = pl.DeviceIdType.MESH
ANY = pl.BlockSpec(memory_space=pl.ANY)
VMEM = pl.BlockSpec(memory_space=pltpu.VMEM)
MIB = 1 << 20
W_COLS = 3328
W_HALF = W_COLS // 2
ROWS = 256
BLOCK = 272
HALF = 128


class Place:
    def __init__(self):
        self.expert = lax.axis_index("expert")
        self.x = lax.axis_index("shard")
        self.core = self.expert % 2
        self.chip = self.expert // 2
        y, z = self.chip % 4, self.chip // 4
        self.first = z + self.core * (y - z)
        self.second = y + self.core * (z - y)
        self.first_stride = 8 - 6 * self.core
        self.second_stride = 2 + 6 * self.core

    def block(self, first, second):
        return ((self.first + first + 4) % 4) * 4 + (self.second + second + 4) % 4

    def at(self, first, second):
        near = ((self.first + first + 4) % 4) * self.first_stride
        return {"expert": near + ((self.second + second + 4) % 4) * self.second_stride + self.core}

    def other_at(self, first, second):
        there = self.at(first, second)["expert"]
        return {"expert": there + 1 - 2 * self.core}

    def along_x(self, step):
        return {"shard": (self.x + step + 4) % 4}

    def sibling(self):
        return {"expert": self.expert + 1 - 2 * self.core}


def greet(devices, wait=True):
    barrier = pltpu.get_barrier_semaphore()
    for device in devices:
        pl.semaphore_signal(barrier, inc=1, device_id=device, device_id_type=MESH)
    if wait:
        wait_for(devices)


def wait_for(devices):
    pl.semaphore_wait(pltpu.get_barrier_semaphore(), len(devices))


class Copy:
    def __init__(self, *parts):
        self.parts = parts

    def made(self):
        return pltpu.make_async_remote_copy(*self.parts, device_id_type=MESH)

    def start(self):
        self.made().start()

    def wait_send(self):
        self.made().wait_send()

    def wait_recv(self):
        self.made().wait_recv()


class Wires:
    def __init__(self, send, recv):
        self.send, self.recv = send, recv

    def copy(self, source, target, number, device):
        return Copy(source, target, self.send.at[number], self.recv.at[number], device)


class GatherRing:
    def __init__(self, wires, base, at, own, right, left, half, rows):
        low, high, full = pl.ds(0, half), pl.ds(half, rows - half), pl.ds(0, rows)
        copy = wires.copy
        self.go = [copy(own, at(0, full), base, right), copy(own, at(0, full), base + 1, left)]
        self.came = [copy(at(-1, full), at(-1, full), base, right), copy(at(1, full), at(1, full), base + 1, left)]
        self.on = [copy(at(-1, low), at(-1, low), base + 2, right), copy(at(1, high), at(1, high), base + 3, left)]
        self.far = [copy(at(2, low), at(2, low), base + 2, right), copy(at(2, high), at(2, high), base + 3, left)]

    def start(self):
        for step in self.go:
            step.start()

    def forward(self, way):
        self.came[way].wait_recv()
        self.on[way].start()

    def wait_far(self):
        for step in self.far:
            step.wait_recv()

    def wait_sent(self):
        for step in self.go + self.on:
            step.wait_send()


class ReduceRing:
    def __init__(self, wires, base, at, near, landing, right, left, half, rows):
        low, high, full = pl.ds(0, half), pl.ds(half, rows - half), pl.ds(0, rows)
        copy = wires.copy
        self.at, self.near, self.landing = at, near, landing
        self.parts = [low, high, full]
        self.far = [copy(at(2, low), near(low), base, right), copy(at(2, high), near(high), base + 1, left)]
        self.mid = [copy(at(1, full), landing(0), base + 2, right), copy(at(-1, full), landing(1), base + 3, left)]

    def start(self):
        for step in self.far:
            step.start()

    def middle(self, way):
        self.far[way].wait_recv()
        side = 1 - 2 * way
        add_into(self.at(side, self.parts[way]), self.near(self.parts[way]))
        self.mid[way].start()

    def middle_both(self):
        for way in range(2):
            self.far[way].wait_recv()
        for way in range(2):
            add_into(self.at(1 - 2 * way, self.parts[way]), self.near(self.parts[way]))
        for way in range(2):
            self.mid[way].start()

    def finish(self, target=None):
        for step in self.mid:
            step.wait_recv()
        own = self.at(0, self.parts[2])
        if target is None:
            add_into(own, self.landing(0), self.landing(1))
        else:
            add_up(target, own, self.landing(0), self.landing(1))

    def wait_sent(self):
        for step in self.far + self.mid:
            step.wait_send()


def add_up(target, *terms):
    if len(target.shape) == 3:
        for k in range(target.shape[0]):
            add_up(target.at[k], *[term.at[k] for term in terms])
        return
    rows, columns = target.shape
    size = min(rows, 16 * max(1, 1024 // columns))

    @pl.loop(0, rows // size)
    def _(i):
        here = pl.ds(pl.multiple_of(i * size, 16), size)
        total = terms[0][here, :].astype(F32)
        for term in terms[1:]:
            total = total + term[here, :].astype(F32)
        target[here, :] = total.astype(target.dtype)


def add_into(target, *terms):
    add_up(target, target, *terms)


def dot(a, b, contract=((1,), (0,))):
    return lax.dot_general(a, b, (contract, ((), ())), preferred_element_type=F32)


NT = ((1,), (1,))
TN = ((0,), (0,))


def call(kernel, out_shape, in_specs, out_specs, scratch, ident, vmem=56):
    return pl.pallas_call(
        kernel,
        out_shape=out_shape,
        in_specs=in_specs,
        out_specs=out_specs,
        scratch_shapes=scratch,
        compiler_params=pltpu.CompilerParams(
            collective_id=ident, has_side_effects=True, vmem_limit_bytes=vmem * MIB
        ),
    )


HEAD_PAIRS = 4
NORM_ROW, QUERY_ROW = 0, 2
ROUTER_ROW = 16
SMALL = 48


def lanes(rows=ROWS, columns=128):
    return lax.broadcasted_iota(jnp.int32, (rows, columns), 1)


def head_map(columns):
    column = lax.broadcasted_iota(jnp.int32, (columns, 128), 0) // 64
    return (column == lax.broadcasted_iota(jnp.int32, (columns, 128), 1)).astype(F32).astype(BF)


def split_dot(a, exact, contract=((1,), (0,))):
    high = a.astype(BF)
    low = (a - high.astype(F32)).astype(BF)
    return dot(high, exact, contract) + dot(low, exact, contract)


def head_scale(v, heads):
    mean = split_dot(v * v, heads) * (1.0 / 64)
    return split_dot(lax.rsqrt(mean + EPS), heads, NT)


def turn(v, cosine, sine):
    lower = lanes() % 64 < 32
    swapped = jnp.where(lower, pltpu.roll(v, 96, 1), pltpu.roll(v, 32, 1))
    return v * cosine + swapped * sine


def split_heads(block, odd):
    keep = lanes() >= 64 if odd else lanes() < 64
    rolled = pltpu.roll(block, 64, 1)
    first, second = (rolled, block) if odd else (block, rolled)
    return jnp.where(keep, first, 0.0), jnp.where(keep, second, 0.0)


def join_heads(first, second, odd):
    low = pltpu.roll(first, 64, 1) if odd else first
    high = second if odd else pltpu.roll(second, 64, 1)
    return jnp.where(lanes() < 64, low, high)


def three_parts(v):
    high = v.astype(BF).astype(F32)
    middle = (v - high).astype(BF).astype(F32)
    return high, middle, v - high - middle


def passed_documents(lengths, rows, first):
    position = (lax.broadcasted_iota(jnp.int32, (rows, 128), 0) + first).astype(F32)
    end = jnp.zeros((1, 1), F32)
    number, start = jnp.zeros((rows, 128), F32), jnp.zeros((rows, 128), F32)
    for d in range(4):
        length = lengths[:, d : d + 1]
        end = end + length
        number = number + jnp.where(position >= end, 1.0, 0.0)
        start = start + jnp.where(position >= end, length, 0.0)
    return number, position - start


def attention_kernel(
    tok,
    routes,
    lengths,
    gains,
    router,
    frequency,
    wk_in,
    wv_in,
    wq_in,
    wo_in,
    g,
    h2_out,
    middle_out,
    mixed_out,
    h1_out,
    qpre_out,
    kpre_out,
    qa_out,
    kv_out,
    wq_out,
    wk_out,
    wv_out,
    wo_out,
    small_out,
    rope_out,
    aug_out,
    places_out,
    g_all,
    small,
    small_all,
    g_own,
    total,
    h2,
    middle,
    mixed,
    h1,
    qpre,
    kpre,
    qa,
    kv,
    wq,
    wk,
    wv,
    wo,
    params_low,
    rope,
    aug,
    places,
    local,
    leave,
    w_send,
    w_recv,
    k_send,
    k_recv,
    g_send,
    g_recv,
):
    me = Place()
    x, core = me.x, me.core
    right, left, sibling = me.along_x(1), me.along_x(-1), me.sibling()
    partners = [right, left, sibling, me.at(1, 0), me.at(-1, 0), me.at(0, 1), me.at(0, -1)]
    greet(partners, wait=False)
    w_wires, k_wires, g_wires = Wires(w_send, w_recv), Wires(k_send, k_recv), Wires(g_send, g_recv)

    def shard(step):
        return (x + step + 4) % 4

    leaving = []

    def store(source, target):
        step = pltpu.make_async_copy(source, target, leave.at[len(leaving)])
        leaving.append(step)
        step.start()

    load_g = pltpu.make_async_copy(g, g_own.at[pl.ds(0, ROWS)], local.at[4])
    load_g.start()
    row = lax.broadcasted_iota(jnp.int32, (16, ROWS), 0)
    source = lax.broadcasted_iota(jnp.int32, (128, ROWS), 0)
    column = lanes(128, ROWS)
    spread = ((column % 16 == source) & ((column % 64) // 16 == x)).astype(F32).astype(BF)

    def tiled(gain):
        return dot(jnp.broadcast_to(gain, (16, 128)), spread)[0:1]

    block = jnp.zeros((16, ROWS), F32)
    parts = (gains[0:1, :].astype(F32), gains[1:2, :].astype(F32), tiled(gains[2:3, 0:128]), tiled(gains[3:4, 0:128]))
    for n, part in enumerate(parts):
        block = jnp.where(row == n, part, block)
    small[pl.ds(0, 16), :] = block.astype(BF)
    small[pl.ds(16, 32), :] = router[...]

    expert = lax.broadcasted_iota(jnp.int32, (32, ROWS), 0)
    hits = sum(jnp.where(routes[k : k + 1, :] == expert, 1.0, 0.0) for k in range(8))
    before = (lax.broadcasted_iota(jnp.int32, (ROWS, ROWS), 0) < lanes(ROWS, ROWS)).astype(F32).astype(BF)
    places[...] = jnp.where(hits > 0.0, dot(hits.astype(BF), before), -1.0)
    packed = jnp.concatenate([places[q * 8 : (q + 1) * 8] for q in range(4)], axis=1)
    g_own[pl.ds(ROWS, 16), :] = jnp.concatenate([packed, jnp.zeros((8, 1024), F32)], axis=0).astype(BF)
    load_g.wait()
    wait_for(partners)
    small_ring = GatherRing(w_wires, 0, lambda k, rows: small_all.at[shard(k), rows], small, right, left, 32, SMALL)
    small_ring.start()

    class Weight:
        def __init__(self, source, target, base):
            def at(k, rows, half):
                start = pl.multiple_of(shard(k) * ROWS + half * HALF + rows.start, 64)
                return target.at[pl.ds(start, rows.size), :]

            own = source.at[pl.ds(pl.multiple_of(core * HALF, HALF), HALF), :]
            full = pl.ds(0, HALF)
            self.ring = GatherRing(w_wires, base, lambda k, rows: at(k, rows, core), own, right, left, 64, HALF)
            self.pass_on = [
                w_wires.copy(at(k, full, core), at(k, full, core), base + 4 + n, sibling) for n, k in enumerate((-1, 1, 2))
            ]
            self.passed = [
                w_wires.copy(at(k, full, 1 - core), at(k, full, 1 - core), base + 4 + n, sibling)
                for n, k in enumerate((-1, 1, 2))
            ]
            self.keep = pltpu.make_async_copy(
                source, target.at[pl.ds(pl.multiple_of(x * ROWS, ROWS), ROWS), :], local.at[base // 7]
            )

        def start(self):
            self.ring.start()

        def forward(self):
            for way in range(2):
                self.ring.forward(way)
                self.pass_on[way].start()

        def finish(self):
            self.ring.wait_far()
            self.pass_on[2].start()

        def ready(self):
            for step in self.passed:
                step.wait_recv()

        def wait_sent(self):
            self.ring.wait_sent()
            for step in self.pass_on:
                step.wait_send()

    key_weight, value_weight = Weight(wk_in, wk, 4), Weight(wv_in, wv, 11)
    query_weight, out_weight = Weight(wq_in, wq, 18), Weight(wo_in, wo, 25)
    weights = [key_weight, value_weight, query_weight, out_weight]
    key_weight.start()
    value_weight.start()
    query_weight.keep.start()
    out_weight.keep.start()

    def g_at(fo):
        return lambda k, rows: g_all.at[me.block(fo, k), rows]

    first = GatherRing(
        g_wires, 0, lambda k, rows: g_all.at[me.block(k, 0), rows], g_own, me.at(1, 0), me.at(-1, 0), HALF, BLOCK
    )
    seconds = [
        GatherRing(
            g_wires,
            4 + 4 * i,
            g_at(fo),
            g_own if fo == 0 else g_all.at[me.block(fo, 0)],
            me.at(0, 1),
            me.at(0, -1),
            HALF,
            BLOCK,
        )
        for i, fo in enumerate((-1, 1, 2, 0))
    ]
    first.start()
    own_copies = [
        pltpu.make_async_copy(g_own, g_all.at[me.block(0, 0)], local.at[4]),
        pltpu.make_async_copy(small, small_all.at[x], local.at[5]),
        key_weight.keep,
        value_weight.keep,
    ]
    for step in own_copies:
        step.start()

    ends = lengths[...].astype(F32)
    doc, since = passed_documents(ends, ROWS, x * ROWS)
    lane = lanes()
    aug[pl.ds(0, ROWS), :] = jnp.where(
        lane.astype(F32) == doc, 16.0, jnp.where(lane == 8, -128.0, 0.0)
    ).astype(BF)
    angles = since * frequency[...]
    rope[0] = jnp.cos(angles)
    sine_table = jnp.sin(angles)
    rope[1] = jnp.where(lane % 64 < 32, -sine_table, sine_table)
    doc = passed_documents(ends, 1024, 0)[0]
    lane = lanes(1024)
    aug[pl.ds(ROWS, 1024), :] = jnp.where(
        lane.astype(F32) == doc, 8.0, jnp.where((lane >= 5) & (lane < 9), 1.0, 0.0)
    ).astype(BF)
    store(rope, rope_out)
    store(aug, aug_out)
    store(places, places_out)
    tokens = tok[...].astype(F32)
    tokens = tokens * lax.rsqrt(jnp.mean(tokens * tokens, axis=1, keepdims=True) + EPS)

    for way in range(2):
        small_ring.forward(way)
    key_weight.forward()
    value_weight.forward()
    query_weight.start()
    first.forward(0)
    first.forward(1)
    seconds[3].start()
    seconds[0].start()
    seconds[1].start()
    small_ring.wait_far()
    own_copies[1].wait()
    shares = [small_all[k].astype(F32) for k in range(4)]
    params = jnp.concatenate(shares, axis=1)
    by_head = jnp.concatenate([shares[0] + shares[1] + shares[2] + shares[3]] * 4, axis=1)
    row = lax.broadcasted_iota(jnp.int32, (SMALL, 1024), 0)
    params = jnp.where((row == 2) | (row == 3), by_head, params)
    params_low[...] = params.astype(BF)
    store(params_low, small_out)
    h1[...] = (tokens * params[0:1]).astype(BF)
    store(h1, h1_out)
    key_weight.finish()
    value_weight.finish()
    key_weight.ready()
    key_weight.keep.wait()
    kpre[...] = dot(h1[...], wk[...])
    value_weight.ready()
    value_weight.keep.wait()
    kv[x, :, pl.ds(512, 512)] = dot(h1[...], wv[...]).astype(BF)
    keys = kpre[...]
    keys = keys * head_scale(keys, head_map(512)) * params[3:4, 0:512]
    for j in range(4):
        block = keys[:, j * 128 : (j + 1) * 128]
        kv[x, :, pl.ds(j * 128, 128)] = turn(block, rope[0], rope[1]).astype(BF)
    kv_ring = GatherRing(k_wires, 0, lambda k, rows: kv.at[shard(k), rows], kv.at[x], right, left, HALF, ROWS)
    query_weight.forward()
    kv_ring.start()
    store(kpre, kpre_out)
    store(wk, wk_out)
    store(wv, wv_out)
    first.wait_far()
    seconds[2].start()
    query_weight.finish()
    query_weight.ready()
    query_weight.keep.wait()
    qpre[...] = dot(h1[...], wq[...])
    store(qpre, qpre_out)
    store(wq, wq_out)
    queries = qpre[...]
    queries = queries * head_scale(queries, head_map(1024)) * params[2:3]
    for j in range(8):
        block = turn(queries[:, j * 128 : (j + 1) * 128], rope[0], rope[1]) * 0.125
        for n, head in enumerate(split_heads(block, j % 2 == 1)):
            start = ((j % 2) * 2 + n) * ROWS
            qa[j // 2, pl.ds(start, ROWS), pl.ds(0, 128)] = head.astype(BF)
            qa[j // 2, pl.ds(start, ROWS), pl.ds(128, 128)] = aug[pl.ds(0, ROWS), :]

    def attend(k):
        there = shard(k)
        marks = aug[pl.ds(pl.multiple_of(there * ROWS + ROWS, ROWS), ROWS), :]

        @pl.loop(0, HEAD_PAIRS)
        def _(pair):
            start = pl.multiple_of(pair * 128, 128)
            keyed = jnp.concatenate([kv[there, :, pl.ds(start, 128)], marks], axis=1)
            valued = jnp.concatenate([kv[there, :, pl.ds(start + 512, 128)], marks], axis=1)
            p = jnp.exp(dot(qa[pair], keyed, NT)).astype(BF)
            weighted = dot(p, valued)
            if k == 0:
                total[pair] = weighted
            else:
                total[pair] += weighted

    attend(0)
    kv_ring.forward(0)
    kv_ring.forward(1)
    out_weight.start()
    seconds[3].forward(0)
    seconds[3].forward(1)
    attend(-1)
    attend(1)
    for ring in seconds[0:2]:
        ring.forward(0)
        ring.forward(1)
    kv_ring.wait_far()
    attend(2)
    store(kv, kv_out)
    out_weight.forward()
    seconds[2].forward(0)
    seconds[2].forward(1)

    live = aug[pl.ds(0, ROWS), 4:5].astype(F32) == 0.0
    lane = lanes(1024)

    @pl.loop(0, HEAD_PAIRS)
    def _(pair):
        weighted = total[pair]
        mass = weighted[:, 133:134]
        heads = weighted[:, 0:128] / mass
        parts = three_parts(-jnp.log(mass))
        marks = qa[pair, :, pl.ds(128, 128)].astype(F32)
        for n, part in enumerate(parts):
            marks = jnp.where(lane == 5 + n, part, marks)
        qa[pair, :, pl.ds(128, 128)] = marks.astype(BF)
        heads = [heads[n * ROWS : (n + 1) * ROWS] for n in range(4)]
        for odd in range(2):
            joined = join_heads(heads[2 * odd], heads[2 * odd + 1], odd == 1)
            start = pl.multiple_of(pair * 256 + odd * 128, 128)
            mixed[:, pl.ds(start, 128)] = jnp.where(live, joined, 0.0).astype(BF)

    store(qa, qa_out)
    store(mixed, mixed_out)
    out_weight.finish()
    out_weight.ready()
    out_weight.keep.wait()
    store(wo, wo_out)
    middle[...] = tok[...].astype(F32) + dot(mixed[...], wo[...])
    store(middle, middle_out)
    scale = lax.rsqrt(jnp.mean(middle[...] * middle[...], axis=1, keepdims=True) + EPS)
    h2[...] = (middle[...] * scale * params_low[1:2, :].astype(F32)).astype(BF)
    store(h2, h2_out)
    for ring in [small_ring, kv_ring, first] + weights:
        ring.wait_sent()
    own_copies[0].wait()
    for ring in seconds:
        ring.wait_far()
    for ring in seconds:
        ring.wait_sent()
    for step in leaving:
        step.wait()


def attention_forward(*arrays):
    dma = pltpu.SemaphoreType.DMA
    s, v = jax.ShapeDtypeStruct, pltpu.VMEM
    stored = (
        ((ROWS, 1024), BF),
        ((ROWS, 1024), F32),
        ((ROWS, 1024), BF),
        ((ROWS, 1024), BF),
        ((ROWS, 1024), F32),
        ((ROWS, 512), F32),
        ((HEAD_PAIRS, 1024, 256), BF),
        ((4, ROWS, 1024), BF),
        ((1024, 1024), BF),
        ((1024, 512), BF),
        ((1024, 512), BF),
        ((1024, 1024), BF),
        ((SMALL, 1024), BF),
        ((2, ROWS, 128), F32),
        ((ROWS + 1024, 128), BF),
        ((32, ROWS), F32),
    )
    return call(
        attention_kernel,
        tuple(s(*one) for one in stored) + (s((16, BLOCK, 1024), BF),),
        [VMEM] * 6 + [ANY] * 5,
        (ANY,) * 17,
        [v((SMALL, ROWS), BF), v((4, SMALL, ROWS), BF), v((BLOCK, 1024), BF), v((HEAD_PAIRS, 1024, 256), F32)]
        + [v(*one) for one in stored]
        + [
            dma((6,)),
            dma((16,)),
            dma((32,)),
            dma((32,)),
            dma((4,)),
            dma((4,)),
            dma((20,)),
            dma((20,)),
        ],
        0,
        vmem=56,
    )(*arrays)


ORDER = (-1, 2, 1, 0)


def nth_place(i):
    return 3 - i


class ColumnWeight:
    def __init__(self, me, wires, base, source, target, offset, half, rows, local):
        def at(k, part):
            return target.at[me.core, (me.x + k + 4) % 4 + offset, part]

        self.ring = GatherRing(wires, base, at, source, me.along_x(1), me.along_x(-1), half, rows)
        self.keep = pltpu.make_async_copy(source, at(0, pl.ds(0, rows)), local)
        mine, other = target.at[me.core, pl.ds(offset, 4)], target.at[1 - me.core, pl.ds(offset, 4)]
        self.pass_on = wires.copy(mine, mine, base + 4, me.sibling())
        self.passed = wires.copy(other, other, base + 4, me.sibling())

    def start(self):
        self.ring.start()
        self.keep.start()

    def forward(self):
        self.ring.forward(0)
        self.ring.forward(1)

    def finish(self):
        self.ring.wait_far()
        self.keep.wait()
        self.pass_on.start()

    def wait_sent(self):
        self.ring.wait_sent()
        self.pass_on.wait_send()


def expert_kernel(
    h_ref,
    g_ref,
    router,
    gate_in,
    up_in,
    down_in,
    dx_out,
    y_out,
    y_near,
    own_g_out,
    own_u_out,
    own_d_out,
    pair_g_out,
    pair_u_out,
    pair_d_out,
    wgu,
    wd,
    wr,
    buf,
    gbuf,
    near,
    landing,
    near_f,
    landing_f,
    xb,
    gxb,
    yb,
    dxb,
    act,
    dgu,
    hot,
    hot_t,
    weight,
    dgate,
    ystage,
    a_send,
    a_recv,
    r_send,
    r_recv,
    e_send,
    e_recv,
    p_send,
    p_recv,
    y_send,
    y_recv,
    local,
    g_local,
    y_local,
):
    me = Place()
    f_right, f_left, s_right, s_left = me.at(1, 0), me.at(-1, 0), me.at(0, 1), me.at(0, -1)
    a_wires, r_wires = Wires(a_send, a_recv), Wires(r_send, r_recv)
    e_wires, p_wires, y_wires = Wires(e_send, e_recv), Wires(p_send, p_recv), Wires(y_send, y_recv)
    own = buf.at[me.block(0, 0), pl.ds(0, ROWS)]
    fetches = [
        pltpu.make_async_copy(h_ref, own, local.at[0]),
        pltpu.make_async_copy(router.at[pl.ds(ROUTER_ROW, 32), :], wr, local.at[1]),
    ]
    for step in fetches:
        step.start()
    gate_weight = ColumnWeight(me, e_wires, 0, gate_in, wgu, 0, 512, 1024, local.at[2])
    up_weight = ColumnWeight(me, e_wires, 5, up_in, wgu, 4, 512, 1024, local.at[3])
    down_weight = ColumnWeight(me, e_wires, 10, down_in, wd, 0, 64, 128, local.at[4])
    weights = [gate_weight, up_weight, down_weight]
    greet([f_right, f_left, s_right, s_left, me.along_x(1), me.along_x(-1), me.sibling()])
    order = nth_place

    first = GatherRing(
        a_wires, 0, lambda k, rows: buf.at[me.block(k, 0), rows], own, f_right, f_left, HALF, ROWS
    )

    def second(i):
        fo = order(i)

        def at(k, rows):
            return buf.at[me.block(fo, k), rows]

        return GatherRing(a_wires, 4 + 4 * i, at, at(0, pl.ds(0, ROWS)), s_right, s_left, HALF, ROWS)

    def reduce_second(i):
        fo = order(i)
        return ReduceRing(
            r_wires,
            4 + 4 * i,
            lambda k, rows: buf.at[me.block(fo, k), rows],
            lambda rows: near.at[i, rows],
            lambda way: landing.at[i, way],
            s_right,
            s_left,
            HALF,
            BLOCK,
        )

    reduce_first = ReduceRing(
        r_wires,
        0,
        lambda k, rows: buf.at[me.block(k, 0), rows],
        lambda rows: near_f.at[rows],
        lambda way: landing_f.at[way],
        f_right,
        f_left,
        HALF,
        BLOCK,
    )

    def load_g(i):
        start = ((me.first + order(i)) % 4) * 4
        return pltpu.make_async_copy(g_ref.at[pl.ds(start, 4)], gbuf.at[i % 2], g_local.at[i % 2])

    def store_y(i, j):
        return pltpu.make_async_copy(ystage.at[j], y_out.at[((me.first + order(i)) % 4) * 4 + j], y_local.at[j])

    def far_y(i):
        block = ystage.at[(me.second + 2) % 4]
        low, high = pl.ds(0, HALF), pl.ds(HALF, HALF)
        return [
            y_wires.copy(block.at[low], y_near.at[i, low], 2 * i, s_right),
            y_wires.copy(block.at[high], y_near.at[i, high], 2 * i + 1, s_left),
        ]

    fetches[0].wait()
    first.start()
    gate_weight.start()
    up_weight.start()
    load_g(0).start()
    first.forward(0)
    second(0).start()
    first.forward(1)
    gate_weight.forward()
    up_weight.forward()
    down_weight.start()
    fetches[1].wait()
    gate_weight.finish()
    second(0).forward(0)
    second(0).forward(1)
    first.wait_far()
    second(1).start()
    down_weight.forward()
    up_weight.finish()
    second(2).start()

    expert_row = lax.broadcasted_iota(jnp.int32, (32, 256), 0)
    slot_row = lax.broadcasted_iota(jnp.int32, (CAP, 256), 0).astype(F32)
    low_row = lax.broadcasted_iota(jnp.int32, (8, 1024), 0)
    quarter = lax.broadcasted_iota(jnp.int32, (8, 1024), 1) // 256
    my_quarter = quarter == me.chip // 4
    my_low = 2 * (me.chip % 4)

    def pick(table, e):
        return jnp.sum(jnp.where(expert_row == 2 * me.chip + e, table, 0.0), axis=0, keepdims=True)

    @pl.loop(0, 4)
    def _(i):
        base = ((me.first + order(i)) % 4) * 4
        slot = i % 2
        second(i).wait_far()

        @pl.when(i < 3)
        def _():
            load_g(i + 1).start()

        load_g(i).wait()

        @pl.loop(0, 4)
        def _(j):
            h = buf[base + j, pl.ds(0, ROWS), :]
            g = gbuf[slot, j, pl.ds(0, ROWS), :]
            packed = gbuf[slot, j, pl.ds(ROWS, 16), :].astype(F32)[0:8]
            places = jnp.concatenate([packed[:, q * 256 : (q + 1) * 256] for q in range(4)], axis=0)
            logits = dot(wr[...], h, NT)
            routed = places >= 0.0
            top = jnp.max(jnp.where(routed, logits, -1e30), axis=0, keepdims=True)
            terms = jnp.where(routed, jnp.exp(jnp.where(routed, logits - top, 0.0)), 0.0)
            gates = terms / jnp.sum(terms, axis=0, keepdims=True)
            for e in range(2):
                hit = pick(places, e) == slot_row
                rows = pl.ds(e * CAP, CAP)
                weight[j, rows, :] = jnp.sum(jnp.where(hit, pick(gates, e), 0.0), axis=1, keepdims=True)
                hot[j, rows, :] = hit.astype(F32).astype(BF)
            hot_t[j] = jnp.transpose(hot[j].astype(F32)).astype(BF)
            xb[i, j] = dot(hot[j], h).astype(BF)
            gxb[i, j] = dot(hot[j], g).astype(BF)


        @pl.when(i > 1)
        def _():
            reduce_second(i - 2).finish()

        @pl.when(i == 3)
        def _():
            reduce_first.start()


        @pl.when(i == 0)
        def _():
            second(1).forward(0)
            second(1).forward(1)
            down_weight.finish()
            second(2).forward(0)
            second(2).forward(1)
            second(3).start()
            for step in weights:
                step.passed.wait_recv()

        @pl.when(i == 1)
        def _():
            second(3).forward(0)
            second(3).forward(1)

        @pl.loop(0, 2)
        def _(e):
            rows = pl.ds(pl.multiple_of(e * CAP, 32), CAP)
            x = xb[i, :, rows, :].reshape(4 * CAP, 1024)
            gx = gxb[i, :, rows, :].reshape(4 * CAP, 1024)
            gate = weight[:, rows, :].reshape(4 * CAP, 1)
            dy = (gate * gx.astype(F32)).astype(BF)
            gxb[i, :, rows, :] = dy.reshape(4, CAP, 1024)
            gate_up = jnp.concatenate([wgu[e, n] for n in range(8)], axis=1)
            down = wd[e].reshape(512, 1024)
            both = dot(x, gate_up)
            gate_pre, up_pre = both[:, 0:512], both[:, 512:1024]
            grad_act = dot(dy, down, NT)
            sig = 1.0 / (1.0 + jnp.exp(-gate_pre))
            silu = gate_pre * sig
            active = (silu * up_pre).astype(BF)
            grad_gate = (grad_act * up_pre * (sig * (1.0 + gate_pre * (1.0 - sig)))).astype(BF)
            grad_up = (grad_act * silu).astype(BF)
            act[i, :, rows, :] = active.reshape(4, CAP, 512)
            dgu[i, :, rows, pl.ds(0, 512)] = grad_gate.reshape(4, CAP, 512)
            dgu[i, :, rows, pl.ds(512, 512)] = grad_up.reshape(4, CAP, 512)
            out = dot(active, down).astype(BF).astype(F32)
            dgate[:, rows, :] = jnp.sum(gx.astype(F32) * out, axis=1, keepdims=True).reshape(4, CAP, 1)
            yb[:, rows, :] = (gate * out).astype(BF).reshape(4, CAP, 1024)


        @pl.when(i > 0)
        def _():
            reduce_second(i - 1).middle(0)
            reduce_second(i - 1).middle(1)

        second(i).wait_sent()

        @pl.when(i == 0)
        def _():
            first.on[0].wait_send()

        @pl.when(i == 2)
        def _():
            first.on[1].wait_send()

        @pl.when(i == 3)
        def _():
            for step in first.go:
                step.wait_send()

        @pl.loop(0, 2)
        def _(e):
            rows = pl.ds(pl.multiple_of(e * CAP, 32), CAP)
            gate_up = jnp.concatenate([wgu[e, n] for n in range(8)], axis=1)
            grad_in = dot(dgu[i, :, rows, :].reshape(4 * CAP, 1024), gate_up, NT)
            dxb[:, rows, :] = grad_in.astype(BF).reshape(4, CAP, 1024)

        @pl.loop(0, 4)
        def _(j):
            buf[base + j, pl.ds(0, ROWS), :] = dot(hot_t[j], dxb[j]).astype(BF)
            spots = hot[j].astype(F32) * dgate[j]
            grad_rows = [jnp.sum(spots[e * CAP : (e + 1) * CAP], axis=0, keepdims=True) for e in range(2)]
            wide = [jnp.concatenate([row] * 4, axis=1) for row in grad_rows]
            mine = jnp.where(low_row == my_low, wide[0], jnp.where(low_row == my_low + 1, wide[1], 0.0))
            mine = jnp.where(my_quarter, mine, 0.0)
            high = mine.astype(BF).astype(F32)
            buf[base + j, pl.ds(ROWS, 16), :] = jnp.concatenate([high, mine - high], axis=0).astype(BF)

        reduce_second(i).start()

        @pl.loop(0, 4)
        def _(j):
            @pl.when(i > 0)
            def _():
                store_y(i - 1, j).wait()

            @pl.when((i > 0) & (j == (me.second + 2) % 4))
            def _():
                for step in far_y(i - 1):
                    step.wait_send()

            ystage[j] = dot(hot_t[j], yb[j]).astype(BF)
            store_y(i, j).start()

        @pl.when(i < 3)
        def _():
            for step in far_y(i):
                step.start()


    for j in range(4):
        store_y(3, j).wait()

    leaving = [None] * 4

    def weight_chunk(number):
        stays, n = number >= 6, number % 6
        expert = me.core if stays else 1 - me.core
        rows = pl.ds(pl.multiple_of(expert * CAP, 32), CAP)
        slot = number % 4
        if leaving[slot] is not None:
            for step in leaving[slot]:
                step()
        if n < 2:
            inner = act[:, :, rows, pl.ds(n * 256, 256)].reshape(16 * CAP, 256)
            outer = gxb[:, :, rows, :].reshape(16 * CAP, 1024)
            parts = [(ystage.at[slot], own_d_out if stays else pair_d_out, n)]
        else:
            n = n - 2
            inner = xb[:, :, rows, pl.ds(n * 256, 256)].reshape(16 * CAP, 256)
            outer = dgu[:, :, rows, :].reshape(16 * CAP, 1024)
            parts = [
                (ystage.at[slot, :, pl.ds(0, 512)], own_g_out if stays else pair_g_out, n),
                (ystage.at[slot, :, pl.ds(512, 512)], own_u_out if stays else pair_u_out, n),
            ]
        ystage[slot] = dot(inner, outer, TN).astype(BF)
        leaving[slot] = []
        for part, (stage, out, n) in enumerate(parts):
            target = out.at[pl.ds(n * 256, 256), :]
            if stays:
                step = pltpu.make_async_copy(stage, target, y_local.at[2 * slot + part])
                leaving[slot].append(step.wait)
            else:
                step = p_wires.copy(stage, target, 2 * number + part, me.sibling())
                leaving[slot].append(step.wait_send)
            step.start()

    for number in range(6):
        weight_chunk(number)
    reduce_first.middle(1)
    reduce_second(3).middle(0)
    reduce_second(3).middle(1)
    reduce_second(2).finish()
    reduce_first.middle(0)
    for number in range(6, 12):
        weight_chunk(number)
    reduce_second(3).finish()
    mine = me.block(0, 0)
    for step in reduce_first.mid:
        step.wait_recv()
    add_into(buf.at[mine], landing_f.at[0], landing_f.at[1])
    result = pltpu.make_async_copy(buf.at[mine], dx_out, local.at[0])
    result.start()
    for steps in leaving:
        for step in steps:
            step()
    for number in range(6):
        outs = (pair_d_out,) if number < 2 else (pair_g_out, pair_u_out)
        for part, out in enumerate(outs):
            here = out.at[pl.ds((number if number < 2 else number - 2) * 256, 256), :]
            p_wires.copy(here, here, 2 * number + part, me.sibling()).wait_recv()
    for step in range(4):
        reduce_second(step).wait_sent()
    reduce_first.wait_sent()
    for step in weights:
        step.wait_sent()
    for i in range(3):
        for step in far_y(i):
            step.wait_recv()
    result.wait()


def expert_stage(*arrays):
    dma = pltpu.SemaphoreType.DMA
    s, v = jax.ShapeDtypeStruct, pltpu.VMEM
    return call(
        expert_kernel,
        (
            s((BLOCK, 1024), BF),
            s((16, ROWS, 1024), BF),
            s((3, ROWS, 1024), BF),
            s((1024, 512), BF),
            s((1024, 512), BF),
            s((512, 1024), BF),
            s((1024, 512), BF),
            s((1024, 512), BF),
            s((512, 1024), BF),
        ),
        [ANY] * 6,
        (ANY,) * 9,
        [
            v((2, 8, 1024, 128), BF),
            v((2, 4, 128, 1024), BF),
            v((32, 1024), BF),
            v((16, BLOCK, 1024), BF),
            v((2, 4, BLOCK, 1024), BF),
            v((4, BLOCK, 1024), BF),
            v((4, 2, BLOCK, 1024), BF),
            v((BLOCK, 1024), BF),
            v((2, BLOCK, 1024), BF),
            v((4, 4, 2 * CAP, 1024), BF),
            v((4, 4, 2 * CAP, 1024), BF),
            v((4, 2 * CAP, 1024), BF),
            v((4, 2 * CAP, 1024), BF),
            v((4, 4, 2 * CAP, 512), BF),
            v((4, 4, 2 * CAP, 1024), BF),
            v((4, 2 * CAP, 256), BF),
            v((4, 256, 2 * CAP), BF),
            v((4, 2 * CAP, 1), F32),
            v((4, 2 * CAP, 1), F32),
            v((4, ROWS, 1024), BF),
            dma((20,)),
            dma((20,)),
            dma((20,)),
            dma((20,)),
            dma((15,)),
            dma((15,)),
            dma((12,)),
            dma((12,)),
            dma((6,)),
            dma((6,)),
            dma((5,)),
            dma((2,)),
            dma((8,)),
        ],
        1,
        vmem=62,
    )(*arrays)


class Sum:
    def __init__(self, me, wires, base, own, pair, part_f, part_x, part_s, part_o, total):
        self.pair, self.part_f, self.part_x, self.part_s, self.part_o = pair, part_f, part_x, part_s, part_o

        def half_of(core):
            return pl.ds(pl.multiple_of(core * HALF, HALF), HALF)

        def cols_of(place):
            return pl.ds(pl.multiple_of(((place + 4) % 4) * 256, 256), 256)

        def there(rows, cols, number, device):
            return wires.copy(total.at[rows, cols], total.at[rows, cols], base + number, device)

        other, first, second = 1 - me.core, me.first, me.second
        kept, steps = half_of(me.core), (1, 2, 3)
        cols = cols_of(first)
        self.kept = own.at[:, kept]
        self.mine_f, self.mine_x = own.at[:, kept, cols], own.at[me.x, kept, cols]
        self.swap = wires.copy(own.at[:, half_of(other), :], pair, base, me.sibling())
        self.out_f = [
            wires.copy(own.at[:, kept, cols_of(first + k)], part_f.at[k - 1], base + k, me.at(k, 0)) for k in steps
        ]
        self.out_x = [
            wires.copy(own.at[(me.x + k) % 4, kept, cols], part_x.at[k - 1], base + 3 + k, me.along_x(k)) for k in steps
        ]
        self.out_s = [wires.copy(part_s.at[0], part_s.at[k], base + 6 + k, me.at(0, k)) for k in steps]
        self.out_s += [wires.copy(part_s.at[0], part_o.at[k], base + 10 + k, me.other_at(0, k)) for k in range(4)]
        self.result, self.result_other = total.at[kept, cols], total.at[half_of(other), cols_of(second)]
        self.back = [there(kept, cols, 13 + k, me.at(k, 0)) for k in steps]
        self.back += [there(kept, cols, 16 + k, me.other_at(k, 0)) for k in steps]
        self.came = [there(kept, cols_of(first - k), 13 + k, me.at(k, 0)) for k in steps]
        self.came += [there(half_of(other), cols_of(second - k), 16 + k, me.at(1, 0)) for k in steps]

    def step(self, number):
        if number == 0:
            self.swap.start()
        elif number == 1:
            self.swap.wait_recv()
            add_into(self.kept, self.pair)
            for copy in self.out_f:
                copy.start()
        elif number == 2:
            for copy in self.out_f:
                copy.wait_recv()
            add_into(self.mine_f, *[self.part_f.at[n] for n in range(3)])
            for copy in self.out_x:
                copy.start()
        elif number == 3:
            for copy in self.out_x:
                copy.wait_recv()
            add_up(self.part_s.at[0], self.mine_x, *[self.part_x.at[n] for n in range(3)])
            for copy in self.out_s:
                copy.start()
        elif number == 4:
            for copy in self.out_s:
                copy.wait_recv()
            add_up(self.result, *[self.part_s.at[n] for n in range(4)])
            add_up(self.result_other, *[self.part_o.at[n] for n in range(4)])
            for copy in self.back:
                copy.start()
        else:
            for copy in self.came:
                copy.wait_recv()

    def wait_sent(self):
        for copy in [self.swap] + self.out_f + self.out_x + self.out_s + self.back:
            copy.wait_send()


class SumByX:
    def __init__(self, me, wires, base, own, pair, near, landing, part_f, part_s, part_o, total):
        self.pair, self.part_f, self.part_s, self.part_o = pair, part_f, part_s, part_o

        def half_of(core):
            return pl.ds(pl.multiple_of(core * HALF, HALF), HALF)

        def cols_of(place):
            return pl.ds(pl.multiple_of(((place + 4) % 4) * 256, 256), 256)

        def there(rows, cols, number, device):
            return wires.copy(total.at[rows, cols], total.at[rows, cols], base + number, device)

        other, first, second = 1 - me.core, me.first, me.second
        kept, steps = half_of(me.core), (1, 2, 3)
        cols = cols_of(first)
        self.kept, self.mine_f = own.at[:, kept], own.at[me.x, kept, cols]
        self.swap = wires.copy(own.at[:, half_of(other), :], pair, base, me.sibling())
        self.ring = ReduceRing(
            wires,
            base + 1,
            lambda k, part: own.at[(me.x + k + 4) % 4, kept].at[part],
            lambda part: near.at[part],
            lambda way: landing.at[way],
            me.along_x(1),
            me.along_x(-1),
            64,
            HALF,
        )
        self.out_f = [
            wires.copy(own.at[me.x, kept, cols_of(first + k)], part_f.at[k - 1], base + 4 + k, me.at(k, 0)) for k in steps
        ]
        self.out_s = [wires.copy(part_s.at[0], part_s.at[k], base + 7 + k, me.at(0, k)) for k in steps]
        self.out_s += [wires.copy(part_s.at[0], part_o.at[k], base + 11 + k, me.other_at(0, k)) for k in range(4)]
        self.result, self.result_other = total.at[kept, cols], total.at[half_of(other), cols_of(second)]
        self.back = [there(kept, cols, 14 + k, me.at(k, 0)) for k in steps]
        self.back += [there(kept, cols, 17 + k, me.other_at(k, 0)) for k in steps]
        self.came = [there(kept, cols_of(first - k), 14 + k, me.at(k, 0)) for k in steps]
        self.came += [there(half_of(other), cols_of(second - k), 17 + k, me.at(1, 0)) for k in steps]

    def step(self, number):
        if number == 0:
            self.swap.start()
        elif number == 1:
            self.swap.wait_recv()
            add_into(self.kept, self.pair)
            self.ring.start()
        elif number == 2:
            self.ring.middle(0)
            self.ring.middle(1)
        elif number == 3:
            self.ring.finish()
            for copy in self.out_f:
                copy.start()
        elif number == 4:
            for copy in self.out_f:
                copy.wait_recv()
            add_up(self.part_s.at[0], self.mine_f, *[self.part_f.at[n] for n in range(3)])
            for copy in self.out_s:
                copy.start()
        elif number == 5:
            for copy in self.out_s:
                copy.wait_recv()
            add_up(self.result, *[self.part_s.at[n] for n in range(4)])
            add_up(self.result_other, *[self.part_o.at[n] for n in range(4)])
            for copy in self.back:
                copy.start()
        else:
            for copy in self.came:
                copy.wait_recv()

    def wait_sent(self):
        self.ring.wait_sent()
        for copy in [self.swap] + self.out_f + self.out_s + self.back:
            copy.wait_send()


LOADED = {
    "summed": ((BLOCK, 1024), BF),
    "h2": ((ROWS, 1024), BF),
    "middle": ((ROWS, 1024), F32),
    "cot": ((ROWS, 1024), BF),
    "tok": ((ROWS, 1024), BF),
    "mixed": ((ROWS, 1024), BF),
    "h1": ((ROWS, 1024), BF),
    "qpre": ((ROWS, 1024), F32),
    "kpre": ((ROWS, 512), F32),
    "qa": ((HEAD_PAIRS, 1024, 256), BF),
    "kv": ((4, ROWS, 1024), BF),
    "wk": ((1024, 512), BF),
    "wv": ((1024, 512), BF),
    "small": ((SMALL, 1024), BF),
    "rope": ((2, ROWS, 128), F32),
    "aug": ((ROWS + 1024, 128), BF),
    "places": ((32, ROWS), F32),
}


def backward_kernel(*refs):
    sources, refs = dict(zip(LOADED, refs)), refs[len(LOADED) :]
    wq, wo, gw, uw, dw, gp, up, dp, y, y_near = refs[:10]
    layer_out, tokens_out, total_out, small_out, g_out, u_out, d_out, y_land = refs[10:18]
    refs = refs[18:]
    held, refs = dict(zip(LOADED, refs)), refs[len(LOADED) :]
    (
        doa,
        dqa,
        dkv,
        wbuf,
        parts,
        pair_w,
        part_f,
        part_x,
        part_s,
        part_o,
        near_w,
        land_w,
        out_part_f,
        out_part_s,
        out_part_o,
        total_w,
        near_k,
        land_k,
        own_g,
        own_u,
        own_d,
        pair_g,
        pair_u,
        pair_d,
        near_g,
        near_u,
        near_d,
        land_g,
        land_u,
        land_d,
        buf,
        y_sum,
        near_y,
        near_last,
        far_block,
        near_f,
        land_f,
        small_part,
        small_pair,
        small_x,
        small_f,
        small_s,
        layer,
        grad_middle,
        small_total,
        final_g,
        final_u,
        final_d,
        e_send,
        e_recv,
        w_send,
        w_recv,
        k_send,
        k_recv,
        y_send,
        y_recv,
        t_send,
        t_recv,
        local,
        fetched,
        leave,
    ) = refs
    summed, h2, middle, cot, tok, mixed, h1, qpre, kpre, qa, kv, wk, wv, small, rope, aug, places = held.values()
    me = Place()
    x, core = me.x, me.core
    right, left, sibling = me.along_x(1), me.along_x(-1), me.sibling()
    planes = [me.at(k, 0) for k in (1, 2, 3)] + [me.at(0, k) for k in (1, 2, 3)] + [me.along_x(k) for k in (1, 2, 3)]
    planes += [me.other_at(0, 0)] + [me.other_at(k, 0) for k in (1, 2, 3)] + [me.other_at(0, k) for k in (1, 2, 3)]
    greet(planes, wait=False)
    e_wires, w_wires, k_wires = Wires(e_send, e_recv), Wires(w_send, w_recv), Wires(k_send, k_recv)
    y_wires, t_wires = Wires(y_send, y_recv), Wires(t_send, t_recv)

    def shard(step):
        return (x + step + 4) % 4

    loads = {
        name: pltpu.make_async_copy(sources[name], held[name], fetched.at[n]) for n, name in enumerate(LOADED)
    }
    pulls = [
        pltpu.make_async_copy(source, target, local.at[n])
        for n, (source, target) in enumerate(
            ((gw, own_g), (uw, own_u), (dw, own_d), (gp, pair_g), (up, pair_u), (dp, pair_d), (wo, wbuf))
        )
    ]
    load_wq = pltpu.make_async_copy(wq, wbuf, local.at[7])

    def place_y(i, k):
        return ((me.first + ORDER[i] + 4) % 4) * 4 + (me.second + k + 4) % 4

    load_sides = [
        pltpu.make_async_copy(y.at[place_y(i, 1 - 2 * way)], buf.at[i, way], local.at[8 + 2 * i + way])
        for i in range(4)
        for way in range(2)
    ]
    load_near = pltpu.make_async_copy(y_near, near_y, local.at[16])
    load_far = pltpu.make_async_copy(y.at[place_y(3, 2)], far_block, local.at[17])
    load_own = [
        pltpu.make_async_copy(y.at[place_y(i, 0)], y_sum.at[(me.first + ORDER[i] + 4) % 4], local.at[18 + i])
        for i in range(4)
    ]

    def ready(*names):
        for name in names:
            loads[name].wait()

    leaving = []

    def store(source, target):
        step = pltpu.make_async_copy(source, target, leave.at[len(leaving)])
        leaving.append(step)
        step.start()

    for name in ("summed", "h2", "small", "places", "middle", "cot"):
        loads[name].start()

    low, high = pl.ds(0, HALF), pl.ds(HALF, HALF)
    s_right, s_left = me.at(0, 1), me.at(0, -1)
    far_y = [
        y_wires.copy(far_block.at[low], near_last.at[low], 4, s_right),
        y_wires.copy(far_block.at[high], near_last.at[high], 5, s_left),
    ]
    mid_y = [
        [
            y_wires.copy(buf.at[i, way], y_land.at[i, way], 6 + 2 * i + way, (s_right, s_left)[way])
            for way in range(2)
        ]
        for i in range(4)
    ]
    load_land = [pltpu.make_async_copy(y_land.at[i], buf.at[i], local.at[8 + i]) for i in range(4)]

    def y_middle(i):
        near = near_last if i == 3 else near_y.at[i]
        add_into(buf.at[i, 0, low], near.at[low])
        add_into(buf.at[i, 1, high], near.at[high])
        for step in mid_y[i]:
            step.start()

    def y_fetch(i):
        for step in mid_y[i]:
            step.wait_recv()
            step.wait_send()
        load_land[i].start()

    def y_finish(i):
        load_land[i].wait()
        add_into(y_sum.at[(me.first + ORDER[i] + 4) % 4], buf.at[i, 0], buf.at[i, 1])

    y_first = ReduceRing(
        y_wires,
        0,
        lambda k, rows: y_sum.at[(me.first + k + 4) % 4, rows],
        lambda rows: near_f.at[rows],
        lambda way: land_f.at[way],
        me.at(1, 0),
        me.at(-1, 0),
        HALF,
        ROWS,
    )
    def weight_sum(n, own):
        return Sum(
            me,
            w_wires,
            20 * n,
            own,
            pair_w.at[n % 2],
            part_f.at[n - 1],
            part_x.at[n - 1],
            part_s.at[n - 1],
            part_o.at[n - 1],
            total_w.at[n],
        )

    out_sum = SumByX(
        me, w_wires, 60, parts.at[0], pair_w.at[0], near_w, land_w, out_part_f, out_part_s, out_part_o, total_w.at[0]
    )
    query_sum, kv_sum = weight_sum(1, parts.at[1]), weight_sum(2, dkv)

    def weight_grad(target, left_rows, right_rows):
        for k in range(4):
            target[k] = dot(left_rows[:, k * ROWS : (k + 1) * ROWS], right_rows, TN).astype(BF)

    def slice_of(k):
        return pl.ds(pl.multiple_of(shard(k) * 128, 128), 128)

    def g_at(k, ref=None):
        return (own_g if ref is None else ref).at[:, slice_of(k)]

    def u_at(k, ref=None):
        return (own_u if ref is None else ref).at[:, slice_of(k)]

    def d_at(k, start=0, size=128, ref=None):
        return (own_d if ref is None else ref).at[pl.ds(pl.multiple_of(shard(k) * 128 + start, 64), size), :]

    e_far = [
        e_wires.copy(g_at(2), near_g, 3, right),
        e_wires.copy(d_at(2, 0, 64), near_d.at[0], 4, right),
        e_wires.copy(u_at(2), near_u, 5, left),
        e_wires.copy(d_at(2, 64, 64), near_d.at[1], 6, left),
    ]
    e_mid = [
        e_wires.copy(ref, land.at[way], 7 + way * 3 + i, device)
        for way, (k, device) in enumerate(((1, right), (-1, left)))
        for i, (ref, land) in enumerate(((g_at(k), land_g), (u_at(k), land_u), (d_at(k), land_d)))
    ]

    def add_pair(k):
        add_into(g_at(k), g_at(k, pair_g))
        add_into(u_at(k), u_at(k, pair_u))
        add_into(d_at(k), d_at(k, ref=pair_d))

    ready("summed", "h2", "small", "places")
    load_far.start()
    for step in pulls[:6]:
        step.start()
    for name in ("mixed", "aug"):
        loads[name].start()
    pulls[6].start()
    params = small[...].astype(F32)
    h2_rows = h2[...]
    numbers = summed[pl.ds(ROWS, 16), :].astype(F32)
    numbers = numbers[0:8] + numbers[8:16]
    grad_gates = jnp.concatenate([numbers[:, q * 256 : (q + 1) * 256] for q in range(4)], axis=0)
    logits = dot(small[pl.ds(ROUTER_ROW, 32), :], h2_rows, NT)
    routed = places[...] >= 0.0
    top = jnp.max(jnp.where(routed, logits, -1e30), axis=0, keepdims=True)
    terms = jnp.where(routed, jnp.exp(jnp.where(routed, logits - top, 0.0)), 0.0)
    gates = terms / jnp.sum(terms, axis=0, keepdims=True)
    grad_logits = gates * (grad_gates - jnp.sum(gates * grad_gates, axis=0, keepdims=True))
    grad_router = split_dot(grad_logits, h2_rows)
    for k in range(4):
        small_part[k, pl.ds(0, 32), :] = grad_router[:, k * ROWS : (k + 1) * ROWS]
        small_part[k, pl.ds(32, 16), :] = jnp.zeros((16, ROWS), F32)
    grad = summed[pl.ds(0, ROWS), :].astype(F32) + split_dot(grad_logits, small[pl.ds(ROUTER_ROW, 32), :], TN)

    def norm_back(v, gain, grad, row):
        scale = lax.rsqrt(jnp.mean(v * v, axis=1, keepdims=True) + EPS)
        normed = v * scale
        gained = gain * grad
        gain_grad = jnp.sum(grad * normed, axis=0, keepdims=True)
        for k in range(4):
            small_part[k, row : row + 1, :] = gain_grad[:, k * ROWS : (k + 1) * ROWS]
        return scale * (gained - normed * jnp.mean(gained * normed, axis=1, keepdims=True))

    ready("middle", "cot", "mixed")
    grad_middle[...] = cot[...].astype(F32) + norm_back(middle[...], params[1:2], grad, 33)
    grad_low = grad_middle[...].astype(BF)
    load_near.start()
    for step in load_sides + load_own:
        step.start()
    for name in ("qa", "kv"):
        loads[name].start()
    wait_for(planes)
    load_far.wait()
    for step in far_y:
        step.start()
    for step in pulls[:6]:
        step.wait()
    add_pair(2)
    for step in e_far:
        step.start()
    weight_grad(parts.at[0], mixed[...], grad_low)
    out_sum.step(0)
    grad_low = grad_middle[...].astype(BF)
    ready("aug")
    live = aug[pl.ds(0, ROWS), 4:5].astype(F32) == 0.0
    pulls[6].wait()
    grad_mixed = jnp.where(live, dot(grad_low, wbuf[...], NT), 0.0).astype(BF).astype(F32)
    row_dots = split_dot(grad_mixed * mixed[...].astype(F32), head_map(1024))
    lane = lanes()
    for j in range(8):
        for n, head in enumerate(split_heads(grad_mixed[:, j * 128 : (j + 1) * 128], j % 2 == 1)):
            start = ((j % 2) * 2 + n) * ROWS
            marks = jnp.zeros((ROWS, 128), F32)
            for m, part in enumerate(three_parts(-row_dots[:, 2 * j + n : 2 * j + n + 1])):
                marks = jnp.where(lane == 5 + m, part, marks)
            doa[j // 2, pl.ds(start, ROWS), pl.ds(0, 128)] = head.astype(BF)
            doa[j // 2, pl.ds(start, ROWS), pl.ds(128, 128)] = marks.astype(BF)

    load_wq.start()
    for step in [load_near] + load_sides + load_own:
        step.wait()
    for i in range(3):
        y_middle(i)
    for name in ("rope", "qpre", "kpre", "h1", "wk", "wv", "tok"):
        loads[name].start()
    ready("qa", "kv")

    def attend(k):
        there = shard(k)
        marks = aug[pl.ds(pl.multiple_of(there * ROWS + ROWS, ROWS), ROWS), :]

        @pl.loop(0, HEAD_PAIRS)
        def _(pair):
            start = pl.multiple_of(pair * 128, 128)
            keys = kv[there, :, pl.ds(start, 128)]
            keyed = jnp.concatenate([keys, marks], axis=1)
            valued = jnp.concatenate([kv[there, :, pl.ds(start + 512, 128)], marks], axis=1)
            p = jnp.exp(dot(qa[pair], keyed, NT))
            ds = (p * dot(doa[pair], valued, NT)).astype(BF)
            dkv[there, :, pl.ds(start + 512, 128)] = dot(p.astype(BF), doa[pair, :, pl.ds(0, 128)], TN).astype(BF)
            dkv[there, :, pl.ds(start, 128)] = dot(ds, qa[pair, :, pl.ds(0, 128)], TN).astype(BF)
            dq = dot(ds, keys)
            if k == 2:
                dqa[pair] = dq
            else:
                dqa[pair] += dq

    kv_ring = ReduceRing(
        k_wires,
        0,
        lambda k, rows: dkv.at[shard(k), rows],
        lambda rows: near_k.at[rows],
        lambda way: land_k.at[way],
        right,
        left,
        HALF,
        ROWS,
    )
    attend(2)
    kv_ring.start()
    out_sum.step(1)
    attend(1)
    for step in far_y:
        step.wait_recv()
    y_middle(3)
    attend(-1)
    kv_ring.middle(0)
    kv_ring.middle(1)
    attend(0)

    def heads_back(pre, grads, gain, count):
        heads = head_map(count)
        scale = head_scale(pre, heads)
        normed = pre * scale
        gained = gain * grads
        mean = split_dot(split_dot(gained * normed, heads) * (1.0 / 64), heads, NT)
        gain_grad = jnp.sum(grads * normed, axis=0, keepdims=True)
        folded = sum(gain_grad[:, j * 128 : (j + 1) * 128] for j in range(count // 128))
        return scale * (gained - normed * mean), folded + pltpu.roll(folded, 64, 1)

    ready("rope", "qpre", "h1")
    blocks = []
    for j in range(8):
        pair, odd = j // 2, j % 2 == 1
        heads = [dqa[pair, pl.ds(((j % 2) * 2 + n) * ROWS, ROWS), :] for n in range(2)]
        blocks.append(turn(join_heads(heads[0], heads[1], odd) * 0.125, rope[0], -rope[1]))
    query_grad, query_gain_grad = heads_back(qpre[...], jnp.concatenate(blocks, axis=1), params[2:3], 1024)
    query_low = query_grad.astype(BF)
    weight_grad(parts.at[1], h1[...], query_low)
    query_sum.step(0)
    for k in (1, -1, 0):
        add_pair(k)
    e_far[0].wait_recv()
    add_into(g_at(1), near_g)
    e_far[1].wait_recv()
    add_into(d_at(1, 0, 64), near_d.at[0])
    e_far[2].wait_recv()
    add_into(u_at(-1), near_u)
    e_far[3].wait_recv()
    add_into(d_at(-1, 64, 64), near_d.at[1])
    query_sum.step(1)
    y_fetch(1)
    load_wq.wait()
    grad_h1 = dot(query_low, wbuf[...], NT)
    ready("kpre")
    y_finish(1)
    y_first.start()

    kv_ring.finish()
    out_sum.step(2)
    own_kv = dkv[x].astype(F32)
    blocks = [turn(own_kv[:, j * 128 : (j + 1) * 128], rope[0], -rope[1]) for j in range(4)]
    key_grad, key_gain_grad = heads_back(kpre[...], jnp.concatenate(blocks, axis=1), params[3:4, 0:512], 512)
    low = jnp.concatenate([key_grad.astype(BF), own_kv[:, 512:1024].astype(BF)], axis=1)
    kv_ring.wait_sent()
    weight_grad(dkv, h1[...], low)
    kv_sum.step(0)
    ready("wk", "wv", "tok")
    grad_h1 = grad_h1 + dot(low[:, 0:512], wk[...], NT) + dot(low[:, 512:1024], wv[...], NT)
    grad_middle[...] += norm_back(tok[...].astype(F32), params[0:1], grad_h1, 32)
    store(grad_middle, tokens_out)
    for k in range(4):
        for row, folded in ((34, query_gain_grad), (35, key_gain_grad)):
            small_part[k, row : row + 1, pl.ds(0, 128)] = pltpu.roll(folded, (128 - 16 * k) % 128, 1)

    t_pair = t_wires.copy(small_part, small_pair, 0, sibling)
    t_pair.start()
    kv_sum.step(1)
    y_fetch(0)
    y_fetch(2)
    y_finish(0)
    y_finish(2)
    query_sum.step(2)
    y_first.middle_both()
    y_fetch(3)
    t_pair.wait_recv()
    t_x = [t_wires.copy(small_part.at[shard(k)], small_x.at[k - 1], k, me.along_x(k)) for k in (1, 2, 3)]
    t_pair.wait_send()
    for k in range(4):
        small_part[k] += small_pair[k]
    for step in t_x:
        step.start()
    y_finish(3)
    query_sum.step(3)
    out_sum.step(3)
    kv_sum.step(2)
    for step in e_mid:
        step.start()
    kv_sum.step(3)
    for step in t_x:
        step.wait_recv()
    small_f[0] = small_part[x] + small_x[0] + small_x[1] + small_x[2]
    t_f = [t_wires.copy(small_f.at[0], small_f.at[k], 3 + k, me.at(k, 0)) for k in (1, 2, 3)]
    for step in t_f:
        step.start()
    out_sum.step(4)
    kv_sum.step(4)
    query_sum.step(4)
    y_first.finish()
    layer[...] = (middle[...] + y_sum[me.first].astype(F32)).astype(BF)
    store(layer, layer_out)
    for step in t_f:
        step.wait_recv()
    small_s[0] = small_f[0] + small_f[1] + small_f[2] + small_f[3]
    t_s = [t_wires.copy(small_s.at[0], small_s.at[k], 6 + k, me.at(0, k)) for k in (1, 2, 3)]
    for step in t_s:
        step.start()
    kv_sum.step(5)
    store(total_w.at[2], total_out.at[2])
    out_sum.step(5)
    query_sum.step(5)
    store(total_w.at[1], total_out.at[1])
    for step in e_mid:
        step.wait_recv()
    for out, at, land, target in (
        (final_g, g_at, land_g, g_out),
        (final_u, u_at, land_u, u_out),
        (final_d, d_at, land_d, d_out),
    ):
        add_up(out, at(0), land.at[0], land.at[1])
        store(out, target)
    out_sum.step(6)
    store(total_w.at[0], total_out.at[0])
    for step in t_s:
        step.wait_recv()
    small_total[...] = small_s[0] + small_s[1] + small_s[2] + small_s[3]
    store(small_total, small_out)
    for step in e_far + e_mid + t_x + t_f + t_s + far_y:
        step.wait_send()
    for ring in [y_first, out_sum, query_sum, kv_sum]:
        ring.wait_sent()
    for step in leaving:
        step.wait()


def backward_stage(*arrays):
    dma = pltpu.SemaphoreType.DMA
    s, v = jax.ShapeDtypeStruct, pltpu.VMEM
    return call(
        backward_kernel,
        (
            s((ROWS, 1024), BF),
            s((ROWS, 1024), F32),
            s((3, ROWS, 1024), BF),
            s((SMALL, ROWS), F32),
            s((1024, 128), F32),
            s((1024, 128), F32),
            s((128, 1024), F32),
            s((4, 2, ROWS, 1024), BF),
        ),
        [ANY] * (len(LOADED) + 10),
        (ANY,) * 8,
        [v(*one) for one in LOADED.values()]
        + [
            v((HEAD_PAIRS, 1024, 256), BF),
            v((HEAD_PAIRS, 1024, 128), F32),
            v((4, ROWS, 1024), BF),
            v((1024, 1024), BF),
            v((2, 4, ROWS, 1024), BF),
            v((2, 4, HALF, 1024), BF),
            v((2, 3, 4, HALF, 256), BF),
            v((2, 3, HALF, 256), BF),
            v((2, 4, HALF, 256), BF),
            v((2, 4, HALF, 256), BF),
            v((HALF, 1024), BF),
            v((2, HALF, 1024), BF),
            v((3, HALF, 256), BF),
            v((4, HALF, 256), BF),
            v((4, HALF, 256), BF),
            v((3, ROWS, 1024), BF),
            v((ROWS, 1024), BF),
            v((2, ROWS, 1024), BF),
            v((1024, 512), BF),
            v((1024, 512), BF),
            v((512, 1024), BF),
            v((1024, 512), BF),
            v((1024, 512), BF),
            v((512, 1024), BF),
            v((1024, 128), BF),
            v((1024, 128), BF),
            v((2, 64, 1024), BF),
            v((2, 1024, 128), BF),
            v((2, 1024, 128), BF),
            v((2, 128, 1024), BF),
            v((4, 2, ROWS, 1024), BF),
            v((4, ROWS, 1024), BF),
            v((3, ROWS, 1024), BF),
            v((ROWS, 1024), BF),
            v((ROWS, 1024), BF),
            v((ROWS, 1024), BF),
            v((2, ROWS, 1024), BF),
            v((4, SMALL, ROWS), F32),
            v((4, SMALL, ROWS), F32),
            v((3, SMALL, ROWS), F32),
            v((4, SMALL, ROWS), F32),
            v((4, SMALL, ROWS), F32),
            v((ROWS, 1024), BF),
            v((ROWS, 1024), F32),
            v((SMALL, ROWS), F32),
            v((1024, 128), F32),
            v((1024, 128), F32),
            v((128, 1024), F32),
            dma((13,)),
            dma((13,)),
            dma((81,)),
            dma((81,)),
            dma((4,)),
            dma((4,)),
            dma((14,)),
            dma((14,)),
            dma((10,)),
            dma((10,)),
            dma((22,)),
            dma((len(LOADED),)),
            dma((9,)),
        ],
        2,
        vmem=63,
    )(*arrays)


def last_kernel(layer, tokens, totals, small, g, u, d, *rest):
    outs, (layer_v, tokens_v, totals_v, small_v, g_v, u_v, d_v), held, sem = rest[:14], rest[14:21], rest[21:25], rest[25]
    sources = (totals, small, tokens, layer, g, u, d)
    inside = (totals_v, small_v, tokens_v, layer_v, g_v, u_v, d_v)
    loads = [pltpu.make_async_copy(source, inner, sem.at[n]) for n, (source, inner) in enumerate(zip(sources, inside))]
    for step in loads:
        step.start()
    layer_out, tokens_out, g_out, u_out, d_out, wq, wk, wv, wo, first, second, head_q, head_k, router = outs
    wq_v, wk_v, wv_v, wo_v = held
    stores = []

    def store(source, target):
        step = pltpu.make_async_copy(source, target, sem.at[7 + len(stores)])
        stores.append(step)
        step.start()

    loads[0].wait()
    wq_v[...] = totals_v[1].astype(F32)
    store(wq_v, wq)
    wo_v[...] = totals_v[0].astype(F32)
    store(wo_v, wo)
    wk_v[...] = totals_v[2, :, pl.ds(0, 512)].astype(F32)
    store(wk_v, wk)
    wv_v[...] = totals_v[2, :, pl.ds(512, 512)].astype(F32)
    store(wv_v, wv)
    loads[1].wait()
    first[...] = small_v[32:33, :]
    second[...] = small_v[33:34, :]
    head_q[...] = small_v[34:35, 0:16]
    head_k[...] = small_v[35:36, 0:16]
    router[...] = small_v[0:32, :]
    for step, inner, target in zip(loads[2:], inside[2:], (tokens_out, layer_out, g_out, u_out, d_out)):
        step.wait()
        store(inner, target)
    for step in stores:
        step.wait()


def last_stage(*arrays):
    s, v = jax.ShapeDtypeStruct, pltpu.VMEM
    return pl.pallas_call(
        last_kernel,
        out_shape=(
            s((ROWS, 1024), BF),
            s((ROWS, 1024), F32),
            s((1024, 128), F32),
            s((1024, 128), F32),
            s((128, 1024), F32),
            s((ROWS, 1024), F32),
            s((ROWS, 512), F32),
            s((ROWS, 512), F32),
            s((ROWS, 1024), F32),
            s((1, ROWS), F32),
            s((1, ROWS), F32),
            s((1, 16), F32),
            s((1, 16), F32),
            s((32, ROWS), F32),
        ),
        in_specs=[ANY] * 7,
        out_specs=(ANY,) * 9 + (VMEM,) * 5,
        scratch_shapes=[
            v((ROWS, 1024), BF),
            v((ROWS, 1024), F32),
            v((3, ROWS, 1024), BF),
            v((SMALL, ROWS), F32),
            v((1024, 128), F32),
            v((1024, 128), F32),
            v((128, 1024), F32),
            v((ROWS, 1024), F32),
            v((ROWS, 512), F32),
            v((ROWS, 512), F32),
            v((ROWS, 1024), F32),
            pltpu.SemaphoreType.DMA((16,)),
        ],
        compiler_params=pltpu.CompilerParams(vmem_limit_bytes=62 * MIB),
    )(*arrays)


def body(
    tokens,
    lengths,
    routes,
    norm1_gain,
    w_query,
    w_key,
    w_value,
    query_gain,
    key_gain,
    w_out,
    norm2_gain,
    w_router,
    w_gate,
    w_up,
    w_down,
    cotangent,
):
    frequency = (ROPE_BASE ** -((np.arange(128) % 32) / 32.0)).astype(np.float32)[None]
    gains = jnp.concatenate(
        [norm1_gain, norm2_gain, jnp.pad(query_gain, (0, ROWS - 16)), jnp.pad(key_gain, (0, ROWS - 16))]
    ).reshape(4, ROWS)
    (h2, middle, mixed, h1, qpre, kpre, qa, kv, wq, wk, wv, wo, small, rope, aug, places, g_all) = attention_forward(
        tokens,
        routes.T,
        lengths,
        gains,
        w_router.T,
        jnp.asarray(frequency),
        w_key,
        w_value,
        w_query,
        w_out,
        cotangent,
    )
    summed, y_part, y_near, *expert_grads = expert_stage(
        h2, g_all, small, w_gate[0], w_up[0], w_down[0]
    )
    results = backward_stage(
        summed,
        h2,
        middle,
        cotangent,
        tokens,
        mixed,
        h1,
        qpre,
        kpre,
        qa,
        kv,
        wk,
        wv,
        small,
        rope,
        aug,
        places,
        wq,
        wo,
        *expert_grads,
        y_part,
        y_near,
    )
    layer, tokens_grad, gate_grad, up_grad, down_grad, wq_g, wk_g, wv_g, wo_g, first, second, head_q, head_k, router = last_stage(
        *results[:7]
    )
    return (
        layer,
        tokens_grad,
        first[0],
        wq_g,
        wk_g,
        wv_g,
        head_q[0],
        head_k[0],
        wo_g,
        second[0],
        router.T,
        gate_grad[None],
        up_grad[None],
        down_grad[None],
    )


def solution(mesh):
    rows = P(("expert", "shard"), None)
    by_shard = P("shard", None)
    columns = P("expert", None, "shard")
    placed = (
        rows,
        P("expert", None),
        rows,
        P("shard"),
        by_shard,
        by_shard,
        by_shard,
        P("shard"),
        P("shard"),
        by_shard,
        P("shard"),
        by_shard,
        columns,
        columns,
        P("expert", "shard", None),
        rows,
    )
    return jax.shard_map(
        body,
        mesh=mesh,
        in_specs=placed,
        out_specs=(
            rows,
            rows,
            P("shard"),
            by_shard,
            by_shard,
            by_shard,
            P("shard"),
            P("shard"),
            by_shard,
            P("shard"),
            by_shard,
            columns,
            columns,
            P("expert", "shard", None),
        ),
        check_vma=False,
    )
```
